512 devices in a mesh: dp: 2 (over z_hi), seq: 64 (over x, z_lo, core), tp: 4 (over y).
Axes of the slice: x: 4, y: 4, z: 16 (z_hi: 2, z_lo: 8; z = z_hi * 8 + z_lo), core: 2. Of those that a mesh axis runs over, the one named last changes fastest.
Arguments:
- tokens: bfloat16 [2, 128, 64, 1152], P('dp', 'seq', None, 'tp'), may hold values from -6 to 6
- modulation: float32 [2, 6, 1152], P('dp'), may hold values from -2 to 2, as said below
- qkv_spatial: bfloat16 [1152, 3, 1152], P('seq', None, 'tp'), may hold values from -0.1875 to 0.1875
- out_spatial: bfloat16 [1152, 1152], P('seq', 'tp'), may hold values from -0.1875 to 0.1875
- qkv_temporal: bfloat16 [1152, 3, 1152], P('seq', None, 'tp'), may hold values from -0.1875 to 0.1875
- out_temporal: bfloat16 [1152, 1152], P('seq', 'tp'), may hold values from -0.1875 to 0.1875
- cotangent: bfloat16 [2, 128, 64, 1152], P('dp', 'seq', None, 'tp'), may hold values from -6 to 6
Outputs:
- output: bfloat16 [2, 128, 64, 1152], P('dp', 'seq', None, 'tp')
- input_grad: bfloat16 [2, 128, 64, 1152], P('dp', 'seq', None, 'tp')
- out_spatial_grad: float32 [1152, 1152], P('seq', 'tp')
- out_temporal_grad: float32 [1152, 1152], P('seq', 'tp')
The draws below stay inside these ranges and needn't reach their ends.
Inputs may be any that keep to these rules, and one draw needn't show every extreme that they name: `modulation`: rows 0, 3 are shifts, rows 1, 4 scales, rows 2, 5 gates; every gate lies in 0.5 to 1.5, every scale in -0.5 to 1.
All inputs are finite; a program needn't handle non-finite values.
Results may differ from the reference program's by a relative error of at most 0.039.
Values may be sent and summed in bfloat16 or wider, within the bound.
A program may use at most 64 MiB of HBM per device.

```python
import jax
import jax.numpy as jnp
from jax import lax

D = 1152
HD = 72
P_SIZE = 64
FRAMES = 128
CLIPS = 2
N_TP = 4


def draw_modulation(key, part):
    key = jax.random.fold_in(key, 17)
    keys = jax.random.split(key, 3)
    shift = jax.random.uniform(keys[0], (CLIPS, 2, D), jnp.float32, -2.0, 2.0)
    scale = jax.random.uniform(keys[1], (CLIPS, 2, D), jnp.float32, -0.5, 1.0)
    gate = jax.random.uniform(keys[2], (CLIPS, 2, D), jnp.float32, 0.5, 1.5)
    stacked = jnp.stack([shift, scale, gate], axis=2)
    return stacked.reshape(CLIPS, 6, D)


def level_of(rng, dims, pieces, smallest, high):
    def one(position, parts):
        steps = jax.random.uniform(jax.random.fold_in(jax.random.fold_in(rng, 6), position), (parts,), jnp.float32, smallest / len(pieces), high / len(pieces))
        return jnp.repeat(jnp.exp(steps), dims[position] // parts).reshape((-1,) + (1,) * (len(dims) - position - 1))

    gain = one(*pieces[0])
    for cut in pieces[1:]:
        gain = gain * one(*cut)
    return gain


def noise(stream_key, extent, scale, limit, pieces=(), dtype=jnp.bfloat16):
    values = scale * jax.random.normal(stream_key, extent, jnp.float32)
    if pieces:
        values = values * level_of(stream_key, extent, pieces, -0.22, 0.18)
    return jnp.clip(values, -limit, limit).astype(dtype)


def setup_inputs(seed: int = 0) -> dict:
    key_list = jax.random.split(jax.random.key(seed), 8)
    return {
        "tokens": noise(key_list[0], (CLIPS, FRAMES, P_SIZE, D), 1.0, 6.0, ((0, 2), (1, 64), (3, 4))),
        "modulation": draw_modulation(jax.random.fold_in(key_list[7], 71), 0),
        "qkv_spatial": noise(key_list[2], (D, 3, D), D ** -0.5, 0.1875, ((0, 64), (2, 4))),
        "out_spatial": noise(key_list[3], (D, D), D ** -0.5, 0.1875, ((0, 64), (1, 4))),
        "qkv_temporal": noise(key_list[4], (D, 3, D), D ** -0.5, 0.1875, ((0, 64), (2, 4))),
        "out_temporal": noise(key_list[5], (D, D), D ** -0.5, 0.1875, ((0, 64), (1, 4))),
        "cotangent": noise(key_list[6], (CLIPS, FRAMES, P_SIZE, D), 1.0, 6.0, ((0, 2), (1, 64), (3, 4))),
    }


EPS = 1e-06
SPATIAL = ('gshe,gthe->ghst', 'ghst,gthe->gshe', 'ghst,gshe->gthe')
TEMPORAL = ('sghe,tghe->ghst', 'ghst,tghe->sghe', 'ghst,sghe->tghe')

def contract(form, left, right):
    return jnp.einsum(form, left.astype(jnp.float32), right.astype(jnp.float32))

def norm_forward(wide, shift, scale):
    values = wide.astype(jnp.float32)
    center = values - lax.optimization_barrier(jnp.mean(values, axis=-1, keepdims=True))
    inverse = lax.rsqrt(lax.optimization_barrier(jnp.mean(center * center, axis=-1, keepdims=True)) + EPS)
    normed = center * inverse
    return ((normed * (1.0 + scale) + shift).astype(jnp.bfloat16), normed, inverse)

def likelihood_of(query, keys, forms):
    scores = contract(forms[0], query, keys) * query.shape[-1] ** (-0.5)
    largest = lax.optimization_barrier(jnp.max(scores, axis=-1, keepdims=True))
    weights = jnp.exp(scores - largest)
    return weights / lax.optimization_barrier(jnp.sum(weights, axis=-1, keepdims=True))

def attend(query, keys, values, forms):
    rounded = likelihood_of(query, keys, forms).astype(jnp.bfloat16)
    return contract(forms[1], rounded, values).astype(jnp.bfloat16)

def attend_back(query, keys, values, grad_out, forms):
    likely = likelihood_of(query, keys, forms)
    grad_values = contract(forms[2], likely.astype(jnp.bfloat16), grad_out).astype(jnp.bfloat16)
    grad_likely = contract(forms[0], grad_out, values)
    spread = grad_likely - lax.optimization_barrier(jnp.sum(likely * grad_likely, axis=-1, keepdims=True))
    grad_scores = (likely * spread * query.shape[-1] ** (-0.5)).astype(jnp.bfloat16)
    grad_query = contract(forms[1], grad_scores, keys).astype(jnp.bfloat16)
    grad_keys = contract(forms[2], grad_scores, query).astype(jnp.bfloat16)
    return (grad_query, grad_keys, grad_values)

def split_heads(flat):
    return flat.reshape(flat.shape[:-1] + (flat.shape[-1] // HD, HD))

def rounded_part(part):
    return lax.optimization_barrier(part.astype(jnp.bfloat16)).astype(jnp.float32)

def head_group_sum(flat, out_weight):
    width = flat.shape[-1] // N_TP
    total = jnp.zeros(flat.shape[:-1] + (out_weight.shape[0],), jnp.float32)
    for group in range(N_TP):
        lower = group * width
        part = contract('abi,oi->abo', flat[..., lower:lower + width], out_weight[:, lower:lower + width])
        total = total + rounded_part(part)
    return total

def input_group_sum(stacked, in_weight):
    width = stacked.shape[-1] // N_TP
    total = jnp.zeros(stacked.shape[:2] + (in_weight.shape[0],), jnp.float32)
    for group in range(N_TP):
        lower = group * width
        part = contract('abch,dch->abd', stacked[..., lower:lower + width], in_weight[:, :, lower:lower + width])
        total = total + rounded_part(part)
    return total

def block_forward(rows, in_weight, out_weight, shift, scale, gate, forms):
    modded, normed, inverse = norm_forward(rows, shift, scale)
    mixed = contract('abd,dch->abch', modded, in_weight).astype(jnp.bfloat16)
    query = split_heads(mixed[:, :, 0])
    keys = split_heads(mixed[:, :, 1])
    values = split_heads(mixed[:, :, 2])
    heads_out = attend(query, keys, values, forms)
    flat = heads_out.reshape(rows.shape)
    attended = head_group_sum(flat, out_weight)
    new_rows = (rows.astype(jnp.float32) + gate * attended).astype(jnp.bfloat16)
    return (new_rows, (normed, inverse, flat, query, keys, values))

def block_backward(grad_new, saved, in_weight, out_weight, scale, gate, forms):
    normed, inverse, flat, query, keys, values = saved
    grad_gate = (gate * grad_new.astype(jnp.float32)).astype(jnp.bfloat16)
    weight_grad = contract('abo,abi->oi', grad_gate, flat)
    grad_flat = contract('abo,oi->abi', grad_gate, out_weight).astype(jnp.bfloat16)
    grad_query, grad_keys, grad_values = attend_back(query, keys, values, split_heads(grad_flat), forms)
    stacked = jnp.stack([grad_query.reshape(grad_flat.shape), grad_keys.reshape(grad_flat.shape), grad_values.reshape(grad_flat.shape)], axis=2)
    summed = input_group_sum(stacked, in_weight)
    scaled = summed * (1.0 + scale)
    first_mean = lax.optimization_barrier(jnp.mean(scaled, axis=-1, keepdims=True))
    second_mean = lax.optimization_barrier(jnp.mean(scaled * normed, axis=-1, keepdims=True))
    grad_in = inverse * (scaled - first_mean - normed * second_mean)
    return ((grad_new.astype(jnp.float32) + grad_in).astype(jnp.bfloat16), weight_grad)

def reference(tokens, modulation, qkv_spatial, out_spatial, qkv_temporal, out_temporal, cotangent):
    results = []
    gradients = []
    spatial_grad = jnp.zeros((D, D), jnp.float32)
    temporal_grad = jnp.zeros((D, D), jnp.float32)
    for clip in range(CLIPS):
        modulators = modulation[clip]
        first, saved_spatial = block_forward(tokens[clip], qkv_spatial, out_spatial, modulators[0], modulators[1], modulators[2], SPATIAL)
        second, saved_temporal = block_forward(first, qkv_temporal, out_temporal, modulators[3], modulators[4], modulators[5], TEMPORAL)
        first_grad, weight_temporal = block_backward(cotangent[clip], saved_temporal, qkv_temporal, out_temporal, modulators[4], modulators[5], TEMPORAL)
        input_grad, weight_spatial = block_backward(first_grad, saved_spatial, qkv_spatial, out_spatial, modulators[1], modulators[2], SPATIAL)
        results.append(second)
        gradients.append(input_grad)
        spatial_grad = spatial_grad + weight_spatial
        temporal_grad = temporal_grad + weight_temporal
    return (jnp.stack(results), jnp.stack(gradients), spatial_grad, temporal_grad)
```

```python
import functools

import jax
import jax.numpy as jnp
from jax import lax
from jax.experimental import pallas as pl
from jax.experimental.pallas import tpu as pltpu
from jax.sharding import PartitionSpec as P

HD = 72
EPS = 1e-06
MAIN = 16
MESH = pl.DeviceIdType.MESH
BF = jnp.bfloat16
F32 = jnp.float32


def mm(a, b):
    return lax.dot_general(a, b, (((1,), (0,)), ((), ())), preferred_element_type=F32)


def mm_nt(a, b):
    return lax.dot_general(a, b, (((1,), (1,)), ((), ())), preferred_element_type=F32)


def mm_tn(a, b):
    return lax.dot_general(a, b, (((0,), (0,)), ((), ())), preferred_element_type=F32)


def iota(shape, axis):
    return lax.broadcasted_iota(jnp.int32, shape, axis)


class Sems:
    def __init__(self):
        self.count = 0

    def take(self, n):
        first = self.count
        self.count += n
        return first


def layout(X, C, Z, Y, DP):
    s = Sems()
    names = {}
    G = X * C
    for name in ("tok", "ggt", "rs1", "fst", "rsg", "rsp", "ggs", "rsf"):
        names[name] = s.take(Y)
    for name in ("cot_x", "fst_x", "fg_x", "out_x"):
        names[name] = s.take(G)
    for name in ("cot_z", "fst_z", "fg_z", "out_z"):
        names[name] = s.take(Z)
    for name in ("zu0", "zd0", "zu0r", "zd0r", "zu1", "zd1"):
        names[name] = s.take(Z)
    names["xp0"] = s.take(15)
    names["xp1"] = s.take(X)
    names["sib0"] = s.take(2 * X)
    names["sib1"] = s.take(X)
    for b in (0, 1):
        names["wc%d" % b] = s.take(1)
        names["wx%d" % b] = s.take(X)
        names["wz%d" % b] = s.take(DP * Z)
    return names, s.count


def kernel(dims, names, tok, cot, mod, wmain, wrest, out, igrad, wg_s, wg_t, *refs):
    X, C, Z, Y, DP, T, F, H, R2 = dims
    G = X * C
    N = Y * F
    (
        ssem, rsem, pm, pr, xw_s, xw_t, gw_t, gw_s, Wm, Rb, Wr,
        cot_a, cot_b, cot_c, fst_a, fst_b, fst_c, fst_d, fg_a, fg_b, fg_c, fg_d, fg_e,
        out_a, out_b, out_c, out_d,
        mp, mpr, qkv, prob, flat_s, stat,
        rs1_a, rs1_b, rsg_a, rsg_b, rsp_a, rsp_b, rsf_a, rsf_b,
        wgp, wgc, wgx, wgxr, wgz, wgzr,
    ) = refs

    d = lax.axis_index("dp")
    s = lax.axis_index("seq")
    y = lax.axis_index("tp")
    x = s // (Z * C)
    z = lax.rem(s // C, Z)
    c = lax.rem(s, C)
    g = x * C + c
    zg = d * Z + z

    def seq_of(x_, z_, c_):
        return (x_ * Z + z_) * C + c_

    def dev(d_, x_, z_, c_, y_):
        return {"dp": d_, "seq": seq_of(x_, z_, c_), "tp": y_}

    def dev_y(y_):
        return dev(d, x, z, c, y_)

    def dev_g(g_):
        return dev(d, g_ // C, z, lax.rem(g_, C), y)

    def dev_z(z_):
        return dev(d, x, z_, c, y)

    def dev_zg(zg_):
        return dev(zg_ // Z, x, lax.rem(zg_, Z), c, y)

    def dev_x(x_):
        return dev(d, x_, z, c, y)

    sibling = dev(d, x, z, 1 - c, y)
    ZG = DP * Z
    sent = []

    def send(src, dst, sem, device):
        copy = pltpu.make_async_remote_copy(
            src_ref=src, dst_ref=dst, send_sem=ssem.at[sem], recv_sem=rsem.at[sem],
            device_id=device, device_id_type=MESH,
        )
        copy.start()
        sent.append(copy)

    def recv(dst, sem):
        pltpu.make_async_remote_copy(
            src_ref=dst, dst_ref=dst, send_sem=ssem.at[sem], recv_sem=rsem.at[sem],
            device_id=sibling, device_id_type=MESH,
        ).wait_recv()

    def ex_send(src, dst, sem, n, me, device):
        for k in range(1, n):
            peer = lax.rem(me + k, n)
            send(src(peer), dst.at[me], sem + k, device(peer))

    def ex_wait(dst, sem, n, me):
        for k in range(1, n):
            recv(dst.at[lax.rem(me + n - k, n)], sem + k)

    barrier = pltpu.get_barrier_semaphore()
    peers = [dev_y(lax.rem(y + k, Y)) for k in range(1, Y)]
    peers += [dev_g(lax.rem(g + k, G)) for k in range(1, G)]
    peers += [dev_zg(lax.rem(zg + k, ZG)) for k in range(1, ZG)]
    for peer in peers:
        pl.semaphore_signal(barrier, inc=1, device_id=peer, device_id_type=MESH)
    pl.semaphore_wait(barrier, len(peers))

    ex_send(lambda p: tok, xw_s, names["tok"], Y, y, dev_y)

    up, down = dev_zg(lax.rem(zg + 1, ZG)), dev_zg(lax.rem(zg + ZG - 1, ZG))
    nup = Z // 2
    ndown = Z - 1 - nup

    def w_slot(b, x_, c_, z_):
        return Wm.at[b, :, x_, c_, z_]

    def z_hop(step, first, b, device, sem, semr):
        z_ = lax.rem(z + first * step + Z * Z, Z)
        src = wmain.at[b] if step == 0 else w_slot(b, x, c, z_)
        send(src, w_slot(b, x, c, z_), sem + step, device)
        if b == 0:
            src = wrest if step == 0 else Rb.at[x, c, z_]
            send(src, Rb.at[x, c, z_], semr + step, device)

    def z_take(step, first, b, sem, semr):
        z_ = lax.rem(z + first * (step + 1) + Z * Z, Z)
        recv(w_slot(b, x, c, z_), sem + step)
        if b == 0:
            recv(Rb.at[x, c, z_], semr + step)

    def z_start(b):
        if nup:
            z_hop(0, -1, b, up, names["zu%d" % b], names["zu0r"])
        if ndown:
            z_hop(0, 1, b, down, names["zd%d" % b], names["zd0r"])

    def z_chain(b):
        for step in range(nup):
            z_take(step, -1, b, names["zu%d" % b], names["zu0r"])
            if step + 1 < nup:
                z_hop(step + 1, -1, b, up, names["zu%d" % b], names["zu0r"])
            if step < ndown:
                z_take(step, 1, b, names["zd%d" % b], names["zd0r"])
                if step + 1 < ndown:
                    z_hop(step + 1, 1, b, down, names["zd%d" % b], names["zd0r"])

    z_start(0)

    row = iota((T, T), 0)
    col = iota((T, T), 1)

    def swap_rows(value, source):
        return mm((col == source).astype(BF), value).astype(BF)

    def to_groups(value):
        return swap_rows(value, lax.rem(row // Z, 2) * (G * Z) + row // (2 * Z) * Z + lax.rem(row, Z))

    def from_groups(value):
        return swap_rows(
            value, lax.rem(row // Z, G) * (2 * Z) + row // (G * Z) * Z + lax.rem(row, Z)
        )

    def to_z(value):
        return swap_rows(value, lax.rem(row, 2 * G) * Z + row // (2 * G))

    def from_z(value):
        return swap_rows(value, lax.rem(row, Z) * (2 * G) + row // Z)

    def x_put(buf, value):
        buf[...] = value.reshape(G, 2 * Z, F)

    def z_put(buf, value):
        buf[...] = value.reshape(Z, 2 * G, F)

    def flatten(buf):
        return buf[...].reshape(T, F)

    x_put(cot_a, to_groups(cot[...]))
    ex_send(lambda p: cot_a.at[p], cot_b, names["cot_x"], G, g, dev_g)
    z_start(1)
    cot_b[g] = cot_a[g]
    xw_s[y] = tok[...]
    for b in (0, 1):
        for k in range(4):
            Wm[b, k, x, c, z] = wmain[b, k]
    Rb[x, c, z] = wrest[...]

    FP = pm.shape[0]
    CZ = C * Z
    j = iota((FP, CZ * MAIN), 1)
    target = (lax.rem(j // MAIN, Z) * C + j // (Z * MAIN)) * (MAIN + R2) + lax.rem(j, MAIN)
    pm[...] = (iota((FP, CZ * MAIN), 0) == target).astype(BF)
    j = iota((FP, X * CZ * R2), 1)
    target = (lax.rem(j // R2, Z) * C + lax.rem(j // (Z * R2), C)) * (MAIN + R2)
    target += MAIN + lax.rem(j, R2)
    hit = iota((FP, X * CZ * R2), 0) == target
    for x_ in range(X):
        pr[x_] = (hit & (j // (CZ * R2) == x_)).astype(BF)

    lane = iota((1, F), 1)
    head = [(lane >= h * HD) & (lane < (h + 1) * HD) for h in range(H)]

    def narrow(slices):
        rest = None
        for x_ in range(X):
            part = slices[x_]
            mp[:, x_ * CZ * MAIN : (x_ + 1) * CZ * MAIN] = mm(part, pm[:F]).astype(BF)
            more = mm(part, pr[x_, :F])
            rest = more if rest is None else rest + more
        mpr[...] = rest.astype(BF)

    def natural(main, rest, x_):
        return mm_nt(main[:, x_ * CZ * MAIN : (x_ + 1) * CZ * MAIN], pm[...]) + mm_nt(rest, pr[x_])

    def norm(xw, at):
        total = None
        for n in range(Y):
            part = jnp.sum(xw[n].astype(F32), axis=-1, keepdims=True)
            total = part if total is None else total + part
        mean = total * (1.0 / N)
        total = None
        for n in range(Y):
            center = xw[n].astype(F32) - mean
            part = jnp.sum(center * center, axis=-1, keepdims=True)
            total = part if total is None else total + part
        inverse = lax.rsqrt(total * (1.0 / N) + EPS)
        stat[2 * at] = mean
        stat[2 * at + 1] = inverse
        slices = []
        for n in range(Y):
            normed = (xw[n].astype(F32) - mean) * inverse
            slices.append((normed * (1.0 + mod[3 * at + 1, n]) + mod[3 * at, n]).astype(BF))
        narrow(slices)

    K = X * CZ * MAIN

    def weight(b, k):
        return Wm[b, k].reshape(K, F), Wr[b * 4 + k]

    def project(b):
        for k in range(3):
            main, rest = weight(b, k)
            qkv[b, k] = (mm(mp[...], main) + mm(mpr[...], rest)).astype(BF)

    def spread(value):
        zero = jnp.zeros_like(value)
        return jnp.concatenate([jnp.where(head[h], value, zero) for h in range(H)], axis=0)

    def gather_heads(value):
        total = None
        for h in range(H):
            part = jnp.where(head[h], value[h * T : (h + 1) * T], 0.0)
            total = part if total is None else total + part
        return total.astype(BF)

    SCALE = HD ** (-0.5)

    def attend(b):
        scores = mm_nt(spread(qkv[b, 0]), qkv[b, 1]) * SCALE
        if b == 0:
            query_frame = lax.rem(iota((H * T, T), 0), T) // (G * Z)
            same = query_frame == iota((H * T, T), 1) // (G * Z)
            scores = jnp.where(same, scores, -1e30)
        weights = jnp.exp(scores - jnp.max(scores, axis=-1, keepdims=True))
        prob[b] = weights / jnp.sum(weights, axis=-1, keepdims=True)
        return gather_heads(mm(prob[b].astype(BF), qkv[b, 2]))

    def attend_back(b, grad):
        grads = spread(grad)
        likely = prob[b]
        grad_values = mm_tn(likely.astype(BF), grads).astype(BF)
        grad_likely = mm_nt(grads, qkv[b, 2])
        shift = grad_likely - jnp.sum(likely * grad_likely, axis=-1, keepdims=True)
        grad_scores = (likely * shift * SCALE).astype(BF)
        grad_query = gather_heads(mm(grad_scores, qkv[b, 1]))
        grad_keys = mm_tn(grad_scores, spread(qkv[b, 0])).astype(BF)
        return grad_query, grad_keys, grad_values

    def out_partial(b, flat, buf):
        main, rest = weight(b, 3)
        part = mm_nt(flat, main).astype(BF)
        part_rest = mm_nt(flat, rest).astype(BF)
        for n in range(Y):
            buf[n] = natural(part, part_rest, n)[:, :F].astype(BF)

    def grad_heads(b):
        main, rest = weight(b, 3)
        return (mm(mp[...], main) + mm(mpr[...], rest)).astype(BF)

    def in_partial(b, grads, xw, buf):
        part, part_rest = None, None
        for k in range(3):
            main, rest = weight(b, k)
            a, r = mm_nt(grads[k], main), mm_nt(grads[k], rest)
            part = a if part is None else part + a
            part_rest = r if part_rest is None else part_rest + r
        part, part_rest = part.astype(BF), part_rest.astype(BF)
        mean, inverse = stat[2 * b], stat[2 * b + 1]
        first, second = None, None
        slices = []
        for n in range(Y):
            value = natural(part, part_rest, n)
            slices.append(value)
            scaled = value[:, :F] * (1.0 + mod[3 * b + 1, n])
            normed = (xw[n].astype(F32) - mean) * inverse
            a = jnp.sum(scaled, axis=-1, keepdims=True)
            r = jnp.sum(scaled * normed, axis=-1, keepdims=True)
            first = a if first is None else first + a
            second = r if second is None else second + r
        spot = iota((1, FP), 1)
        for n in range(Y):
            value = jnp.where(spot == F, first, jnp.where(spot == F + 1, second, slices[n]))
            buf[n] = value.astype(BF)

    def in_finish(b, buf, xw, incoming):
        total = buf[0].astype(F32)
        for n in range(1, Y):
            total = total + buf[n].astype(F32)
        first = total[:, F : F + 1] * (1.0 / N)
        second = total[:, F + 1 : F + 2] * (1.0 / N)
        scaled = total[:, :F] * (1.0 + mod[3 * b + 1, y])
        normed = (xw[y].astype(F32) - stat[2 * b]) * stat[2 * b + 1]
        grad = stat[2 * b + 1] * (scaled - first - normed * second)
        return (incoming.astype(F32) + grad).astype(BF)

    def add_up(buf):
        total = buf[0].astype(F32)
        for n in range(1, Y):
            total = total + buf[n].astype(F32)
        return total

    def gated(b, value):
        return (mod[3 * b + 2, y] * value.astype(F32)).astype(BF)

    def wg_start(b, flat):
        main = mm_tn(mp[...], flat).astype(BF)
        rest = mm_tn(mpr[...], flat).astype(BF)
        wgp[b, :, :, :Z] = main.reshape(X, C, Z, MAIN, F)
        wgp[b, :, :, Z] = rest.reshape(X, C, Z * R2, F)
        send(wgp.at[b, :, 1 - c], wgc.at[b], names["wc%d" % b], sibling)

    def wg_second(b):
        recv(wgc.at[b], names["wc%d" % b])
        wgx[b] = (wgp[b, :, c].astype(F32) + wgc[b].astype(F32)).astype(BF)
        ex_send(lambda p: wgx.at[b, p], wgxr.at[b], names["wx%d" % b], X, x, dev_x)
        wgxr[b, x] = wgx[b, x]

    def wg_third(b):
        ex_wait(wgxr.at[b], names["wx%d" % b], X, x)
        total = wgxr[b, 0].astype(F32)
        for n in range(1, X):
            total = total + wgxr[b, n].astype(F32)
        total = total.astype(BF)
        for n in range(Z):
            wgz[b, n, 0] = total[n]
            wgz[b, n, 1] = total[Z]
        ex_send(
            lambda p: wgz.at[b, lax.rem(p, Z)], wgzr.at[b], names["wz%d" % b], ZG, zg, dev_zg
        )
        wgzr[b, zg] = wgz[b, z]

    def wg_end(b, ref):
        ex_wait(wgzr.at[b], names["wz%d" % b], ZG, zg)
        main = wgzr[b, 0, 0].astype(F32)
        rest = wgzr[b, 0, 1].astype(F32)
        for n in range(1, ZG):
            main = main + wgzr[b, n, 0].astype(F32)
            rest = rest + wgzr[b, n, 1].astype(F32)
        ref[:MAIN] = main
        at = iota((Z * R2, F), 0)
        for r in range(R2):
            ref[MAIN + r : MAIN + r + 1] = jnp.sum(
                jnp.where(at == z * R2 + r, rest, 0.0), axis=0, keepdims=True
            )

    z_chain(0)
    right, left = lax.rem(x + 1, X), lax.rem(x + X - 1, X)
    across = lax.rem(x + X // 2, X)

    def piece(x_, k):
        return Rb.at[x_, c] if k == 4 else Wm.at[0, k, x_, c]

    xp = names["xp0"]
    ahead, behind = (0, 1, 2, 3, 4), (2, 4, 0, 1, 3)
    for n in range(5):
        send(piece(x, ahead[n]), piece(x, ahead[n]), xp + ahead[n], dev_x(right))
        if X > 2:
            send(piece(x, behind[n]), piece(x, behind[n]), xp + 5 + behind[n], dev_x(left))

    def to_sibling(b, x_, n):
        send(Wm.at[b, :, x_, c], Wm.at[b, :, x_, c], names["sib%d" % b] + n, sibling)
        if b == 0:
            send(Rb.at[x_, c], Rb.at[x_, c], names["sib0"] + X + n, sibling)

    def from_sibling(b, x_, n):
        recv(Wm.at[b, :, x_, 1 - c], names["sib%d" % b] + n)
        if b == 0:
            recv(Rb.at[x_, 1 - c], names["sib0"] + X + n)

    to_sibling(0, x, 0)

    ex_wait(cot_b, names["cot_x"], G, g)
    z_put(cot_c.at[0], to_z(flatten(cot_b)))
    ex_send(lambda p: cot_c.at[0, p], cot_c.at[1], names["cot_z"], Z, z, dev_z)
    cot_c[1, z] = cot_c[0, z]

    ex_wait(xw_s, names["tok"], Y, y)
    norm(xw_s, 0)

    if X > 2:
        for k in (0, 1):
            recv(piece(left, k), xp + k)
            send(piece(left, k), piece(left, k), xp + 10 + k, dev_x(right))
            if k == 0:
                for m in (2, 4):
                    recv(piece(right, m), xp + 5 + m)
                    send(piece(right, m), piece(right, m), xp + 10 + m, dev_x(left))
        for k in (2, 3, 4):
            recv(piece(left, k), xp + k)
        to_sibling(0, left, 1)
        for k in (0, 1, 3):
            recv(piece(right, k), xp + 5 + k)
        send(piece(right, 3), piece(right, 3), xp + 13, dev_x(left))
        to_sibling(0, right, 2)
        z_chain(1)
        for k in range(5):
            recv(piece(across, k), xp + 10 + k)
        to_sibling(0, across, 3)
        from_sibling(0, x, 0)
        from_sibling(0, left, 1)
        from_sibling(0, right, 2)
        from_sibling(0, across, 3)
    else:
        for k in range(5):
            recv(piece(left, k), xp + k)
        to_sibling(0, left, 1)
        z_chain(1)
        from_sibling(0, x, 0)
        from_sibling(0, left, 1)
    for k in range(1, X):
        to_x = lax.rem(x + k, X)
        send(Wm.at[1, :, x, c], Wm.at[1, :, x, c], names["xp1"] + k, dev_x(to_x))
    to_sibling(1, x, 0)

    ex_wait(cot_c.at[1], names["cot_z"], Z, z)
    cot_t = flatten(cot_c.at[1])
    gw_t[y] = gated(1, cot_t)
    ex_send(lambda p: gw_t.at[y], gw_t, names["ggt"], Y, y, dev_y)

    n_rest = CZ * 8 * R2
    o = iota((n_rest, n_rest), 0)
    source = lax.rem(o // R2, CZ) * (8 * R2) + o // (CZ * R2) * R2 + lax.rem(o, R2)
    shuffle = (iota((n_rest, n_rest), 1) == source).astype(BF)
    for x_ in range(X):
        rest = mm(shuffle, Rb[x_].reshape(n_rest, F)).astype(BF)
        Wr[:, x_ * CZ * R2 : (x_ + 1) * CZ * R2] = rest.reshape(8, CZ * R2, F)

    project(0)
    flat_s[...] = attend(0)
    out_partial(0, flat_s[...], rs1_a)
    ex_send(lambda p: rs1_a.at[p], rs1_b, names["rs1"], Y, y, dev_y)
    rs1_b[y] = rs1_a[y]

    for k in range(1, X):
        x_ = lax.rem(x + X - k, X)
        recv(Wm.at[1, :, x_, c], names["xp1"] + k)
        to_sibling(1, x_, k)

    ex_wait(rs1_b, names["rs1"], Y, y)
    first = tok[...].astype(F32) + mod[2, y] * add_up(rs1_b)
    x_put(fst_a, to_groups(first.astype(BF)))
    ex_send(lambda p: fst_a.at[p], fst_b, names["fst_x"], G, g, dev_g)
    fst_b[g] = fst_a[g]

    from_sibling(1, x, 0)
    for k in range(1, X):
        from_sibling(1, lax.rem(x + X - k, X), k)
    ex_wait(gw_t, names["ggt"], Y, y)

    ex_wait(fst_b, names["fst_x"], G, g)
    z_put(fst_c, to_z(flatten(fst_b)))
    ex_send(lambda p: fst_c.at[p], fst_d, names["fst_z"], Z, z, dev_z)
    fst_d[z] = fst_c[z]

    ex_wait(fst_d, names["fst_z"], Z, z)
    xw_t[y] = flatten(fst_d)
    ex_send(lambda p: xw_t.at[y], xw_t, names["fst"], Y, y, dev_y)

    narrow([gw_t[n] for n in range(Y)])
    grad_t = grad_heads(1)

    ex_wait(xw_t, names["fst"], Y, y)
    norm(xw_t, 1)
    project(1)
    flat_t = attend(1)
    grads = attend_back(1, grad_t)
    in_partial(1, grads, xw_t, rsg_a)
    ex_send(lambda p: rsg_a.at[p], rsg_b, names["rsg"], Y, y, dev_y)
    rsg_b[y] = rsg_a[y]

    out_partial(1, flat_t, rsp_a)
    ex_send(lambda p: rsp_a.at[p], rsp_b, names["rsp"], Y, y, dev_y)
    rsp_b[y] = rsp_a[y]

    ex_wait(rsg_b, names["rsg"], Y, y)
    z_put(fg_a, in_finish(1, rsg_b, xw_t, cot_t))
    ex_send(lambda p: fg_a.at[p], fg_b, names["fg_z"], Z, z, dev_z)
    fg_b[z] = fg_a[z]

    narrow([gw_t[n] for n in range(Y)])
    wg_start(1, flat_t)

    ex_wait(fg_b, names["fg_z"], Z, z)
    x_put(fg_c, from_z(flatten(fg_b)))
    ex_send(lambda p: fg_c.at[p], fg_d, names["fg_x"], G, g, dev_g)
    fg_d[g] = fg_c[g]

    ex_wait(rsp_b, names["rsp"], Y, y)
    second = xw_t[y].astype(F32) + mod[5, y] * add_up(rsp_b)
    z_put(out_a, second.astype(BF))
    ex_send(lambda p: out_a.at[p], out_b, names["out_z"], Z, z, dev_z)
    out_b[z] = out_a[z]

    ex_wait(fg_d, names["fg_x"], G, g)
    fg_e[...] = from_groups(flatten(fg_d))
    gw_s[y] = gated(0, fg_e[...])
    ex_send(lambda p: gw_s.at[y], gw_s, names["ggs"], Y, y, dev_y)

    wg_second(1)
    ex_wait(out_b, names["out_z"], Z, z)
    x_put(out_c, from_z(flatten(out_b)))
    ex_send(lambda p: out_c.at[p], out_d, names["out_x"], G, g, dev_g)
    out_d[g] = out_c[g]

    ex_wait(gw_s, names["ggs"], Y, y)
    narrow([gw_s[n] for n in range(Y)])
    wg_start(0, flat_s[...])
    grad_s = grad_heads(0)
    wg_third(1)
    wg_second(0)
    grads = attend_back(0, grad_s)
    wg_third(0)
    in_partial(0, grads, xw_s, rsf_a)
    ex_send(lambda p: rsf_a.at[p], rsf_b, names["rsf"], Y, y, dev_y)
    rsf_b[y] = rsf_a[y]

    ex_wait(out_d, names["out_x"], G, g)
    out[...] = from_groups(flatten(out_d))
    wg_end(1, wg_t)
    ex_wait(rsf_b, names["rsf"], Y, y)
    igrad[...] = in_finish(0, rsf_b, xw_s, fg_e[...])
    wg_end(0, wg_s)
    for copy in sent:
        copy.wait_send()


def on_device(sizes, tokens, modulation, qkv_s, out_s, qkv_t, out_t, cotangent):
    DP, S, Y = sizes
    frames, patches, F = tokens.shape[1:]
    T = frames * patches
    X, C = Y, 2
    Z = S // (X * C)
    G = X * C
    H = F // HD
    rows = out_s.shape[0]
    R2 = rows - MAIN
    FP = (F + 2 + 127) // 128 * 128
    dims = (X, C, Z, Y, DP, T, F, H, R2)
    names, count = layout(X, C, Z, Y, DP)

    def joined(qkv, out):
        return jnp.concatenate([qkv.transpose(1, 0, 2), out[None]], axis=0)

    weights = jnp.stack([joined(qkv_s, out_s), joined(qkv_t, out_t)])
    wmain = weights[:, :, :MAIN]
    wrest = weights[:, :, MAIN:].reshape(8 * R2, F)
    mod = modulation.reshape(6, Y, 1, F)

    K, KR = X * C * Z * MAIN, X * C * Z * R2
    xs, zs = pltpu.VMEM((G, 2 * Z, F), BF), pltpu.VMEM((Z, 2 * G, F), BF)
    wide, padded = pltpu.VMEM((Y, T, F), BF), pltpu.VMEM((Y, T, FP), BF)
    scratch = [
        pltpu.SemaphoreType.DMA((count,)),
        pltpu.SemaphoreType.DMA((count,)),
        pltpu.VMEM((FP, C * Z * MAIN), BF),
        pltpu.VMEM((X, FP, KR), BF),
        wide, wide, wide, wide,
        pltpu.VMEM((2, 4, X, C, Z, MAIN, F), BF),
        pltpu.VMEM((X, C, Z, 8 * R2, F), BF),
        pltpu.VMEM((8, KR, F), BF),
        xs, xs, pltpu.VMEM((2, Z, 2 * G, F), BF),
        xs, xs, zs, zs,
        zs, zs, xs, xs, pltpu.VMEM((T, F), BF),
        zs, zs, xs, xs,
        pltpu.VMEM((T, K), BF),
        pltpu.VMEM((T, KR), BF),
        pltpu.VMEM((2, 3, T, F), BF),
        pltpu.VMEM((2, H * T, T), F32),
        pltpu.VMEM((T, F), BF),
        pltpu.VMEM((4, T, 1), F32),
        wide, wide, padded, padded, wide, wide, padded, padded,
        pltpu.VMEM((2, X, C, Z + 1, MAIN, F), BF),
        pltpu.VMEM((2, X, Z + 1, MAIN, F), BF),
        pltpu.VMEM((2, X, Z + 1, MAIN, F), BF),
        pltpu.VMEM((2, X, Z + 1, MAIN, F), BF),
        pltpu.VMEM((2, Z, 2, MAIN, F), BF),
        pltpu.VMEM((2, DP * Z, 2, MAIN, F), BF),
    ]
    vmem = pl.BlockSpec(memory_space=pltpu.VMEM)
    out, igrad, wg_s, wg_t = pl.pallas_call(
        functools.partial(kernel, dims, names),
        out_shape=(
            jax.ShapeDtypeStruct((T, F), BF),
            jax.ShapeDtypeStruct((T, F), BF),
            jax.ShapeDtypeStruct((rows, F), F32),
            jax.ShapeDtypeStruct((rows, F), F32),
        ),
        in_specs=[vmem] * 5,
        out_specs=(vmem,) * 4,
        scratch_shapes=scratch,
        compiler_params=pltpu.CompilerParams(
            collective_id=0, has_side_effects=True, vmem_limit_bytes=56 * 2**20
        ),
    )(tokens.reshape(T, F), cotangent.reshape(T, F), mod, wmain, wrest)
    shape = (1, frames, patches, F)
    return out.reshape(shape), igrad.reshape(shape), wg_s, wg_t


def solution(mesh):
    sizes = tuple(mesh.shape[a] for a in ("dp", "seq", "tp"))
    placed = (
        P("dp", "seq", None, "tp"),
        P("dp", None, None),
        P("seq", None, "tp"),
        P("seq", "tp"),
        P("seq", None, "tp"),
        P("seq", "tp"),
        P("dp", "seq", None, "tp"),
    )
    return jax.shard_map(
        functools.partial(on_device, sizes),
        mesh=mesh,
        in_specs=placed,
        out_specs=(
            P("dp", "seq", None, "tp"),
            P("dp", "seq", None, "tp"),
            P("seq", "tp"),
            P("seq", "tp"),
        ),
        check_vma=False,
    )
```

```python
import functools

import jax
import jax.numpy as jnp
from jax import lax
from jax.experimental import pallas as pl
from jax.experimental.pallas import tpu as pltpu
from jax.sharding import PartitionSpec as P

HD = 72
EPS = 1e-06
MAIN = 16
MESH = pl.DeviceIdType.MESH
BF = jnp.bfloat16
F32 = jnp.float32


def mm(a, b):
    return lax.dot_general(a, b, (((1,), (0,)), ((), ())), preferred_element_type=F32)


def mm_nt(a, b):
    return lax.dot_general(a, b, (((1,), (1,)), ((), ())), preferred_element_type=F32)


def mm_tn(a, b):
    return lax.dot_general(a, b, (((0,), (0,)), ((), ())), preferred_element_type=F32)


def iota(shape, axis):
    return lax.broadcasted_iota(jnp.int32, shape, axis)


class Sems:
    def __init__(self):
        self.count = 0

    def take(self, n):
        first = self.count
        self.count += n
        return first


def layout(X, C, Z, Y, DP):
    s = Sems()
    names = {}
    G = X * C
    for name in ("tok", "ggt", "rs1", "fst", "rsg", "rsp", "ggs", "rsf"):
        names[name] = s.take(Y)
    for name in ("cot_x", "fst_x", "fg_x", "out_x"):
        names[name] = s.take(G)
    for name in ("cot_z", "fst_z", "fg_z", "out_z"):
        names[name] = s.take(Z)
    for name in ("zu0", "zd0", "zu1", "zd1", "xr0", "xl0", "xo0"):
        names[name] = s.take(Z)
    names["sib0"] = s.take(X * Z)
    names["xp1"] = s.take(X)
    names["sib1"] = s.take(X)
    for b in (0, 1):
        names["wc%d" % b] = s.take(1)
        names["wx%d" % b] = s.take(X)
        names["wz%d" % b] = s.take(DP * Z)
    return names, s.count


def kernel(dims, names, tok, cot, mods, wown, wown_t, out, igrad, wg_s, wg_t, *refs):
    X, C, Z, Y, DP, T, F, FP, H, R2 = dims
    G = X * C
    N = Y * F
    (
        ssem, rsem, mod, pm, pr, xw_s, xw_t, gw_t, gw_s, Ws, Wt, Wr, cotp,
        cot_a, cot_b, cot_c, fst_a, fst_b, fst_c, fst_d, fg_a, fg_b, fg_c, fg_d, fg_e,
        out_a, out_b, out_c, out_d,
        mp, mpr, qkv, prob, flat_s, stat,
        rs1_a, rs1_b, rsg_a, rsg_b, rsp_a, rsp_b, rsf_a, rsf_b,
        wgp, wgc, wgx, wgxr, wgz, wgzr,
    ) = refs

    d = lax.axis_index("dp")
    s = lax.axis_index("seq")
    y = lax.axis_index("tp")
    x = s // (Z * C)
    z = lax.rem(s // C, Z)
    c = lax.rem(s, C)
    g = x * C + c
    zg = d * Z + z

    def seq_of(x_, z_, c_):
        return (x_ * Z + z_) * C + c_

    def dev(d_, x_, z_, c_, y_):
        return {"dp": d_, "seq": seq_of(x_, z_, c_), "tp": y_}

    def dev_y(y_):
        return dev(d, x, z, c, y_)

    def dev_g(g_):
        return dev(d, g_ // C, z, lax.rem(g_, C), y)

    def dev_z(z_):
        return dev(d, x, z_, c, y)

    def dev_zg(zg_):
        return dev(zg_ // Z, x, lax.rem(zg_, Z), c, y)

    def dev_x(x_):
        return dev(d, x_, z, c, y)

    sibling = dev(d, x, z, 1 - c, y)
    ZG = DP * Z
    sent = []

    def send(src, dst, sem, device):
        copy = pltpu.make_async_remote_copy(
            src_ref=src, dst_ref=dst, send_sem=ssem.at[sem], recv_sem=rsem.at[sem],
            device_id=device, device_id_type=MESH,
        )
        copy.start()
        sent.append(copy)

    def recv(dst, sem):
        pltpu.make_async_remote_copy(
            src_ref=dst, dst_ref=dst, send_sem=ssem.at[sem], recv_sem=rsem.at[sem],
            device_id=sibling, device_id_type=MESH,
        ).wait_recv()

    def ex_send(src, dst, sem, n, me, device):
        for k in range(1, n):
            peer = lax.rem(me + k, n)
            send(src(peer), dst.at[me], sem + k, device(peer))

    def ex_wait(dst, sem, n, me):
        for k in range(1, n):
            recv(dst.at[lax.rem(me + n - k, n)], sem + k)

    barrier = pltpu.get_barrier_semaphore()
    peers = [dev_y(lax.rem(y + k, Y)) for k in range(1, Y)]
    peers += [dev_g(lax.rem(g + k, G)) for k in range(1, G)]
    peers += [dev_zg(lax.rem(zg + k, ZG)) for k in range(1, ZG)]
    for peer in peers:
        pl.semaphore_signal(barrier, inc=1, device_id=peer, device_id_type=MESH)
    pl.semaphore_wait(barrier, len(peers))

    up, down = dev_zg(lax.rem(zg + 1, ZG)), dev_zg(lax.rem(zg + ZG - 1, ZG))
    right, left = lax.rem(x + 1, X), lax.rem(x + X - 1, X)
    across = lax.rem(x + X // 2, X)
    nup = Z // 2
    ndown = Z - 1 - nup

    def w_slot(b, x_, c_, z_):
        return (Wt if b else Ws).at[:, x_, c_, z_]

    def z_hop(step, first, b):
        z_ = lax.rem(z + first * step + Z * Z, Z)
        slot = w_slot(b, x, c, z_)
        src = (wown_t if b else wown) if step == 0 else slot
        send(src, slot, names["z%s%d" % ("u" if first < 0 else "d", b)] + step, up if first < 0 else down)

    def z_take(step, first, b):
        z_ = lax.rem(z + first * (step + 1) + Z * Z, Z)
        recv(w_slot(b, x, c, z_), names["z%s%d" % ("u" if first < 0 else "d", b)] + step)
        return z_

    def z_start(b):
        if nup:
            z_hop(0, -1, b)
        if ndown:
            z_hop(0, 1, b)

    def z_chain(b, arrived):
        for step in range(nup):
            z_ = z_take(step, -1, b)
            if step + 1 < nup:
                z_hop(step + 1, -1, b)
            arrived(2 * step + 1, z_)
            if step < ndown:
                z_ = z_take(step, 1, b)
                if step + 1 < ndown:
                    z_hop(step + 1, 1, b)
                arrived(2 * step + 2, z_)

    def order(i):
        return lax.rem(z + (-(i + 1) // 2 if i % 2 else i // 2) + Z, Z)

    def x_hop(i, own=False):
        slot = w_slot(0, x, c, order(i))
        src = wown if own else slot
        send(src, slot, names["xr0"] + i, dev_x(right))
        if X > 2:
            send(src, slot, names["xl0"] + i, dev_x(left))
        send(src, w_slot(0, x, c, order(i)), names["sib0"] + i, sibling)

    def x_take(i):
        recv(w_slot(0, left, c, order(i)), names["xr0"] + i)
        if X > 2:
            slot = w_slot(0, left, c, order(i))
            if i % 2 == 0:
                send(slot, slot, names["xo0"] + i, dev_x(right))
            send(slot, slot, names["sib0"] + Z + i, sibling)
            slot = w_slot(0, right, c, order(i))
            recv(slot, names["xl0"] + i)
            if i % 2 == 1:
                send(slot, slot, names["xo0"] + i, dev_x(left))
            send(slot, slot, names["sib0"] + 2 * Z + i, sibling)
        else:
            slot = w_slot(0, left, c, order(i))
            send(slot, slot, names["sib0"] + Z + i, sibling)

    def x_last(i):
        slot = w_slot(0, across, c, order(i))
        recv(slot, names["xo0"] + i)
        send(slot, slot, names["sib0"] + 3 * Z + i, sibling)

    z_start(0)
    x_hop(0, True)
    xw_s[y] = jnp.zeros((T, FP), BF)
    xw_s[y, :, :F] = tok[...]
    ex_send(lambda p: xw_s.at[y], xw_s, names["tok"], Y, y, dev_y)
    cotp[...] = jnp.zeros((T, FP), BF)
    cotp[:, :F] = cot[...]

    row = iota((T, T), 0)
    col = iota((T, T), 1)

    def swap_rows(value, source):
        return mm((col == source).astype(BF), value).astype(BF)

    def to_groups(value):
        return swap_rows(value, lax.rem(row // Z, 2) * (G * Z) + row // (2 * Z) * Z + lax.rem(row, Z))

    def from_groups(value):
        return swap_rows(
            value, lax.rem(row // Z, G) * (2 * Z) + row // (G * Z) * Z + lax.rem(row, Z)
        )

    def to_z(value):
        return swap_rows(value, lax.rem(row, 2 * G) * Z + row // (2 * G))

    def from_z(value):
        return swap_rows(value, lax.rem(row, Z) * (2 * G) + row // Z)

    def x_put(buf, value):
        buf[...] = value.reshape(G, 2 * Z, FP)

    def z_put(buf, value):
        buf[...] = value.reshape(Z, 2 * G, FP)

    def flatten(buf):
        return buf[...].reshape(T, FP)

    x_put(cot_a, to_groups(cotp[...]))
    ex_send(lambda p: cot_a.at[p], cot_b, names["cot_x"], G, g, dev_g)
    cot_b[g] = cot_a[g]
    for k in range(5):
        Ws[k, x, c, z] = wown[k]
    for k in range(4):
        Wt[k, x, c, z] = wown_t[k]
    mod[...] = jnp.zeros((6, Y, 1, FP), F32)
    for i in range(6):
        for n in range(Y):
            mod[i, n, :, :F] = mods[i : i + 1, n * F : (n + 1) * F]

    CZ = C * Z
    j = iota((FP, CZ * MAIN), 1)
    target = (lax.rem(j // MAIN, Z) * C + j // (Z * MAIN)) * (MAIN + R2) + lax.rem(j, MAIN)
    pm[...] = (iota((FP, CZ * MAIN), 0) == target).astype(BF)
    j = iota((FP, X * CZ * R2), 1)
    target = (lax.rem(j // R2, Z) * C + lax.rem(j // (Z * R2), C)) * (MAIN + R2)
    target += MAIN + lax.rem(j, R2)
    hit = iota((FP, X * CZ * R2), 0) == target
    for x_ in range(X):
        pr[x_] = (hit & (j // (CZ * R2) == x_)).astype(BF)

    lane = iota((1, FP), 1)
    inside = lane < F
    head = [(lane >= h * HD) & (lane < (h + 1) * HD) for h in range(H)]

    def narrow(slices):
        rest = None
        for x_ in range(X):
            part = slices[x_]
            mp[:, x_ * CZ * MAIN : (x_ + 1) * CZ * MAIN] = mm(part, pm[...]).astype(BF)
            more = mm(part, pr[x_])
            rest = more if rest is None else rest + more
        mpr[...] = rest.astype(BF)

    def natural(main, rest, x_):
        return mm_nt(main[:, x_ * CZ * MAIN : (x_ + 1) * CZ * MAIN], pm[...]) + mm_nt(rest, pr[x_])

    def norm(xw, at):
        total = None
        for n in range(Y):
            part = jnp.sum(xw[n].astype(F32), axis=-1, keepdims=True)
            total = part if total is None else total + part
        mean = total * (1.0 / N)
        total = None
        for n in range(Y):
            center = jnp.where(inside, xw[n].astype(F32) - mean, 0.0)
            part = jnp.sum(center * center, axis=-1, keepdims=True)
            total = part if total is None else total + part
        inverse = lax.rsqrt(total * (1.0 / N) + EPS)
        stat[2 * at] = mean
        stat[2 * at + 1] = inverse
        slices = []
        for n in range(Y):
            normed = (xw[n].astype(F32) - mean) * inverse
            slices.append((normed * (1.0 + mod[3 * at + 1, n]) + mod[3 * at, n]).astype(BF))
        narrow(slices)

    K = X * CZ * MAIN

    def weight(b, k):
        return (Wt if b else Ws)[k].reshape(K, FP), Wr[b * 4 + k]

    def project(b):
        for k in range(3):
            main, rest = weight(b, k)
            qkv[b, k] = (mm(mp[...], main) + mm(mpr[...], rest)).astype(BF)

    def spread(value):
        zero = jnp.zeros_like(value)
        return jnp.concatenate([jnp.where(head[h], value, zero) for h in range(H)], axis=0)

    def gather_heads(value):
        total = None
        for h in range(H):
            part = jnp.where(head[h], value[h * T : (h + 1) * T], 0.0)
            total = part if total is None else total + part
        return total.astype(BF)

    SCALE = HD ** (-0.5)

    def attend(b):
        scores = mm_nt(spread(qkv[b, 0]), qkv[b, 1]) * SCALE
        if b == 0:
            query_frame = lax.rem(iota((H * T, T), 0), T) // (G * Z)
            same = query_frame == iota((H * T, T), 1) // (G * Z)
            scores = jnp.where(same, scores, -1e30)
        weights = jnp.exp(scores - jnp.max(scores, axis=-1, keepdims=True))
        prob[b] = weights / jnp.sum(weights, axis=-1, keepdims=True)
        return gather_heads(mm(prob[b].astype(BF), qkv[b, 2]))

    def attend_back(b, grad):
        grads = spread(grad)
        likely = prob[b]
        grad_values = mm_tn(likely.astype(BF), grads).astype(BF)
        grad_likely = mm_nt(grads, qkv[b, 2])
        shift = grad_likely - jnp.sum(likely * grad_likely, axis=-1, keepdims=True)
        grad_scores = (likely * shift * SCALE).astype(BF)
        grad_query = gather_heads(mm(grad_scores, qkv[b, 1]))
        grad_keys = mm_tn(grad_scores, spread(qkv[b, 0])).astype(BF)
        return grad_query, grad_keys, grad_values

    def out_partial(b, flat, buf):
        main, rest = weight(b, 3)
        part = mm_nt(flat, main).astype(BF)
        part_rest = mm_nt(flat, rest).astype(BF)
        for n in range(Y):
            buf[n] = natural(part, part_rest, n).astype(BF)

    def grad_heads(b):
        main, rest = weight(b, 3)
        return (mm(mp[...], main) + mm(mpr[...], rest)).astype(BF)

    def in_partial(b, grads, xw, buf):
        part, part_rest = None, None
        for k in range(3):
            main, rest = weight(b, k)
            a, r = mm_nt(grads[k], main), mm_nt(grads[k], rest)
            part = a if part is None else part + a
            part_rest = r if part_rest is None else part_rest + r
        part, part_rest = part.astype(BF), part_rest.astype(BF)
        mean, inverse = stat[2 * b], stat[2 * b + 1]
        first, second = None, None
        slices = []
        for n in range(Y):
            value = natural(part, part_rest, n)
            slices.append(value)
            scaled = value * (1.0 + mod[3 * b + 1, n])
            normed = (xw[n].astype(F32) - mean) * inverse
            a = jnp.sum(scaled, axis=-1, keepdims=True)
            r = jnp.sum(scaled * normed, axis=-1, keepdims=True)
            first = a if first is None else first + a
            second = r if second is None else second + r
        for n in range(Y):
            value = jnp.where(lane == F, first, jnp.where(lane == F + 1, second, slices[n]))
            buf[n] = value.astype(BF)

    def in_finish(b, buf, xw, incoming):
        total = buf[0].astype(F32)
        for n in range(1, Y):
            total = total + buf[n].astype(F32)
        first = total[:, F : F + 1] * (1.0 / N)
        second = total[:, F + 1 : F + 2] * (1.0 / N)
        scaled = total * (1.0 + mod[3 * b + 1, y])
        normed = (xw[y].astype(F32) - stat[2 * b]) * stat[2 * b + 1]
        grad = stat[2 * b + 1] * (scaled - first - normed * second)
        return jnp.where(inside, incoming.astype(F32) + grad, 0.0).astype(BF)

    def add_up(buf):
        total = buf[0].astype(F32)
        for n in range(1, Y):
            total = total + buf[n].astype(F32)
        return total

    def gated(b, value):
        return (mod[3 * b + 2, y] * value.astype(F32)).astype(BF)

    FULL = FP - 128
    WP = 128 - (F - FULL)

    def shift_lanes(n):
        a, b = iota((FP, 128), 0), iota((FP, 128), 1)
        return ((a - n * WP == b - (128 - WP)) & (b >= 128 - WP)).astype(BF)

    def wg_start(b, flat):
        main = mm_tn(mp[...], flat).astype(BF)
        rest = mm_tn(mpr[...], flat).astype(BF)
        wgp[b, :, :, :Z] = main.reshape(X, C, Z, MAIN, FP)
        wgp[b, :, :, Z] = rest.reshape(X, C, Z * R2, FP)
        send(wgp.at[b, :, 1 - c], wgc.at[b], names["wc%d" % b], sibling)

    def wg_second(b):
        recv(wgc.at[b], names["wc%d" % b])
        wgx[b] = (wgp[b, :, c].astype(F32) + wgc[b].astype(F32)).astype(BF)
        ex_send(lambda p: wgx.at[b, p], wgxr.at[b], names["wx%d" % b], X, x, dev_x)
        wgxr[b, x] = wgx[b, x]

    def wg_third(b):
        ex_wait(wgxr.at[b], names["wx%d" % b], X, x)
        total = wgxr[b, 0].astype(F32)
        for n in range(1, X):
            total = total + wgxr[b, n].astype(F32)
        total = total.astype(BF)
        main, rest = total[:Z].reshape(Z * MAIN, FP), total[Z]
        wgz[b, :, :, :FULL] = main[:, :FULL].reshape(Z, MAIN, FULL)
        tail = main[:, FULL:].astype(F32)
        for n in range(F // WP):
            pick = shift_lanes(n)
            o = iota((Z * MAIN, Z * R2), 0)
            slot = lax.rem(o, MAIN) - n * R2
            rows = (o // MAIN) * R2 + slot == iota((Z * MAIN, Z * R2), 1)
            rows = (rows & (slot >= 0) & (slot < R2)).astype(BF)
            tail = tail + mm(rows, mm(rest, pick).astype(BF))
        wgz[b, :, :, FULL:] = tail.astype(BF).reshape(Z, MAIN, 128)
        ex_send(
            lambda p: wgz.at[b, lax.rem(p, Z)], wgzr.at[b], names["wz%d" % b], ZG, zg, dev_zg
        )
        wgzr[b, zg] = wgz[b, z]

    def wg_end(b, ref):
        ex_wait(wgzr.at[b], names["wz%d" % b], ZG, zg)
        total = wgzr[b, 0].astype(F32)
        for n in range(1, ZG):
            total = total + wgzr[b, n].astype(F32)
        ref[:MAIN, :FULL] = total[:, :FULL]
        tail = total[:, FULL:]
        ref[:MAIN, FULL:] = tail[:, : F - FULL]
        for n in range(F // WP):
            ref[MAIN : MAIN + R2, n * WP : (n + 1) * WP] = tail[n * R2 : (n + 1) * R2, 128 - WP :]

    late = 2

    def arrived(i, z_):
        x_hop(i)
        if i >= late:
            x_take(i - late)

    z_chain(0, arrived)
    z_start(1)

    ex_wait(cot_b, names["cot_x"], G, g)
    z_put(cot_c.at[0], to_z(flatten(cot_b)))
    ex_send(lambda p: cot_c.at[0, p], cot_c.at[1], names["cot_z"], Z, z, dev_z)
    cot_c[1, z] = cot_c[0, z]

    ex_wait(xw_s, names["tok"], Y, y)
    norm(xw_s, 0)

    for i in range(Z - late, Z):
        x_take(i)
    z_chain(1, lambda i, z_: None)
    if X > 2:
        for i in range(Z):
            x_last(i)
    for i in range(Z):
        recv(w_slot(0, x, 1 - c, order(i)), names["sib0"] + i)
        recv(w_slot(0, left, 1 - c, order(i)), names["sib0"] + Z + i)
        if X > 2:
            recv(w_slot(0, right, 1 - c, order(i)), names["sib0"] + 2 * Z + i)
            recv(w_slot(0, across, 1 - c, order(i)), names["sib0"] + 3 * Z + i)

    def to_sibling(x_, n):
        send(Wt.at[:, x_, c], Wt.at[:, x_, c], names["sib1"] + n, sibling)

    for k in range(1, X):
        to_x = lax.rem(x + k, X)
        send(Wt.at[:, x, c], Wt.at[:, x, c], names["xp1"] + k, dev_x(to_x))
    to_sibling(x, 0)

    ex_wait(cot_c.at[1], names["cot_z"], Z, z)
    cot_t = flatten(cot_c.at[1])
    gw_t[y] = gated(1, cot_t)
    ex_send(lambda p: gw_t.at[y], gw_t, names["ggt"], Y, y, dev_y)

    n_rest = CZ * 8 * R2
    o = iota((n_rest, n_rest), 0)
    source = lax.rem(o // R2, CZ) * (8 * R2) + o // (CZ * R2) * R2 + lax.rem(o, R2)
    shuffle = (iota((n_rest, n_rest), 1) == source).astype(BF)
    for x_ in range(X):
        rest = mm(shuffle, Ws[4, x_].reshape(n_rest, FP)).astype(BF)
        Wr[:, x_ * CZ * R2 : (x_ + 1) * CZ * R2] = rest.reshape(8, CZ * R2, FP)

    project(0)
    flat_s[...] = attend(0)
    out_partial(0, flat_s[...], rs1_a)
    ex_send(lambda p: rs1_a.at[p], rs1_b, names["rs1"], Y, y, dev_y)
    rs1_b[y] = rs1_a[y]

    for k in range(1, X):
        x_ = lax.rem(x + X - k, X)
        recv(Wt.at[:, x_, c], names["xp1"] + k)
        to_sibling(x_, k)

    ex_wait(rs1_b, names["rs1"], Y, y)
    first = xw_s[y].astype(F32) + mod[2, y] * add_up(rs1_b)
    x_put(fst_a, to_groups(first.astype(BF)))
    ex_send(lambda p: fst_a.at[p], fst_b, names["fst_x"], G, g, dev_g)
    fst_b[g] = fst_a[g]

    for k in range(X):
        recv(Wt.at[:, lax.rem(x + X - k, X), 1 - c], names["sib1"] + k)
    ex_wait(gw_t, names["ggt"], Y, y)

    ex_wait(fst_b, names["fst_x"], G, g)
    z_put(fst_c, to_z(flatten(fst_b)))
    ex_send(lambda p: fst_c.at[p], fst_d, names["fst_z"], Z, z, dev_z)
    fst_d[z] = fst_c[z]

    ex_wait(fst_d, names["fst_z"], Z, z)
    xw_t[y] = flatten(fst_d)
    ex_send(lambda p: xw_t.at[y], xw_t, names["fst"], Y, y, dev_y)

    narrow([gw_t[n] for n in range(Y)])
    grad_t = grad_heads(1)

    ex_wait(xw_t, names["fst"], Y, y)
    norm(xw_t, 1)
    project(1)
    flat_t = attend(1)
    grads = attend_back(1, grad_t)
    in_partial(1, grads, xw_t, rsg_a)
    ex_send(lambda p: rsg_a.at[p], rsg_b, names["rsg"], Y, y, dev_y)
    rsg_b[y] = rsg_a[y]

    out_partial(1, flat_t, rsp_a)
    ex_send(lambda p: rsp_a.at[p], rsp_b, names["rsp"], Y, y, dev_y)
    rsp_b[y] = rsp_a[y]

    ex_wait(rsg_b, names["rsg"], Y, y)
    z_put(fg_a, in_finish(1, rsg_b, xw_t, cot_t))
    ex_send(lambda p: fg_a.at[p], fg_b, names["fg_z"], Z, z, dev_z)
    fg_b[z] = fg_a[z]

    narrow([gw_t[n] for n in range(Y)])
    wg_start(1, flat_t)

    ex_wait(fg_b, names["fg_z"], Z, z)
    x_put(fg_c, from_z(flatten(fg_b)))
    ex_send(lambda p: fg_c.at[p], fg_d, names["fg_x"], G, g, dev_g)
    fg_d[g] = fg_c[g]

    ex_wait(rsp_b, names["rsp"], Y, y)
    second = xw_t[y].astype(F32) + mod[5, y] * add_up(rsp_b)
    z_put(out_a, second.astype(BF))
    ex_send(lambda p: out_a.at[p], out_b, names["out_z"], Z, z, dev_z)
    out_b[z] = out_a[z]

    ex_wait(fg_d, names["fg_x"], G, g)
    fg_e[...] = from_groups(flatten(fg_d))
    gw_s[y] = gated(0, fg_e[...])
    ex_send(lambda p: gw_s.at[y], gw_s, names["ggs"], Y, y, dev_y)

    wg_second(1)
    ex_wait(out_b, names["out_z"], Z, z)
    x_put(out_c, from_z(flatten(out_b)))
    ex_send(lambda p: out_c.at[p], out_d, names["out_x"], G, g, dev_g)
    out_d[g] = out_c[g]

    ex_wait(gw_s, names["ggs"], Y, y)
    narrow([gw_s[n] for n in range(Y)])
    wg_start(0, flat_s[...])
    grad_s = grad_heads(0)
    wg_third(1)
    wg_second(0)
    grads = attend_back(0, grad_s)
    wg_third(0)
    in_partial(0, grads, xw_s, rsf_a)
    ex_send(lambda p: rsf_a.at[p], rsf_b, names["rsf"], Y, y, dev_y)
    rsf_b[y] = rsf_a[y]

    ex_wait(out_d, names["out_x"], G, g)
    out[...] = from_groups(flatten(out_d))[:, :F]
    wg_end(1, wg_t)
    ex_wait(rsf_b, names["rsf"], Y, y)
    igrad[...] = in_finish(0, rsf_b, xw_s, fg_e[...])[:, :F]
    wg_end(0, wg_s)
    for copy in sent:
        copy.wait_send()


def on_device(sizes, tokens, modulation, qkv_s, out_s, qkv_t, out_t, cotangent):
    DP, S, Y = sizes
    frames, patches, F = tokens.shape[1:]
    T = frames * patches
    X, C = Y, 2
    Z = S // (X * C)
    G = X * C
    H = F // HD
    rows = out_s.shape[0]
    R2 = rows - MAIN
    FP = (F + 2 + 127) // 128 * 128
    dims = (X, C, Z, Y, DP, T, F, FP, H, R2)
    names, count = layout(X, C, Z, Y, DP)

    def joined(qkv, out):
        both = jnp.concatenate([qkv.transpose(1, 0, 2), out[None]], axis=0)
        return jnp.pad(both, ((0, 0), (0, 0), (0, FP - F)))

    first, second = joined(qkv_s, out_s), joined(qkv_t, out_t)
    rest = jnp.concatenate([first[:, MAIN:], second[:, MAIN:]]).reshape(1, 8 * R2, FP)
    wown = jnp.concatenate([first[:, :MAIN], rest])
    wown_t = second[:, :MAIN]

    K, KR = X * C * Z * MAIN, X * C * Z * R2
    xs, zs = pltpu.VMEM((G, 2 * Z, FP), BF), pltpu.VMEM((Z, 2 * G, FP), BF)
    wide = pltpu.VMEM((Y, T, FP), BF)
    scratch = [
        pltpu.SemaphoreType.DMA((count,)),
        pltpu.SemaphoreType.DMA((count,)),
        pltpu.VMEM((6, Y, 1, FP), F32),
        pltpu.VMEM((FP, C * Z * MAIN), BF),
        pltpu.VMEM((X, FP, KR), BF),
        wide, wide, wide, wide,
        pltpu.VMEM((5, X, C, Z, MAIN, FP), BF),
        pltpu.VMEM((4, X, C, Z, MAIN, FP), BF),
        pltpu.VMEM((8, KR, FP), BF),
        pltpu.VMEM((T, FP), BF),
        xs, xs, pltpu.VMEM((2, Z, 2 * G, FP), BF),
        xs, xs, zs, zs,
        zs, zs, xs, xs, pltpu.VMEM((T, FP), BF),
        zs, zs, xs, xs,
        pltpu.VMEM((T, K), BF),
        pltpu.VMEM((T, KR), BF),
        pltpu.VMEM((2, 3, T, FP), BF),
        pltpu.VMEM((2, H * T, T), F32),
        pltpu.VMEM((T, FP), BF),
        pltpu.VMEM((4, T, 1), F32),
        wide, wide, wide, wide, wide, wide, wide, wide,
        pltpu.VMEM((2, X, C, Z + 1, MAIN, FP), BF),
        pltpu.VMEM((2, X, Z + 1, MAIN, FP), BF),
        pltpu.VMEM((2, X, Z + 1, MAIN, FP), BF),
        pltpu.VMEM((2, X, Z + 1, MAIN, FP), BF),
        pltpu.VMEM((2, Z, MAIN, FP), BF),
        pltpu.VMEM((2, DP * Z, MAIN, FP), BF),
    ]
    vmem = pl.BlockSpec(memory_space=pltpu.VMEM)
    out, igrad, wg_s, wg_t = pl.pallas_call(
        functools.partial(kernel, dims, names),
        out_shape=(
            jax.ShapeDtypeStruct((T, F), BF),
            jax.ShapeDtypeStruct((T, F), BF),
            jax.ShapeDtypeStruct((rows, F), F32),
            jax.ShapeDtypeStruct((rows, F), F32),
        ),
        in_specs=[vmem] * 5,
        out_specs=(vmem,) * 4,
        scratch_shapes=scratch,
        compiler_params=pltpu.CompilerParams(
            collective_id=0, has_side_effects=True, vmem_limit_bytes=56 * 2**20
        ),
    )(tokens.reshape(T, F), cotangent.reshape(T, F), modulation[0], wown, wown_t)
    shape = (1, frames, patches, F)
    return out.reshape(shape), igrad.reshape(shape), wg_s, wg_t


def solution(mesh):
    sizes = tuple(mesh.shape[a] for a in ("dp", "seq", "tp"))
    placed = (
        P("dp", "seq", None, "tp"),
        P("dp", None, None),
        P("seq", None, "tp"),
        P("seq", "tp"),
        P("seq", None, "tp"),
        P("seq", "tp"),
        P("dp", "seq", None, "tp"),
    )
    return jax.shard_map(
        functools.partial(on_device, sizes),
        mesh=mesh,
        in_specs=placed,
        out_specs=(
            P("dp", "seq", None, "tp"),
            P("dp", "seq", None, "tp"),
            P("seq", "tp"),
            P("seq", "tp"),
        ),
        check_vma=False,
    )
```

```python
import functools

import jax
import jax.numpy as jnp
from jax import lax
from jax.experimental import pallas as pl
from jax.experimental.pallas import tpu as pltpu
from jax.sharding import PartitionSpec as P

HD = 72
EPS = 1e-06
MAIN = 16
MESH = pl.DeviceIdType.MESH
BF = jnp.bfloat16
F32 = jnp.float32


def mm(a, b):
    return lax.dot_general(a, b, (((1,), (0,)), ((), ())), preferred_element_type=F32)


def mm_nt(a, b):
    return lax.dot_general(a, b, (((1,), (1,)), ((), ())), preferred_element_type=F32)


def mm_tn(a, b):
    return lax.dot_general(a, b, (((0,), (0,)), ((), ())), preferred_element_type=F32)


def iota(shape, axis):
    return lax.broadcasted_iota(jnp.int32, shape, axis)


class Sems:
    def __init__(self):
        self.count = 0

    def take(self, n):
        first = self.count
        self.count += n
        return first


def layout(X, C, Z, Y, DP):
    s = Sems()
    names = {}
    G = X * C
    for name in ("tok", "ggt", "rs1", "fst", "rsg", "rsp", "ggs", "rsf"):
        names[name] = s.take(Y)
    for name in ("cot_x", "fst_x", "fg_x", "out_x"):
        names[name] = s.take(G)
    for name in ("cot_z", "fst_z", "fg_z", "out_z"):
        names[name] = s.take(Z)
    for name in ("zu0", "zd0", "zu1", "zd1", "xr0", "xl0", "xo0"):
        names[name] = s.take(Z)
    names["sib0"] = s.take(X * Z)
    names["xp1"] = s.take(X)
    names["sib1"] = s.take(X)
    for b in (0, 1):
        names["wc%d" % b] = s.take(1)
        names["wx%d" % b] = s.take(X)
        names["wz%d" % b] = s.take(DP * Z)
    return names, s.count


def kernel(dims, names, tok, cot, mods, wown, wown_t, out, igrad, wg_s, wg_t, *refs):
    X, C, Z, Y, DP, T, F, FP, H, R2 = dims
    G = X * C
    N = Y * F
    (
        ssem, rsem, mod, pm, pr, xw_s, xw_t, gw_t, gw_s, Ws, Wt, Wr, cotp,
        cot_a, cot_b, cot_c, fst_a, fst_b, fst_c, fst_d, fg_a, fg_b, fg_c, fg_d, fg_e,
        out_a, out_b, out_c, out_d,
        mp, mpr, qkv, prob, flat_s, stat,
        rs1_a, rs1_b, rsg_a, rsg_b, rsp_a, rsp_b, rsf_a, rsf_b,
        wgp, wgc, wgx, wgxr, wgz, wgzr,
    ) = refs

    d = lax.axis_index("dp")
    s = lax.axis_index("seq")
    y = lax.axis_index("tp")
    x = s // (Z * C)
    z = lax.rem(s // C, Z)
    c = lax.rem(s, C)
    g = x * C + c
    zg = d * Z + z

    def seq_of(x_, z_, c_):
        return (x_ * Z + z_) * C + c_

    def dev(d_, x_, z_, c_, y_):
        return {"dp": d_, "seq": seq_of(x_, z_, c_), "tp": y_}

    def dev_y(y_):
        return dev(d, x, z, c, y_)

    def dev_g(g_):
        return dev(d, g_ // C, z, lax.rem(g_, C), y)

    def dev_z(z_):
        return dev(d, x, z_, c, y)

    def dev_zg(zg_):
        return dev(zg_ // Z, x, lax.rem(zg_, Z), c, y)

    def dev_x(x_):
        return dev(d, x_, z, c, y)

    sibling = dev(d, x, z, 1 - c, y)
    ZG = DP * Z
    sent = []

    def send(src, dst, sem, device):
        copy = pltpu.make_async_remote_copy(
            src_ref=src, dst_ref=dst, send_sem=ssem.at[sem], recv_sem=rsem.at[sem],
            device_id=device, device_id_type=MESH,
        )
        copy.start()
        sent.append(copy)

    def recv(dst, sem):
        pltpu.make_async_remote_copy(
            src_ref=dst, dst_ref=dst, send_sem=ssem.at[sem], recv_sem=rsem.at[sem],
            device_id=sibling, device_id_type=MESH,
        ).wait_recv()

    def ex_send(src, dst, sem, n, me, device):
        for k in range(1, n):
            peer = lax.rem(me + k, n)
            send(src(peer), dst.at[me], sem + k, device(peer))

    def ex_wait(dst, sem, n, me):
        for k in range(1, n):
            recv(dst.at[lax.rem(me + n - k, n)], sem + k)

    barrier = pltpu.get_barrier_semaphore()
    peers = [dev_y(lax.rem(y + k, Y)) for k in range(1, Y)]
    peers += [dev_g(lax.rem(g + k, G)) for k in range(1, G)]
    peers += [dev_zg(lax.rem(zg + k, ZG)) for k in range(1, ZG)]
    for peer in peers:
        pl.semaphore_signal(barrier, inc=1, device_id=peer, device_id_type=MESH)
    pl.semaphore_wait(barrier, len(peers))

    up, down = dev_zg(lax.rem(zg + 1, ZG)), dev_zg(lax.rem(zg + ZG - 1, ZG))
    right, left = lax.rem(x + 1, X), lax.rem(x + X - 1, X)
    across = lax.rem(x + X // 2, X)
    nup = Z // 2
    ndown = Z - 1 - nup

    def w_slot(b, x_, c_, z_):
        return (Wt if b else Ws).at[:, x_, c_, z_]

    def z_hop(step, first, b):
        z_ = lax.rem(z + first * step + Z * Z, Z)
        slot = w_slot(b, x, c, z_)
        src = (wown_t if b else wown) if step == 0 else slot
        send(src, slot, names["z%s%d" % ("u" if first < 0 else "d", b)] + step, up if first < 0 else down)

    def z_take(step, first, b):
        z_ = lax.rem(z + first * (step + 1) + Z * Z, Z)
        recv(w_slot(b, x, c, z_), names["z%s%d" % ("u" if first < 0 else "d", b)] + step)
        return z_

    def z_start(b):
        if nup:
            z_hop(0, -1, b)
        if ndown:
            z_hop(0, 1, b)

    def z_step(b, step):
        z_take(step, -1, b)
        if step + 1 < nup:
            z_hop(step + 1, -1, b)
        if step >= ndown:
            return [2 * step + 1]
        z_take(step, 1, b)
        if step + 1 < ndown:
            z_hop(step + 1, 1, b)
        return [2 * step + 1, 2 * step + 2]

    def order(i):
        return lax.rem(z + (-(i + 1) // 2 if i % 2 else i // 2) + Z, Z)

    def x_hop(i, own=False):
        slot = w_slot(0, x, c, order(i))
        src = wown if own else slot
        send(src, slot, names["xr0"] + i, dev_x(right))
        if X > 2:
            send(src, slot, names["xl0"] + i, dev_x(left))
        send(src, w_slot(0, x, c, order(i)), names["sib0"] + i, sibling)

    def x_take(i):
        recv(w_slot(0, left, c, order(i)), names["xr0"] + i)
        if X > 2:
            slot = w_slot(0, left, c, order(i))
            if i % 2 == 0:
                send(slot, slot, names["xo0"] + i, dev_x(right))
            send(slot, slot, names["sib0"] + Z + i, sibling)
            slot = w_slot(0, right, c, order(i))
            recv(slot, names["xl0"] + i)
            if i % 2 == 1:
                send(slot, slot, names["xo0"] + i, dev_x(left))
            send(slot, slot, names["sib0"] + 2 * Z + i, sibling)
        else:
            slot = w_slot(0, left, c, order(i))
            send(slot, slot, names["sib0"] + Z + i, sibling)

    def x_last(i):
        slot = w_slot(0, across, c, order(i))
        recv(slot, names["xo0"] + i)
        send(slot, slot, names["sib0"] + 3 * Z + i, sibling)

    z_start(0)
    x_hop(0, True)
    xw_s[y] = jnp.zeros((T, FP), BF)
    xw_s[y, :, :F] = tok[...]
    ex_send(lambda p: xw_s.at[y], xw_s, names["tok"], Y, y, dev_y)
    cotp[...] = jnp.zeros((T, FP), BF)
    cotp[:, :F] = cot[...]

    row = iota((T, T), 0)
    col = iota((T, T), 1)

    def swap_rows(value, source):
        return mm((col == source).astype(BF), value).astype(BF)

    def to_groups(value):
        return swap_rows(value, lax.rem(row // Z, 2) * (G * Z) + row // (2 * Z) * Z + lax.rem(row, Z))

    def from_groups(value):
        return swap_rows(
            value, lax.rem(row // Z, G) * (2 * Z) + row // (G * Z) * Z + lax.rem(row, Z)
        )

    def to_z(value):
        return swap_rows(value, lax.rem(row, 2 * G) * Z + row // (2 * G))

    def from_z(value):
        return swap_rows(value, lax.rem(row, Z) * (2 * G) + row // Z)

    def x_put(buf, value):
        buf[...] = value.reshape(G, 2 * Z, FP)

    def z_put(buf, value):
        buf[...] = value.reshape(Z, 2 * G, FP)

    def flatten(buf):
        return buf[...].reshape(T, FP)

    x_put(cot_a, to_groups(cotp[...]))
    ex_send(lambda p: cot_a.at[p], cot_b, names["cot_x"], G, g, dev_g)
    cot_b[g] = cot_a[g]
    for k in range(5):
        Ws[k, x, c, z] = wown[k]
    for k in range(4):
        Wt[k, x, c, z] = wown_t[k]
    mod[...] = jnp.zeros((6, Y, 1, FP), F32)
    for i in range(6):
        for n in range(Y):
            mod[i, n, :, :F] = mods[i : i + 1, n * F : (n + 1) * F]

    CZ = C * Z
    j = iota((FP, CZ * MAIN), 1)
    target = (lax.rem(j // MAIN, Z) * C + j // (Z * MAIN)) * (MAIN + R2) + lax.rem(j, MAIN)
    pm[...] = (iota((FP, CZ * MAIN), 0) == target).astype(BF)
    j = iota((FP, X * CZ * R2), 1)
    target = (lax.rem(j // R2, Z) * C + lax.rem(j // (Z * R2), C)) * (MAIN + R2)
    target += MAIN + lax.rem(j, R2)
    hit = iota((FP, X * CZ * R2), 0) == target
    for x_ in range(X):
        pr[x_] = (hit & (j // (CZ * R2) == x_)).astype(BF)

    lane = iota((1, FP), 1)
    inside = lane < F
    head = [(lane >= h * HD) & (lane < (h + 1) * HD) for h in range(H)]

    def narrow(slices):
        rest = None
        for x_ in range(X):
            part = slices[x_]
            mp[:, x_ * CZ * MAIN : (x_ + 1) * CZ * MAIN] = mm(part, pm[...]).astype(BF)
            more = mm(part, pr[x_])
            rest = more if rest is None else rest + more
        mpr[...] = rest.astype(BF)

    def natural(main, rest, x_):
        return mm_nt(main[:, x_ * CZ * MAIN : (x_ + 1) * CZ * MAIN], pm[...]) + mm_nt(rest, pr[x_])

    def norm(xw, at):
        total = None
        for n in range(Y):
            part = jnp.sum(xw[n].astype(F32), axis=-1, keepdims=True)
            total = part if total is None else total + part
        mean = total * (1.0 / N)
        total = None
        for n in range(Y):
            center = jnp.where(inside, xw[n].astype(F32) - mean, 0.0)
            part = jnp.sum(center * center, axis=-1, keepdims=True)
            total = part if total is None else total + part
        inverse = lax.rsqrt(total * (1.0 / N) + EPS)
        stat[2 * at] = mean
        stat[2 * at + 1] = inverse
        slices = []
        for n in range(Y):
            normed = (xw[n].astype(F32) - mean) * inverse
            slices.append((normed * (1.0 + mod[3 * at + 1, n]) + mod[3 * at, n]).astype(BF))
        narrow(slices)

    K = X * CZ * MAIN

    def weight(b, k):
        return (Wt if b else Ws)[k].reshape(K, FP), Wr[b * 4 + k]

    def project(b):
        for k in range(3):
            main, rest = weight(b, k)
            qkv[b, k] = (mm(mp[...], main) + mm(mpr[...], rest)).astype(BF)

    def spread(value):
        zero = jnp.zeros_like(value)
        return jnp.concatenate([jnp.where(head[h], value, zero) for h in range(H)], axis=0)

    def gather_heads(value):
        total = None
        for h in range(H):
            part = jnp.where(head[h], value[h * T : (h + 1) * T], 0.0)
            total = part if total is None else total + part
        return total.astype(BF)

    SCALE = HD ** (-0.5)

    def attend(b):
        scores = mm_nt(spread(qkv[b, 0]), qkv[b, 1]) * SCALE
        if b == 0:
            query_frame = lax.rem(iota((H * T, T), 0), T) // (G * Z)
            same = query_frame == iota((H * T, T), 1) // (G * Z)
            scores = jnp.where(same, scores, -1e30)
        weights = jnp.exp(scores - jnp.max(scores, axis=-1, keepdims=True))
        prob[b] = weights / jnp.sum(weights, axis=-1, keepdims=True)
        return gather_heads(mm(prob[b].astype(BF), qkv[b, 2]))

    def attend_back(b, grad):
        grads = spread(grad)
        likely = prob[b]
        grad_values = mm_tn(likely.astype(BF), grads).astype(BF)
        grad_likely = mm_nt(grads, qkv[b, 2])
        shift = grad_likely - jnp.sum(likely * grad_likely, axis=-1, keepdims=True)
        grad_scores = (likely * shift * SCALE).astype(BF)
        grad_query = gather_heads(mm(grad_scores, qkv[b, 1]))
        grad_keys = mm_tn(grad_scores, spread(qkv[b, 0])).astype(BF)
        return grad_query, grad_keys, grad_values

    def out_partial(b, flat, buf):
        main, rest = weight(b, 3)
        part = mm_nt(flat, main).astype(BF)
        part_rest = mm_nt(flat, rest).astype(BF)
        for n in range(Y):
            buf[n] = natural(part, part_rest, n).astype(BF)

    def grad_heads(b):
        main, rest = weight(b, 3)
        return (mm(mp[...], main) + mm(mpr[...], rest)).astype(BF)

    def in_partial(b, grads, xw, buf):
        part, part_rest = None, None
        for k in range(3):
            main, rest = weight(b, k)
            a, r = mm_nt(grads[k], main), mm_nt(grads[k], rest)
            part = a if part is None else part + a
            part_rest = r if part_rest is None else part_rest + r
        part, part_rest = part.astype(BF), part_rest.astype(BF)
        mean, inverse = stat[2 * b], stat[2 * b + 1]
        first, second = None, None
        slices = []
        for n in range(Y):
            value = natural(part, part_rest, n)
            slices.append(value)
            scaled = value * (1.0 + mod[3 * b + 1, n])
            normed = (xw[n].astype(F32) - mean) * inverse
            a = jnp.sum(scaled, axis=-1, keepdims=True)
            r = jnp.sum(scaled * normed, axis=-1, keepdims=True)
            first = a if first is None else first + a
            second = r if second is None else second + r
        for n in range(Y):
            value = jnp.where(lane == F, first, jnp.where(lane == F + 1, second, slices[n]))
            buf[n] = value.astype(BF)

    def in_finish(b, buf, xw, incoming):
        total = buf[0].astype(F32)
        for n in range(1, Y):
            total = total + buf[n].astype(F32)
        first = total[:, F : F + 1] * (1.0 / N)
        second = total[:, F + 1 : F + 2] * (1.0 / N)
        scaled = total * (1.0 + mod[3 * b + 1, y])
        normed = (xw[y].astype(F32) - stat[2 * b]) * stat[2 * b + 1]
        grad = stat[2 * b + 1] * (scaled - first - normed * second)
        return jnp.where(inside, incoming.astype(F32) + grad, 0.0).astype(BF)

    def add_up(buf):
        total = buf[0].astype(F32)
        for n in range(1, Y):
            total = total + buf[n].astype(F32)
        return total

    def gated(b, value):
        return (mod[3 * b + 2, y] * value.astype(F32)).astype(BF)

    FULL = FP - 128
    WP = 128 - (F - FULL)

    def shift_lanes(n):
        a, b = iota((FP, 128), 0), iota((FP, 128), 1)
        return ((a - n * WP == b - (128 - WP)) & (b >= 128 - WP)).astype(BF)

    def wg_start(b, flat):
        main = mm_tn(mp[...], flat).astype(BF)
        rest = mm_tn(mpr[...], flat).astype(BF)
        wgp[b, :, :, :Z] = main.reshape(X, C, Z, MAIN, FP)
        wgp[b, :, :, Z] = rest.reshape(X, C, Z * R2, FP)
        send(wgp.at[b, :, 1 - c], wgc.at[b], names["wc%d" % b], sibling)

    def wg_second(b):
        recv(wgc.at[b], names["wc%d" % b])
        wgx[b] = (wgp[b, :, c].astype(F32) + wgc[b].astype(F32)).astype(BF)
        ex_send(lambda p: wgx.at[b, p], wgxr.at[b], names["wx%d" % b], X, x, dev_x)
        wgxr[b, x] = wgx[b, x]

    def wg_third(b):
        ex_wait(wgxr.at[b], names["wx%d" % b], X, x)
        total = wgxr[b, 0].astype(F32)
        for n in range(1, X):
            total = total + wgxr[b, n].astype(F32)
        total = total.astype(BF)
        main, rest = total[:Z].reshape(Z * MAIN, FP), total[Z]
        wgz[b, :, :, :FULL] = main[:, :FULL].reshape(Z, MAIN, FULL)
        tail = main[:, FULL:].astype(F32)
        for n in range(F // WP):
            pick = shift_lanes(n)
            o = iota((Z * MAIN, Z * R2), 0)
            slot = lax.rem(o, MAIN) - n * R2
            rows = (o // MAIN) * R2 + slot == iota((Z * MAIN, Z * R2), 1)
            rows = (rows & (slot >= 0) & (slot < R2)).astype(BF)
            tail = tail + mm(rows, mm(rest, pick).astype(BF))
        wgz[b, :, :, FULL:] = tail.astype(BF).reshape(Z, MAIN, 128)
        ex_send(
            lambda p: wgz.at[b, lax.rem(p, Z)], wgzr.at[b], names["wz%d" % b], ZG, zg, dev_zg
        )
        wgzr[b, zg] = wgz[b, z]

    def wg_end(b, ref):
        ex_wait(wgzr.at[b], names["wz%d" % b], ZG, zg)
        total = wgzr[b, 0].astype(F32)
        for n in range(1, ZG):
            total = total + wgzr[b, n].astype(F32)
        ref[:MAIN, :FULL] = total[:, :FULL]
        tail = total[:, FULL:]
        ref[:MAIN, FULL:] = tail[:, : F - FULL]
        for n in range(F // WP):
            ref[MAIN : MAIN + R2, n * WP : (n + 1) * WP] = tail[n * R2 : (n + 1) * R2, 128 - WP :]

    before = [0]
    for step in range(nup):
        here = z_step(0, step)
        for i in here:
            x_hop(i)
        for i in before:
            x_take(i)
        before = here
    z_start(1)

    ex_wait(cot_b, names["cot_x"], G, g)
    z_put(cot_c.at[0], to_z(flatten(cot_b)))
    ex_send(lambda p: cot_c.at[0, p], cot_c.at[1], names["cot_z"], Z, z, dev_z)
    cot_c[1, z] = cot_c[0, z]

    ex_wait(xw_s, names["tok"], Y, y)
    norm(xw_s, 0)

    for i in before:
        x_take(i)
    if X > 2:
        for i in range(Z):
            x_last(i)
    for i in range(Z):
        recv(w_slot(0, x, 1 - c, order(i)), names["sib0"] + i)
        recv(w_slot(0, left, 1 - c, order(i)), names["sib0"] + Z + i)
        if X > 2:
            recv(w_slot(0, right, 1 - c, order(i)), names["sib0"] + 2 * Z + i)
            recv(w_slot(0, across, 1 - c, order(i)), names["sib0"] + 3 * Z + i)

    def to_sibling(x_, n):
        send(Wt.at[:, x_, c], Wt.at[:, x_, c], names["sib1"] + n, sibling)

    z_steps = iter(range(nup))

    def z_later(n):
        for _ in range(n):
            step = next(z_steps, None)
            if step is not None:
                z_step(1, step)

    z_later(1)

    ex_wait(cot_c.at[1], names["cot_z"], Z, z)
    cot_t = flatten(cot_c.at[1])
    gw_t[y] = gated(1, cot_t)
    ex_send(lambda p: gw_t.at[y], gw_t, names["ggt"], Y, y, dev_y)

    n_rest = CZ * 8 * R2
    o = iota((n_rest, n_rest), 0)
    source = lax.rem(o // R2, CZ) * (8 * R2) + o // (CZ * R2) * R2 + lax.rem(o, R2)
    shuffle = (iota((n_rest, n_rest), 1) == source).astype(BF)
    for x_ in range(X):
        rest = mm(shuffle, Ws[4, x_].reshape(n_rest, FP)).astype(BF)
        Wr[:, x_ * CZ * R2 : (x_ + 1) * CZ * R2] = rest.reshape(8, CZ * R2, FP)

    project(0)
    z_later(1)
    flat_s[...] = attend(0)
    z_later(1)
    out_partial(0, flat_s[...], rs1_a)
    ex_send(lambda p: rs1_a.at[p], rs1_b, names["rs1"], Y, y, dev_y)
    rs1_b[y] = rs1_a[y]

    z_later(nup)
    for k in range(1, X):
        to_x = lax.rem(x + k, X)
        send(Wt.at[:, x, c], Wt.at[:, x, c], names["xp1"] + k, dev_x(to_x))
    to_sibling(x, 0)
    ex_wait(rs1_b, names["rs1"], Y, y)
    first = xw_s[y].astype(F32) + mod[2, y] * add_up(rs1_b)
    x_put(fst_a, to_groups(first.astype(BF)))
    ex_send(lambda p: fst_a.at[p], fst_b, names["fst_x"], G, g, dev_g)
    fst_b[g] = fst_a[g]
    ex_wait(fst_b, names["fst_x"], G, g)
    z_put(fst_c, to_z(flatten(fst_b)))
    ex_send(lambda p: fst_c.at[p], fst_d, names["fst_z"], Z, z, dev_z)
    fst_d[z] = fst_c[z]
    for k in range(1, X):
        x_ = lax.rem(x + X - k, X)
        recv(Wt.at[:, x_, c], names["xp1"] + k)
        to_sibling(x_, k)

    for k in range(X):
        recv(Wt.at[:, lax.rem(x + X - k, X), 1 - c], names["sib1"] + k)
    ex_wait(gw_t, names["ggt"], Y, y)

    ex_wait(fst_d, names["fst_z"], Z, z)
    xw_t[y] = flatten(fst_d)
    ex_send(lambda p: xw_t.at[y], xw_t, names["fst"], Y, y, dev_y)

    narrow([gw_t[n] for n in range(Y)])
    grad_t = grad_heads(1)

    ex_wait(xw_t, names["fst"], Y, y)
    norm(xw_t, 1)
    project(1)
    flat_t = attend(1)
    grads = attend_back(1, grad_t)
    in_partial(1, grads, xw_t, rsg_a)
    ex_send(lambda p: rsg_a.at[p], rsg_b, names["rsg"], Y, y, dev_y)
    rsg_b[y] = rsg_a[y]

    out_partial(1, flat_t, rsp_a)
    ex_send(lambda p: rsp_a.at[p], rsp_b, names["rsp"], Y, y, dev_y)
    rsp_b[y] = rsp_a[y]

    ex_wait(rsg_b, names["rsg"], Y, y)
    z_put(fg_a, in_finish(1, rsg_b, xw_t, cot_t))
    ex_send(lambda p: fg_a.at[p], fg_b, names["fg_z"], Z, z, dev_z)
    fg_b[z] = fg_a[z]

    narrow([gw_t[n] for n in range(Y)])
    wg_start(1, flat_t)

    ex_wait(fg_b, names["fg_z"], Z, z)
    x_put(fg_c, from_z(flatten(fg_b)))
    ex_send(lambda p: fg_c.at[p], fg_d, names["fg_x"], G, g, dev_g)
    fg_d[g] = fg_c[g]

    ex_wait(rsp_b, names["rsp"], Y, y)
    second = xw_t[y].astype(F32) + mod[5, y] * add_up(rsp_b)
    z_put(out_a, second.astype(BF))
    ex_send(lambda p: out_a.at[p], out_b, names["out_z"], Z, z, dev_z)
    out_b[z] = out_a[z]

    ex_wait(fg_d, names["fg_x"], G, g)
    fg_e[...] = from_groups(flatten(fg_d))
    gw_s[y] = gated(0, fg_e[...])
    ex_send(lambda p: gw_s.at[y], gw_s, names["ggs"], Y, y, dev_y)

    wg_second(1)
    ex_wait(out_b, names["out_z"], Z, z)
    x_put(out_c, from_z(flatten(out_b)))
    ex_send(lambda p: out_c.at[p], out_d, names["out_x"], G, g, dev_g)
    out_d[g] = out_c[g]

    ex_wait(gw_s, names["ggs"], Y, y)
    narrow([gw_s[n] for n in range(Y)])
    wg_start(0, flat_s[...])
    grad_s = grad_heads(0)
    wg_third(1)
    wg_second(0)
    grads = attend_back(0, grad_s)
    wg_third(0)
    in_partial(0, grads, xw_s, rsf_a)
    ex_send(lambda p: rsf_a.at[p], rsf_b, names["rsf"], Y, y, dev_y)
    rsf_b[y] = rsf_a[y]

    ex_wait(out_d, names["out_x"], G, g)
    out[...] = from_groups(flatten(out_d))[:, :F]
    wg_end(1, wg_t)
    ex_wait(rsf_b, names["rsf"], Y, y)
    igrad[...] = in_finish(0, rsf_b, xw_s, fg_e[...])[:, :F]
    wg_end(0, wg_s)
    for copy in sent:
        copy.wait_send()


def hand_on(*refs):
    for source, target in zip(refs[:4], refs[4:]):
        target[...] = source[...]


def on_device(sizes, tokens, modulation, qkv_s, out_s, qkv_t, out_t, cotangent):
    DP, S, Y = sizes
    frames, patches, F = tokens.shape[1:]
    T = frames * patches
    X, C = Y, 2
    Z = S // (X * C)
    G = X * C
    H = F // HD
    rows = out_s.shape[0]
    R2 = rows - MAIN
    FP = (F + 2 + 127) // 128 * 128
    dims = (X, C, Z, Y, DP, T, F, FP, H, R2)
    names, count = layout(X, C, Z, Y, DP)

    def joined(qkv, out):
        both = jnp.concatenate([qkv.transpose(1, 0, 2), out[None]], axis=0)
        return jnp.pad(both, ((0, 0), (0, 0), (0, FP - F)))

    first, second = joined(qkv_s, out_s), joined(qkv_t, out_t)
    rest = jnp.concatenate([first[:, MAIN:], second[:, MAIN:]]).reshape(1, 8 * R2, FP)
    wown = jnp.concatenate([first[:, :MAIN], rest])
    wown_t = second[:, :MAIN]

    K, KR = X * C * Z * MAIN, X * C * Z * R2
    xs, zs = pltpu.VMEM((G, 2 * Z, FP), BF), pltpu.VMEM((Z, 2 * G, FP), BF)
    wide = pltpu.VMEM((Y, T, FP), BF)
    scratch = [
        pltpu.SemaphoreType.DMA((count,)),
        pltpu.SemaphoreType.DMA((count,)),
        pltpu.VMEM((6, Y, 1, FP), F32),
        pltpu.VMEM((FP, C * Z * MAIN), BF),
        pltpu.VMEM((X, FP, KR), BF),
        wide, wide, wide, wide,
        pltpu.VMEM((5, X, C, Z, MAIN, FP), BF),
        pltpu.VMEM((4, X, C, Z, MAIN, FP), BF),
        pltpu.VMEM((8, KR, FP), BF),
        pltpu.VMEM((T, FP), BF),
        xs, xs, pltpu.VMEM((2, Z, 2 * G, FP), BF),
        xs, xs, zs, zs,
        zs, zs, xs, xs, pltpu.VMEM((T, FP), BF),
        zs, zs, xs, xs,
        pltpu.VMEM((T, K), BF),
        pltpu.VMEM((T, KR), BF),
        pltpu.VMEM((2, 3, T, FP), BF),
        pltpu.VMEM((2, H * T, T), F32),
        pltpu.VMEM((T, FP), BF),
        pltpu.VMEM((4, T, 1), F32),
        wide, wide, wide, wide, wide, wide, wide, wide,
        pltpu.VMEM((2, X, C, Z + 1, MAIN, FP), BF),
        pltpu.VMEM((2, X, Z + 1, MAIN, FP), BF),
        pltpu.VMEM((2, X, Z + 1, MAIN, FP), BF),
        pltpu.VMEM((2, X, Z + 1, MAIN, FP), BF),
        pltpu.VMEM((2, Z, MAIN, FP), BF),
        pltpu.VMEM((2, DP * Z, MAIN, FP), BF),
    ]
    vmem = pl.BlockSpec(memory_space=pltpu.VMEM)
    out, igrad, wg_s, wg_t = pl.pallas_call(
        functools.partial(kernel, dims, names),
        out_shape=(
            jax.ShapeDtypeStruct((T, F), BF),
            jax.ShapeDtypeStruct((T, F), BF),
            jax.ShapeDtypeStruct((rows, F), F32),
            jax.ShapeDtypeStruct((rows, F), F32),
        ),
        in_specs=[vmem] * 5,
        out_specs=(vmem,) * 4,
        scratch_shapes=scratch,
        compiler_params=pltpu.CompilerParams(
            collective_id=0, has_side_effects=True, vmem_limit_bytes=56 * 2**20
        ),
    )(tokens.reshape(T, F), cotangent.reshape(T, F), modulation[0], wown, wown_t)
    out, igrad, wg_s, wg_t = pl.pallas_call(
        hand_on,
        out_shape=tuple(jax.ShapeDtypeStruct(v.shape, v.dtype) for v in (out, igrad, wg_s, wg_t)),
        in_specs=[vmem] * 4,
        out_specs=(vmem,) * 4,
    )(out, igrad, wg_s, wg_t)
    shape = (1, frames, patches, F)
    return out.reshape(shape), igrad.reshape(shape), wg_s, wg_t


def solution(mesh):
    sizes = tuple(mesh.shape[a] for a in ("dp", "seq", "tp"))
    placed = (
        P("dp", "seq", None, "tp"),
        P("dp", None, None),
        P("seq", None, "tp"),
        P("seq", "tp"),
        P("seq", None, "tp"),
        P("seq", "tp"),
        P("dp", "seq", None, "tp"),
    )
    return jax.shard_map(
        functools.partial(on_device, sizes),
        mesh=mesh,
        in_specs=placed,
        out_specs=(
            P("dp", "seq", None, "tp"),
            P("dp", "seq", None, "tp"),
            P("seq", "tp"),
            P("seq", "tp"),
        ),
        check_vma=False,
    )
```

```python
import functools

import jax
import jax.numpy as jnp
from jax import lax
from jax.experimental import pallas as pl
from jax.experimental.pallas import tpu as pltpu
from jax.sharding import PartitionSpec as P

HD = 72
EPS = 1e-06
MAIN = 16
MESH = pl.DeviceIdType.MESH
BF = jnp.bfloat16
F32 = jnp.float32


def mm(a, b):
    return lax.dot_general(a, b, (((1,), (0,)), ((), ())), preferred_element_type=F32)


def mm_nt(a, b):
    return lax.dot_general(a, b, (((1,), (1,)), ((), ())), preferred_element_type=F32)


def mm_tn(a, b):
    return lax.dot_general(a, b, (((0,), (0,)), ((), ())), preferred_element_type=F32)


def iota(shape, axis):
    return lax.broadcasted_iota(jnp.int32, shape, axis)


class Sems:
    def __init__(self):
        self.count = 0

    def take(self, n):
        first = self.count
        self.count += n
        return first


def layout(X, C, Z, Y, DP):
    s = Sems()
    names = {}
    G = X * C
    for name in ("tok", "ggt", "rs1", "fst", "rsg", "rsp", "ggs", "rsf"):
        names[name] = s.take(Y)
    for name in ("cot_x", "fst_x", "fg_x", "out_x"):
        names[name] = s.take(G)
    for name in ("cot_z", "fst_z", "fg_z", "out_z"):
        names[name] = s.take(Z)
    for name in ("zu0", "zd0", "zu1", "zd1", "xr0", "xl0", "xo0"):
        names[name] = s.take(Z)
    names["sib0"] = s.take(X * Z)
    names["xp1"] = s.take(X)
    names["sib1"] = s.take(X)
    for b in (0, 1):
        names["wc%d" % b] = s.take(1)
        names["wx%d" % b] = s.take(X)
        names["wz%d" % b] = s.take(DP * Z)
    return names, s.count


def kernel(dims, names, tok, cot, mods, qkv_s, out_s, qkv_t, out_t, out, igrad, wg_s, wg_t, *refs):
    X, C, Z, Y, DP, T, F, FP, H, R2 = dims
    G = X * C
    N = Y * F
    (
        ssem, rsem, wown, wown_t, mod, pm, pr, xw_s, xw_t, gw_t, gw_s, Ws, Wt, Wr, cotp,
        cot_a, cot_b, cot_c, fst_a, fst_b, fst_c, fst_d, fg_a, fg_b, fg_c, fg_d, fg_e,
        out_a, out_b, out_c, out_d,
        mp, mpr, qkv, prob, flat_s, stat,
        rs1_a, rs1_b, rsg_a, rsg_b, rsp_a, rsp_b, rsf_a, rsf_b,
        wgp, wgc, wgx, wgxr, wgz, wgzr,
    ) = refs

    d = lax.axis_index("dp")
    s = lax.axis_index("seq")
    y = lax.axis_index("tp")
    x = s // (Z * C)
    z = lax.rem(s // C, Z)
    c = lax.rem(s, C)
    g = x * C + c
    zg = d * Z + z

    def seq_of(x_, z_, c_):
        return (x_ * Z + z_) * C + c_

    def dev(d_, x_, z_, c_, y_):
        return {"dp": d_, "seq": seq_of(x_, z_, c_), "tp": y_}

    def dev_y(y_):
        return dev(d, x, z, c, y_)

    def dev_g(g_):
        return dev(d, g_ // C, z, lax.rem(g_, C), y)

    def dev_z(z_):
        return dev(d, x, z_, c, y)

    def dev_zg(zg_):
        return dev(zg_ // Z, x, lax.rem(zg_, Z), c, y)

    def dev_x(x_):
        return dev(d, x_, z, c, y)

    sibling = dev(d, x, z, 1 - c, y)
    ZG = DP * Z
    sent = []

    def send(src, dst, sem, device):
        copy = pltpu.make_async_remote_copy(
            src_ref=src, dst_ref=dst, send_sem=ssem.at[sem], recv_sem=rsem.at[sem],
            device_id=device, device_id_type=MESH,
        )
        copy.start()
        sent.append(copy)

    def recv(dst, sem):
        pltpu.make_async_remote_copy(
            src_ref=dst, dst_ref=dst, send_sem=ssem.at[sem], recv_sem=rsem.at[sem],
            device_id=sibling, device_id_type=MESH,
        ).wait_recv()

    def ex_send(src, dst, sem, n, me, device):
        for k in range(1, n):
            peer = lax.rem(me + k, n)
            send(src(peer), dst.at[me], sem + k, device(peer))

    def ex_wait(dst, sem, n, me):
        for k in range(1, n):
            recv(dst.at[lax.rem(me + n - k, n)], sem + k)

    barrier = pltpu.get_barrier_semaphore()
    peers = [dev_y(lax.rem(y + k, Y)) for k in range(1, Y)]
    peers += [dev_g(lax.rem(g + k, G)) for k in range(1, G)]
    peers += [dev_zg(lax.rem(zg + k, ZG)) for k in range(1, ZG)]
    for peer in peers:
        pl.semaphore_signal(barrier, inc=1, device_id=peer, device_id_type=MESH)

    rows = MAIN + R2

    def widened(value):
        return jnp.concatenate([value, jnp.zeros((value.shape[0], FP - F), F32)], axis=1)

    rest = []
    for ref, qkv_ref, out_ref in ((wown, qkv_s, out_s), (wown_t, qkv_t, out_t)):
        value = qkv_ref[...].astype(F32)
        for k in range(4):
            part = value[:, k, :] if k < 3 else out_ref[...].astype(F32)
            part = widened(part.reshape(rows, F))
            ref[k] = part[:MAIN].astype(BF)
            rest.append(part[MAIN:])
    wown[4] = jnp.concatenate(rest, axis=0).astype(BF)

    pl.semaphore_wait(barrier, len(peers))

    up, down = dev_zg(lax.rem(zg + 1, ZG)), dev_zg(lax.rem(zg + ZG - 1, ZG))
    right, left = lax.rem(x + 1, X), lax.rem(x + X - 1, X)
    across = lax.rem(x + X // 2, X)
    nup = Z // 2
    ndown = Z - 1 - nup

    def w_slot(b, x_, c_, z_):
        return (Wt if b else Ws).at[:, x_, c_, z_]

    def z_hop(step, first, b):
        z_ = lax.rem(z + first * step + Z * Z, Z)
        slot = w_slot(b, x, c, z_)
        src = (wown_t if b else wown) if step == 0 else slot
        send(src, slot, names["z%s%d" % ("u" if first < 0 else "d", b)] + step, up if first < 0 else down)

    def z_take(step, first, b):
        z_ = lax.rem(z + first * (step + 1) + Z * Z, Z)
        recv(w_slot(b, x, c, z_), names["z%s%d" % ("u" if first < 0 else "d", b)] + step)
        return z_

    def z_start(b):
        if nup:
            z_hop(0, -1, b)
        if ndown:
            z_hop(0, 1, b)

    def z_step(b, step):
        z_take(step, -1, b)
        if step + 1 < nup:
            z_hop(step + 1, -1, b)
        if step >= ndown:
            return [2 * step + 1]
        z_take(step, 1, b)
        if step + 1 < ndown:
            z_hop(step + 1, 1, b)
        return [2 * step + 1, 2 * step + 2]

    def order(i):
        return lax.rem(z + (-(i + 1) // 2 if i % 2 else i // 2) + Z, Z)

    def x_hop(i, own=False):
        slot = w_slot(0, x, c, order(i))
        src = wown if own else slot
        send(src, slot, names["xr0"] + i, dev_x(right))
        if X > 2:
            send(src, slot, names["xl0"] + i, dev_x(left))
        send(src, w_slot(0, x, c, order(i)), names["sib0"] + i, sibling)

    def x_take(i):
        recv(w_slot(0, left, c, order(i)), names["xr0"] + i)
        if X > 2:
            slot = w_slot(0, left, c, order(i))
            if i % 2 == 0:
                send(slot, slot, names["xo0"] + i, dev_x(right))
            send(slot, slot, names["sib0"] + Z + i, sibling)
            slot = w_slot(0, right, c, order(i))
            recv(slot, names["xl0"] + i)
            if i % 2 == 1:
                send(slot, slot, names["xo0"] + i, dev_x(left))
            send(slot, slot, names["sib0"] + 2 * Z + i, sibling)
        else:
            slot = w_slot(0, left, c, order(i))
            send(slot, slot, names["sib0"] + Z + i, sibling)

    def x_last(i):
        slot = w_slot(0, across, c, order(i))
        recv(slot, names["xo0"] + i)
        send(slot, slot, names["sib0"] + 3 * Z + i, sibling)

    z_start(0)
    x_hop(0, True)
    xw_s[y] = jnp.zeros((T, FP), BF)
    xw_s[y, :, :F] = tok[...]
    ex_send(lambda p: xw_s.at[y], xw_s, names["tok"], Y, y, dev_y)
    cotp[...] = jnp.zeros((T, FP), BF)
    cotp[:, :F] = cot[...]

    row = iota((T, T), 0)
    col = iota((T, T), 1)

    def swap_rows(value, source):
        return mm((col == source).astype(BF), value).astype(BF)

    def to_groups(value):
        return swap_rows(value, lax.rem(row // Z, 2) * (G * Z) + row // (2 * Z) * Z + lax.rem(row, Z))

    def from_groups(value):
        return swap_rows(
            value, lax.rem(row // Z, G) * (2 * Z) + row // (G * Z) * Z + lax.rem(row, Z)
        )

    def to_z(value):
        return swap_rows(value, lax.rem(row, 2 * G) * Z + row // (2 * G))

    def from_z(value):
        return swap_rows(value, lax.rem(row, Z) * (2 * G) + row // Z)

    def x_put(buf, value):
        buf[...] = value.reshape(G, 2 * Z, FP)

    def z_put(buf, value):
        buf[...] = value.reshape(Z, 2 * G, FP)

    def flatten(buf):
        return buf[...].reshape(T, FP)

    x_put(cot_a, to_groups(cotp[...]))
    ex_send(lambda p: cot_a.at[p], cot_b, names["cot_x"], G, g, dev_g)
    cot_b[g] = cot_a[g]
    for k in range(5):
        Ws[k, x, c, z] = wown[k]
    for k in range(4):
        Wt[k, x, c, z] = wown_t[k]
    mod[...] = jnp.zeros((6, Y, 1, FP), F32)
    for i in range(6):
        for n in range(Y):
            mod[i, n, :, :F] = mods[0, i : i + 1, n * F : (n + 1) * F]

    CZ = C * Z
    j = iota((FP, CZ * MAIN), 1)
    target = (lax.rem(j // MAIN, Z) * C + j // (Z * MAIN)) * (MAIN + R2) + lax.rem(j, MAIN)
    pm[...] = (iota((FP, CZ * MAIN), 0) == target).astype(BF)
    j = iota((FP, X * CZ * R2), 1)
    target = (lax.rem(j // R2, Z) * C + lax.rem(j // (Z * R2), C)) * (MAIN + R2)
    target += MAIN + lax.rem(j, R2)
    hit = iota((FP, X * CZ * R2), 0) == target
    for x_ in range(X):
        pr[x_] = (hit & (j // (CZ * R2) == x_)).astype(BF)

    lane = iota((1, FP), 1)
    inside = lane < F
    head = [(lane >= h * HD) & (lane < (h + 1) * HD) for h in range(H)]

    def narrow(slices):
        rest = None
        for x_ in range(X):
            part = slices[x_]
            mp[:, x_ * CZ * MAIN : (x_ + 1) * CZ * MAIN] = mm(part, pm[...]).astype(BF)
            more = mm(part, pr[x_])
            rest = more if rest is None else rest + more
        mpr[...] = rest.astype(BF)

    def natural(main, rest, x_):
        return mm_nt(main[:, x_ * CZ * MAIN : (x_ + 1) * CZ * MAIN], pm[...]) + mm_nt(rest, pr[x_])

    def norm(xw, at):
        total = None
        for n in range(Y):
            part = jnp.sum(xw[n].astype(F32), axis=-1, keepdims=True)
            total = part if total is None else total + part
        mean = total * (1.0 / N)
        total = None
        for n in range(Y):
            center = jnp.where(inside, xw[n].astype(F32) - mean, 0.0)
            part = jnp.sum(center * center, axis=-1, keepdims=True)
            total = part if total is None else total + part
        inverse = lax.rsqrt(total * (1.0 / N) + EPS)
        stat[2 * at] = mean
        stat[2 * at + 1] = inverse
        slices = []
        for n in range(Y):
            normed = (xw[n].astype(F32) - mean) * inverse
            slices.append((normed * (1.0 + mod[3 * at + 1, n]) + mod[3 * at, n]).astype(BF))
        narrow(slices)

    K = X * CZ * MAIN

    def weight(b, k):
        return (Wt if b else Ws)[k].reshape(K, FP), Wr[b * 4 + k]

    def project(b):
        for k in range(3):
            main, rest = weight(b, k)
            qkv[b, k] = (mm(mp[...], main) + mm(mpr[...], rest)).astype(BF)

    def spread(value):
        zero = jnp.zeros_like(value)
        return jnp.concatenate([jnp.where(head[h], value, zero) for h in range(H)], axis=0)

    def gather_heads(value):
        total = None
        for h in range(H):
            part = jnp.where(head[h], value[h * T : (h + 1) * T], 0.0)
            total = part if total is None else total + part
        return total.astype(BF)

    SCALE = HD ** (-0.5)

    def attend(b):
        scores = mm_nt(spread(qkv[b, 0]), qkv[b, 1]) * SCALE
        if b == 0:
            query_frame = lax.rem(iota((H * T, T), 0), T) // (G * Z)
            same = query_frame == iota((H * T, T), 1) // (G * Z)
            scores = jnp.where(same, scores, -1e30)
        weights = jnp.exp(scores - jnp.max(scores, axis=-1, keepdims=True))
        prob[b] = weights / jnp.sum(weights, axis=-1, keepdims=True)
        return gather_heads(mm(prob[b].astype(BF), qkv[b, 2]))

    def attend_back(b, grad):
        grads = spread(grad)
        likely = prob[b]
        grad_values = mm_tn(likely.astype(BF), grads).astype(BF)
        grad_likely = mm_nt(grads, qkv[b, 2])
        shift = grad_likely - jnp.sum(likely * grad_likely, axis=-1, keepdims=True)
        grad_scores = (likely * shift * SCALE).astype(BF)
        grad_query = gather_heads(mm(grad_scores, qkv[b, 1]))
        grad_keys = mm_tn(grad_scores, spread(qkv[b, 0])).astype(BF)
        return grad_query, grad_keys, grad_values

    def out_partial(b, flat, buf):
        main, rest = weight(b, 3)
        part = mm_nt(flat, main).astype(BF)
        part_rest = mm_nt(flat, rest).astype(BF)
        for n in range(Y):
            buf[n] = natural(part, part_rest, n).astype(BF)

    def grad_heads(b):
        main, rest = weight(b, 3)
        return (mm(mp[...], main) + mm(mpr[...], rest)).astype(BF)

    def in_partial(b, grads, xw, buf):
        part, part_rest = None, None
        for k in range(3):
            main, rest = weight(b, k)
            a, r = mm_nt(grads[k], main), mm_nt(grads[k], rest)
            part = a if part is None else part + a
            part_rest = r if part_rest is None else part_rest + r
        part, part_rest = part.astype(BF), part_rest.astype(BF)
        mean, inverse = stat[2 * b], stat[2 * b + 1]
        first, second = None, None
        slices = []
        for n in range(Y):
            value = natural(part, part_rest, n)
            slices.append(value)
            scaled = value * (1.0 + mod[3 * b + 1, n])
            normed = (xw[n].astype(F32) - mean) * inverse
            a = jnp.sum(scaled, axis=-1, keepdims=True)
            r = jnp.sum(scaled * normed, axis=-1, keepdims=True)
            first = a if first is None else first + a
            second = r if second is None else second + r
        for n in range(Y):
            value = jnp.where(lane == F, first, jnp.where(lane == F + 1, second, slices[n]))
            buf[n] = value.astype(BF)

    def in_finish(b, buf, xw, incoming):
        total = buf[0].astype(F32)
        for n in range(1, Y):
            total = total + buf[n].astype(F32)
        first = total[:, F : F + 1] * (1.0 / N)
        second = total[:, F + 1 : F + 2] * (1.0 / N)
        scaled = total * (1.0 + mod[3 * b + 1, y])
        normed = (xw[y].astype(F32) - stat[2 * b]) * stat[2 * b + 1]
        grad = stat[2 * b + 1] * (scaled - first - normed * second)
        return jnp.where(inside, incoming.astype(F32) + grad, 0.0).astype(BF)

    def add_up(buf):
        total = buf[0].astype(F32)
        for n in range(1, Y):
            total = total + buf[n].astype(F32)
        return total

    def gated(b, value):
        return (mod[3 * b + 2, y] * value.astype(F32)).astype(BF)

    FULL = FP - 128
    WP = 128 - (F - FULL)

    def shift_lanes(n):
        a, b = iota((FP, 128), 0), iota((FP, 128), 1)
        return ((a - n * WP == b - (128 - WP)) & (b >= 128 - WP)).astype(BF)

    def wg_start(b, flat):
        main = mm_tn(mp[...], flat).astype(BF)
        rest = mm_tn(mpr[...], flat).astype(BF)
        wgp[b, :, :, :Z] = main.reshape(X, C, Z, MAIN, FP)
        wgp[b, :, :, Z] = rest.reshape(X, C, Z * R2, FP)
        send(wgp.at[b, :, 1 - c], wgc.at[b], names["wc%d" % b], sibling)

    def wg_second(b):
        recv(wgc.at[b], names["wc%d" % b])
        wgx[b] = (wgp[b, :, c].astype(F32) + wgc[b].astype(F32)).astype(BF)
        ex_send(lambda p: wgx.at[b, p], wgxr.at[b], names["wx%d" % b], X, x, dev_x)
        wgxr[b, x] = wgx[b, x]

    def wg_third(b):
        ex_wait(wgxr.at[b], names["wx%d" % b], X, x)
        total = wgxr[b, 0].astype(F32)
        for n in range(1, X):
            total = total + wgxr[b, n].astype(F32)
        total = total.astype(BF)
        main, rest = total[:Z].reshape(Z * MAIN, FP), total[Z]
        wgz[b, :, :, :FULL] = main[:, :FULL].reshape(Z, MAIN, FULL)
        tail = main[:, FULL:].astype(F32)
        for n in range(F // WP):
            pick = shift_lanes(n)
            o = iota((Z * MAIN, Z * R2), 0)
            slot = lax.rem(o, MAIN) - n * R2
            rows = (o // MAIN) * R2 + slot == iota((Z * MAIN, Z * R2), 1)
            rows = (rows & (slot >= 0) & (slot < R2)).astype(BF)
            tail = tail + mm(rows, mm(rest, pick).astype(BF))
        wgz[b, :, :, FULL:] = tail.astype(BF).reshape(Z, MAIN, 128)
        ex_send(
            lambda p: wgz.at[b, lax.rem(p, Z)], wgzr.at[b], names["wz%d" % b], ZG, zg, dev_zg
        )
        wgzr[b, zg] = wgz[b, z]

    def wg_end(b, ref):
        ex_wait(wgzr.at[b], names["wz%d" % b], ZG, zg)
        total = wgzr[b, 0].astype(F32)
        for n in range(1, ZG):
            total = total + wgzr[b, n].astype(F32)
        ref[:MAIN, :FULL] = total[:, :FULL]
        tail = total[:, FULL:]
        ref[:MAIN, FULL:] = tail[:, : F - FULL]
        for n in range(F // WP):
            ref[MAIN : MAIN + R2, n * WP : (n + 1) * WP] = tail[n * R2 : (n + 1) * R2, 128 - WP :]

    before = [0]
    for step in range(nup):
        here = z_step(0, step)
        for i in here:
            x_hop(i)
        for i in before:
            x_take(i)
        before = here
    z_start(1)

    ex_wait(cot_b, names["cot_x"], G, g)
    z_put(cot_c.at[0], to_z(flatten(cot_b)))
    ex_send(lambda p: cot_c.at[0, p], cot_c.at[1], names["cot_z"], Z, z, dev_z)
    cot_c[1, z] = cot_c[0, z]

    ex_wait(xw_s, names["tok"], Y, y)
    norm(xw_s, 0)

    for i in before:
        x_take(i)
    if X > 2:
        for i in range(Z):
            x_last(i)
    for i in range(Z):
        recv(w_slot(0, x, 1 - c, order(i)), names["sib0"] + i)
        recv(w_slot(0, left, 1 - c, order(i)), names["sib0"] + Z + i)
        if X > 2:
            recv(w_slot(0, right, 1 - c, order(i)), names["sib0"] + 2 * Z + i)
            recv(w_slot(0, across, 1 - c, order(i)), names["sib0"] + 3 * Z + i)

    def to_sibling(x_, n):
        send(Wt.at[:, x_, c], Wt.at[:, x_, c], names["sib1"] + n, sibling)

    z_steps = iter(range(nup))

    def z_later(n):
        for _ in range(n):
            step = next(z_steps, None)
            if step is not None:
                z_step(1, step)

    z_later(1)

    ex_wait(cot_c.at[1], names["cot_z"], Z, z)
    cot_t = flatten(cot_c.at[1])
    gw_t[y] = gated(1, cot_t)
    ex_send(lambda p: gw_t.at[y], gw_t, names["ggt"], Y, y, dev_y)

    n_rest = CZ * 8 * R2
    o = iota((n_rest, n_rest), 0)
    source = lax.rem(o // R2, CZ) * (8 * R2) + o // (CZ * R2) * R2 + lax.rem(o, R2)
    shuffle = (iota((n_rest, n_rest), 1) == source).astype(BF)
    for x_ in range(X):
        rest = mm(shuffle, Ws[4, x_].reshape(n_rest, FP)).astype(BF)
        Wr[:, x_ * CZ * R2 : (x_ + 1) * CZ * R2] = rest.reshape(8, CZ * R2, FP)

    project(0)
    z_later(1)
    flat_s[...] = attend(0)
    z_later(1)
    out_partial(0, flat_s[...], rs1_a)
    ex_send(lambda p: rs1_a.at[p], rs1_b, names["rs1"], Y, y, dev_y)
    rs1_b[y] = rs1_a[y]

    z_later(nup)
    for k in range(1, X):
        to_x = lax.rem(x + k, X)
        send(Wt.at[:, x, c], Wt.at[:, x, c], names["xp1"] + k, dev_x(to_x))
    to_sibling(x, 0)
    ex_wait(rs1_b, names["rs1"], Y, y)
    first = xw_s[y].astype(F32) + mod[2, y] * add_up(rs1_b)
    x_put(fst_a, to_groups(first.astype(BF)))
    ex_send(lambda p: fst_a.at[p], fst_b, names["fst_x"], G, g, dev_g)
    fst_b[g] = fst_a[g]
    ex_wait(fst_b, names["fst_x"], G, g)
    z_put(fst_c, to_z(flatten(fst_b)))
    ex_send(lambda p: fst_c.at[p], fst_d, names["fst_z"], Z, z, dev_z)
    fst_d[z] = fst_c[z]
    for k in range(1, X):
        x_ = lax.rem(x + X - k, X)
        recv(Wt.at[:, x_, c], names["xp1"] + k)
        to_sibling(x_, k)

    for k in range(X):
        recv(Wt.at[:, lax.rem(x + X - k, X), 1 - c], names["sib1"] + k)
    ex_wait(gw_t, names["ggt"], Y, y)

    ex_wait(fst_d, names["fst_z"], Z, z)
    xw_t[y] = flatten(fst_d)
    ex_send(lambda p: xw_t.at[y], xw_t, names["fst"], Y, y, dev_y)

    narrow([gw_t[n] for n in range(Y)])
    grad_t = grad_heads(1)

    ex_wait(xw_t, names["fst"], Y, y)
    norm(xw_t, 1)
    project(1)
    flat_t = attend(1)
    grads = attend_back(1, grad_t)
    in_partial(1, grads, xw_t, rsg_a)
    ex_send(lambda p: rsg_a.at[p], rsg_b, names["rsg"], Y, y, dev_y)
    rsg_b[y] = rsg_a[y]

    out_partial(1, flat_t, rsp_a)
    ex_send(lambda p: rsp_a.at[p], rsp_b, names["rsp"], Y, y, dev_y)
    rsp_b[y] = rsp_a[y]

    ex_wait(rsg_b, names["rsg"], Y, y)
    z_put(fg_a, in_finish(1, rsg_b, xw_t, cot_t))
    ex_send(lambda p: fg_a.at[p], fg_b, names["fg_z"], Z, z, dev_z)
    fg_b[z] = fg_a[z]

    narrow([gw_t[n] for n in range(Y)])
    wg_start(1, flat_t)

    ex_wait(fg_b, names["fg_z"], Z, z)
    x_put(fg_c, from_z(flatten(fg_b)))
    ex_send(lambda p: fg_c.at[p], fg_d, names["fg_x"], G, g, dev_g)
    fg_d[g] = fg_c[g]

    ex_wait(rsp_b, names["rsp"], Y, y)
    second = xw_t[y].astype(F32) + mod[5, y] * add_up(rsp_b)
    z_put(out_a, second.astype(BF))
    ex_send(lambda p: out_a.at[p], out_b, names["out_z"], Z, z, dev_z)
    out_b[z] = out_a[z]

    ex_wait(fg_d, names["fg_x"], G, g)
    fg_e[...] = from_groups(flatten(fg_d))
    gw_s[y] = gated(0, fg_e[...])
    ex_send(lambda p: gw_s.at[y], gw_s, names["ggs"], Y, y, dev_y)

    wg_second(1)
    ex_wait(out_b, names["out_z"], Z, z)
    x_put(out_c, from_z(flatten(out_b)))
    ex_send(lambda p: out_c.at[p], out_d, names["out_x"], G, g, dev_g)
    out_d[g] = out_c[g]

    ex_wait(gw_s, names["ggs"], Y, y)
    narrow([gw_s[n] for n in range(Y)])
    wg_start(0, flat_s[...])
    grad_s = grad_heads(0)
    wg_third(1)
    wg_second(0)
    grads = attend_back(0, grad_s)
    wg_third(0)
    in_partial(0, grads, xw_s, rsf_a)
    ex_send(lambda p: rsf_a.at[p], rsf_b, names["rsf"], Y, y, dev_y)
    rsf_b[y] = rsf_a[y]

    ex_wait(out_d, names["out_x"], G, g)
    out[...] = from_groups(flatten(out_d))[:, :F]
    wg_end(1, wg_t)
    ex_wait(rsf_b, names["rsf"], Y, y)
    igrad[...] = in_finish(0, rsf_b, xw_s, fg_e[...])[:, :F]
    wg_end(0, wg_s)
    for copy in sent:
        copy.wait_send()


def hand_on(*refs):
    for source, target in zip(refs[:4], refs[4:]):
        target[...] = source[...]


def on_device(sizes, tokens, modulation, qkv_s, out_s, qkv_t, out_t, cotangent):
    DP, S, Y = sizes
    frames, patches, F = tokens.shape[1:]
    T = frames * patches
    X, C = Y, 2
    Z = S // (X * C)
    G = X * C
    H = F // HD
    rows = out_s.shape[0]
    R2 = rows - MAIN
    FP = (F + 2 + 127) // 128 * 128
    dims = (X, C, Z, Y, DP, T, F, FP, H, R2)
    names, count = layout(X, C, Z, Y, DP)

    K, KR = X * C * Z * MAIN, X * C * Z * R2
    xs, zs = pltpu.VMEM((G, 2 * Z, FP), BF), pltpu.VMEM((Z, 2 * G, FP), BF)
    wide = pltpu.VMEM((Y, T, FP), BF)
    scratch = [
        pltpu.SemaphoreType.DMA((count,)),
        pltpu.SemaphoreType.DMA((count,)),
        pltpu.VMEM((5, MAIN, FP), BF),
        pltpu.VMEM((4, MAIN, FP), BF),
        pltpu.VMEM((6, Y, 1, FP), F32),
        pltpu.VMEM((FP, C * Z * MAIN), BF),
        pltpu.VMEM((X, FP, KR), BF),
        wide, wide, wide, wide,
        pltpu.VMEM((5, X, C, Z, MAIN, FP), BF),
        pltpu.VMEM((4, X, C, Z, MAIN, FP), BF),
        pltpu.VMEM((8, KR, FP), BF),
        pltpu.VMEM((T, FP), BF),
        xs, xs, pltpu.VMEM((2, Z, 2 * G, FP), BF),
        xs, xs, zs, zs,
        zs, zs, xs, xs, pltpu.VMEM((T, FP), BF),
        zs, zs, xs, xs,
        pltpu.VMEM((T, K), BF),
        pltpu.VMEM((T, KR), BF),
        pltpu.VMEM((2, 3, T, FP), BF),
        pltpu.VMEM((2, H * T, T), F32),
        pltpu.VMEM((T, FP), BF),
        pltpu.VMEM((4, T, 1), F32),
        wide, wide, wide, wide, wide, wide, wide, wide,
        pltpu.VMEM((2, X, C, Z + 1, MAIN, FP), BF),
        pltpu.VMEM((2, X, Z + 1, MAIN, FP), BF),
        pltpu.VMEM((2, X, Z + 1, MAIN, FP), BF),
        pltpu.VMEM((2, X, Z + 1, MAIN, FP), BF),
        pltpu.VMEM((2, Z, MAIN, FP), BF),
        pltpu.VMEM((2, DP * Z, MAIN, FP), BF),
    ]
    vmem = pl.BlockSpec(memory_space=pltpu.VMEM)
    out, igrad, wg_s, wg_t = pl.pallas_call(
        functools.partial(kernel, dims, names),
        out_shape=(
            jax.ShapeDtypeStruct((T, F), BF),
            jax.ShapeDtypeStruct((T, F), BF),
            jax.ShapeDtypeStruct((rows, F), F32),
            jax.ShapeDtypeStruct((rows, F), F32),
        ),
        in_specs=[vmem] * 7,
        out_specs=(vmem,) * 4,
        scratch_shapes=scratch,
        compiler_params=pltpu.CompilerParams(
            collective_id=0, has_side_effects=True, vmem_limit_bytes=56 * 2**20
        ),
    )(tokens.reshape(T, F), cotangent.reshape(T, F), modulation, qkv_s, out_s, qkv_t, out_t)
    out, igrad, wg_s, wg_t = pl.pallas_call(
        hand_on,
        out_shape=tuple(jax.ShapeDtypeStruct(v.shape, v.dtype) for v in (out, igrad, wg_s, wg_t)),
        in_specs=[vmem] * 4,
        out_specs=(vmem,) * 4,
    )(out, igrad, wg_s, wg_t)
    shape = (1, frames, patches, F)
    return out.reshape(shape), igrad.reshape(shape), wg_s, wg_t


def solution(mesh):
    sizes = tuple(mesh.shape[a] for a in ("dp", "seq", "tp"))
    placed = (
        P("dp", "seq", None, "tp"),
        P("dp", None, None),
        P("seq", None, "tp"),
        P("seq", "tp"),
        P("seq", None, "tp"),
        P("seq", "tp"),
        P("dp", "seq", None, "tp"),
    )
    return jax.shard_map(
        functools.partial(on_device, sizes),
        mesh=mesh,
        in_specs=placed,
        out_specs=(
            P("dp", "seq", None, "tp"),
            P("dp", "seq", None, "tp"),
            P("seq", "tp"),
            P("seq", "tp"),
        ),
        check_vma=False,
    )
```

```python
import functools

import jax
import jax.numpy as jnp
from jax import lax
from jax.experimental import pallas as pl
from jax.experimental.pallas import tpu as pltpu
from jax.sharding import PartitionSpec as P

HD = 72
EPS = 1e-06
MAIN = 16
MESH = pl.DeviceIdType.MESH
BF = jnp.bfloat16
F32 = jnp.float32


def mm(a, b):
    return lax.dot_general(a, b, (((1,), (0,)), ((), ())), preferred_element_type=F32)


def mm_nt(a, b):
    return lax.dot_general(a, b, (((1,), (1,)), ((), ())), preferred_element_type=F32)


def mm_tn(a, b):
    return lax.dot_general(a, b, (((0,), (0,)), ((), ())), preferred_element_type=F32)


def iota(shape, axis):
    return lax.broadcasted_iota(jnp.int32, shape, axis)


class Sems:
    def __init__(self):
        self.count = 0

    def take(self, n):
        first = self.count
        self.count += n
        return first


def layout(X, C, Z, Y, DP):
    s = Sems()
    names = {}
    G = X * C
    for name in ("tok", "ggt", "rs1", "fst", "rsg", "rsp", "ggs", "rsf", "hw"):
        names[name] = s.take(Y)
    for name in ("cot_x", "fst_x", "fg_x", "out_x"):
        names[name] = s.take(G)
    for name in ("cot_z", "fst_z", "fg_z", "out_z"):
        names[name] = s.take(Z)
    for name in ("zu0", "zd0", "zu1", "zd1", "xr0", "xl0", "xo0"):
        names[name] = s.take(Z)
    names["sib0"] = s.take(X * Z)
    names["xp1"] = s.take(X)
    names["sib1"] = s.take(X)
    for b in (0, 1):
        names["wc%d" % b] = s.take(1)
        names["wx%d" % b] = s.take(X)
        names["wz%d" % b] = s.take(DP * Z)
    return names, s.count


def kernel(dims, names, tok, cot, mods, qkv_s, out_s, qkv_t, out_t, out, igrad, wg_s, wg_t, *refs):
    X, C, Z, Y, DP, T, F, FP, H, R2 = dims
    G = X * C
    N = Y * F
    (
        ssem, rsem, wown, wown_t, mod, pm, pr, xw_s, xw_t, gw_t, gw_s, Ws, Wt, Wr, cotp,
        cot_a, cot_b, cot_c, fst_a, fst_b, fst_c, fst_d, fg_a, fg_b, fg_c, fg_d, fg_e,
        out_a, out_b, out_c, out_d,
        mp, mpr, qkv, prob, flat_s, hw, stat,
        rs1_a, rs1_b, rsg_a, rsg_b, rsp_a, rsp_b, rsf_a, rsf_b,
        wgp, wgc, wgx, wgxr, wgz, wgzr,
    ) = refs

    d = lax.axis_index("dp")
    s = lax.axis_index("seq")
    y = lax.axis_index("tp")
    x = s // (Z * C)
    z = lax.rem(s // C, Z)
    c = lax.rem(s, C)
    g = x * C + c
    zg = d * Z + z

    def seq_of(x_, z_, c_):
        return (x_ * Z + z_) * C + c_

    def dev(d_, x_, z_, c_, y_):
        return {"dp": d_, "seq": seq_of(x_, z_, c_), "tp": y_}

    def dev_y(y_):
        return dev(d, x, z, c, y_)

    def dev_g(g_):
        return dev(d, g_ // C, z, lax.rem(g_, C), y)

    def dev_z(z_):
        return dev(d, x, z_, c, y)

    def dev_zg(zg_):
        return dev(zg_ // Z, x, lax.rem(zg_, Z), c, y)

    def dev_x(x_):
        return dev(d, x_, z, c, y)

    sibling = dev(d, x, z, 1 - c, y)
    ZG = DP * Z
    sent = []

    def send(src, dst, sem, device):
        copy = pltpu.make_async_remote_copy(
            src_ref=src, dst_ref=dst, send_sem=ssem.at[sem], recv_sem=rsem.at[sem],
            device_id=device, device_id_type=MESH,
        )
        copy.start()
        sent.append(copy)

    def recv(dst, sem):
        pltpu.make_async_remote_copy(
            src_ref=dst, dst_ref=dst, send_sem=ssem.at[sem], recv_sem=rsem.at[sem],
            device_id=sibling, device_id_type=MESH,
        ).wait_recv()

    def ex_send(src, dst, sem, n, me, device):
        for k in range(1, n):
            peer = lax.rem(me + k, n)
            send(src(peer), dst.at[me], sem + k, device(peer))

    def ex_wait(dst, sem, n, me):
        for k in range(1, n):
            recv(dst.at[lax.rem(me + n - k, n)], sem + k)

    barrier = pltpu.get_barrier_semaphore()
    peers = [dev_y(lax.rem(y + k, Y)) for k in range(1, Y)]
    peers += [dev_g(lax.rem(g + k, G)) for k in range(1, G)]
    peers += [dev_zg(lax.rem(zg + k, ZG)) for k in range(1, ZG)]
    for peer in peers:
        pl.semaphore_signal(barrier, inc=1, device_id=peer, device_id_type=MESH)
    aligned = x == y
    corner = [(dev(d, y, z, c, n), aligned & (y == n)) for n in range(Y)]
    corner += [(dev(d, n, z, c, x), aligned & (x == n)) for n in range(X)]
    for peer, own in corner:

        @pl.when(jnp.logical_not(own))
        def _(peer=peer):
            pl.semaphore_signal(barrier, inc=1, device_id=peer, device_id_type=MESH)

    rows = MAIN + R2

    def widened(value):
        return jnp.concatenate([value, jnp.zeros((value.shape[0], FP - F), F32)], axis=1)

    rest = []
    for ref, qkv_ref, out_ref in ((wown, qkv_s, out_s), (wown_t, qkv_t, out_t)):
        value = qkv_ref[...].astype(F32)
        for k in range(4):
            part = value[:, k, :] if k < 3 else out_ref[...].astype(F32)
            part = widened(part.reshape(rows, F))
            ref[k] = part[:MAIN].astype(BF)
            rest.append(part[MAIN:])
    wown[4] = jnp.concatenate(rest, axis=0).astype(BF)

    pl.semaphore_wait(barrier, len(peers) + jnp.where(aligned, len(corner) - 2, len(corner)))

    up, down = dev_zg(lax.rem(zg + 1, ZG)), dev_zg(lax.rem(zg + ZG - 1, ZG))
    right, left = lax.rem(x + 1, X), lax.rem(x + X - 1, X)
    across = lax.rem(x + X // 2, X)
    nup = Z // 2
    ndown = Z - 1 - nup

    def w_slot(b, x_, c_, z_):
        return (Wt if b else Ws).at[:, x_, c_, z_]

    def z_hop(step, first, b):
        z_ = lax.rem(z + first * step + Z * Z, Z)
        slot = w_slot(b, x, c, z_)
        src = (wown_t if b else wown) if step == 0 else slot
        send(src, slot, names["z%s%d" % ("u" if first < 0 else "d", b)] + step, up if first < 0 else down)

    def z_take(step, first, b):
        z_ = lax.rem(z + first * (step + 1) + Z * Z, Z)
        recv(w_slot(b, x, c, z_), names["z%s%d" % ("u" if first < 0 else "d", b)] + step)
        return z_

    def z_start(b):
        if nup:
            z_hop(0, -1, b)
        if ndown:
            z_hop(0, 1, b)

    def z_step(b, step):
        z_take(step, -1, b)
        if step + 1 < nup:
            z_hop(step + 1, -1, b)
        if step >= ndown:
            return [2 * step + 1]
        z_take(step, 1, b)
        if step + 1 < ndown:
            z_hop(step + 1, 1, b)
        return [2 * step + 1, 2 * step + 2]

    def order(i):
        return lax.rem(z + (-(i + 1) // 2 if i % 2 else i // 2) + Z, Z)

    def x_hop(i, own=False):
        slot = w_slot(0, x, c, order(i))
        src = wown if own else slot
        send(src, slot, names["xr0"] + i, dev_x(right))
        if X > 2:
            send(src, slot, names["xl0"] + i, dev_x(left))
        send(src, w_slot(0, x, c, order(i)), names["sib0"] + i, sibling)

    def x_take(i):
        recv(w_slot(0, left, c, order(i)), names["xr0"] + i)
        if X > 2:
            slot = w_slot(0, left, c, order(i))
            if i % 2 == 0:
                send(slot, slot, names["xo0"] + i, dev_x(right))
            send(slot, slot, names["sib0"] + Z + i, sibling)
            slot = w_slot(0, right, c, order(i))
            recv(slot, names["xl0"] + i)
            if i % 2 == 1:
                send(slot, slot, names["xo0"] + i, dev_x(left))
            send(slot, slot, names["sib0"] + 2 * Z + i, sibling)
        else:
            slot = w_slot(0, left, c, order(i))
            send(slot, slot, names["sib0"] + Z + i, sibling)

    def x_last(i):
        slot = w_slot(0, across, c, order(i))
        recv(slot, names["xo0"] + i)
        send(slot, slot, names["sib0"] + 3 * Z + i, sibling)

    z_start(0)
    x_hop(0, True)
    xw_s[y] = jnp.zeros((T, FP), BF)
    xw_s[y, :, :F] = tok[...]
    ex_send(lambda p: xw_s.at[y], xw_s, names["tok"], Y, y, dev_y)
    cotp[...] = jnp.zeros((T, FP), BF)
    cotp[:, :F] = cot[...]

    row = iota((T, T), 0)
    col = iota((T, T), 1)

    def swap_rows(value, source):
        return mm((col == source).astype(BF), value).astype(BF)

    def to_groups(value):
        return swap_rows(value, lax.rem(row // Z, 2) * (G * Z) + row // (2 * Z) * Z + lax.rem(row, Z))

    def from_groups(value):
        return swap_rows(
            value, lax.rem(row // Z, G) * (2 * Z) + row // (G * Z) * Z + lax.rem(row, Z)
        )

    def to_z(value):
        return swap_rows(value, lax.rem(row, 2 * G) * Z + row // (2 * G))

    def from_z(value):
        return swap_rows(value, lax.rem(row, Z) * (2 * G) + row // Z)

    def x_put(buf, value):
        buf[...] = value.reshape(G, 2 * Z, FP)

    def z_put(buf, value):
        buf[...] = value.reshape(Z, 2 * G, FP)

    def flatten(buf):
        return buf[...].reshape(T, FP)

    x_put(cot_a, to_groups(cotp[...]))
    ex_send(lambda p: cot_a.at[p], cot_b, names["cot_x"], G, g, dev_g)
    cot_b[g] = cot_a[g]
    for k in range(5):
        Ws[k, x, c, z] = wown[k]
    for k in range(4):
        Wt[k, x, c, z] = wown_t[k]
    mod[...] = jnp.zeros((6, Y, 1, FP), F32)
    for i in range(6):
        for n in range(Y):
            mod[i, n, :, :F] = mods[0, i : i + 1, n * F : (n + 1) * F]

    CZ = C * Z
    j = iota((FP, CZ * MAIN), 1)
    target = (lax.rem(j // MAIN, Z) * C + j // (Z * MAIN)) * (MAIN + R2) + lax.rem(j, MAIN)
    pm[...] = (iota((FP, CZ * MAIN), 0) == target).astype(BF)
    j = iota((FP, X * CZ * R2), 1)
    target = (lax.rem(j // R2, Z) * C + lax.rem(j // (Z * R2), C)) * (MAIN + R2)
    target += MAIN + lax.rem(j, R2)
    hit = iota((FP, X * CZ * R2), 0) == target
    for x_ in range(X):
        pr[x_] = (hit & (j // (CZ * R2) == x_)).astype(BF)

    lane = iota((1, FP), 1)
    inside = lane < F
    head = [(lane >= h * HD) & (lane < (h + 1) * HD) for h in range(H)]

    def narrow(slices):
        rest = None
        for x_ in range(X):
            part = slices[x_]
            mp[:, x_ * CZ * MAIN : (x_ + 1) * CZ * MAIN] = mm(part, pm[...]).astype(BF)
            more = mm(part, pr[x_])
            rest = more if rest is None else rest + more
        mpr[...] = rest.astype(BF)

    def natural(main, rest, x_):
        return mm_nt(main[:, x_ * CZ * MAIN : (x_ + 1) * CZ * MAIN], pm[...]) + mm_nt(rest, pr[x_])

    def norm(xw, at):
        total = None
        for n in range(Y):
            part = jnp.sum(xw[n].astype(F32), axis=-1, keepdims=True)
            total = part if total is None else total + part
        mean = total * (1.0 / N)
        total = None
        for n in range(Y):
            center = jnp.where(inside, xw[n].astype(F32) - mean, 0.0)
            part = jnp.sum(center * center, axis=-1, keepdims=True)
            total = part if total is None else total + part
        inverse = lax.rsqrt(total * (1.0 / N) + EPS)
        stat[2 * at] = mean
        stat[2 * at + 1] = inverse
        slices = []
        for n in range(Y):
            normed = (xw[n].astype(F32) - mean) * inverse
            slices.append((normed * (1.0 + mod[3 * at + 1, n]) + mod[3 * at, n]).astype(BF))
        narrow(slices)

    K = X * CZ * MAIN

    def weight(b, k):
        return (Wt if b else Ws)[k].reshape(K, FP), Wr[b * 4 + k]

    def project(b):
        for k in range(3):
            main, rest = weight(b, k)
            qkv[b, k] = (mm(mp[...], main) + mm(mpr[...], rest)).astype(BF)

    def spread(value):
        zero = jnp.zeros_like(value)
        return jnp.concatenate([jnp.where(head[h], value, zero) for h in range(H)], axis=0)

    def gather_heads(value):
        total = None
        for h in range(H):
            part = jnp.where(head[h], value[h * T : (h + 1) * T], 0.0)
            total = part if total is None else total + part
        return total.astype(BF)

    SCALE = HD ** (-0.5)

    def attend(b):
        scores = mm_nt(spread(qkv[b, 0]), qkv[b, 1]) * SCALE
        if b == 0:
            query_frame = lax.rem(iota((H * T, T), 0), T) // (G * Z)
            same = query_frame == iota((H * T, T), 1) // (G * Z)
            scores = jnp.where(same, scores, -1e30)
        weights = jnp.exp(scores - jnp.max(scores, axis=-1, keepdims=True))
        prob[b] = weights / jnp.sum(weights, axis=-1, keepdims=True)
        return gather_heads(mm(prob[b].astype(BF), qkv[b, 2]))

    def attend_back(b, grad):
        grads = spread(grad)
        likely = prob[b]
        grad_values = mm_tn(likely.astype(BF), grads).astype(BF)
        grad_likely = mm_nt(grads, qkv[b, 2])
        shift = grad_likely - jnp.sum(likely * grad_likely, axis=-1, keepdims=True)
        grad_scores = (likely * shift * SCALE).astype(BF)
        grad_query = gather_heads(mm(grad_scores, qkv[b, 1]))
        grad_keys = mm_tn(grad_scores, spread(qkv[b, 0])).astype(BF)
        return grad_query, grad_keys, grad_values

    def out_partial(b, flat, buf):
        main, rest = weight(b, 3)
        part = mm_nt(flat, main).astype(BF)
        part_rest = mm_nt(flat, rest).astype(BF)
        for n in range(Y):
            buf[n] = natural(part, part_rest, n).astype(BF)

    def grad_heads(b):
        main, rest = weight(b, 3)
        return (mm(mp[...], main) + mm(mpr[...], rest)).astype(BF)

    def in_partial(b, grads, xw, buf):
        part, part_rest = None, None
        for k in range(3):
            main, rest = weight(b, k)
            a, r = mm_nt(grads[k], main), mm_nt(grads[k], rest)
            part = a if part is None else part + a
            part_rest = r if part_rest is None else part_rest + r
        part, part_rest = part.astype(BF), part_rest.astype(BF)
        mean, inverse = stat[2 * b], stat[2 * b + 1]
        first, second = None, None
        slices = []
        for n in range(Y):
            value = natural(part, part_rest, n)
            slices.append(value)
            scaled = value * (1.0 + mod[3 * b + 1, n])
            normed = (xw[n].astype(F32) - mean) * inverse
            a = jnp.sum(scaled, axis=-1, keepdims=True)
            r = jnp.sum(scaled * normed, axis=-1, keepdims=True)
            first = a if first is None else first + a
            second = r if second is None else second + r
        for n in range(Y):
            value = jnp.where(lane == F, first, jnp.where(lane == F + 1, second, slices[n]))
            buf[n] = value.astype(BF)

    def in_finish(b, buf, xw, incoming):
        total = buf[0].astype(F32)
        for n in range(1, Y):
            total = total + buf[n].astype(F32)
        first = total[:, F : F + 1] * (1.0 / N)
        second = total[:, F + 1 : F + 2] * (1.0 / N)
        scaled = total * (1.0 + mod[3 * b + 1, y])
        normed = (xw[y].astype(F32) - stat[2 * b]) * stat[2 * b + 1]
        grad = stat[2 * b + 1] * (scaled - first - normed * second)
        return jnp.where(inside, incoming.astype(F32) + grad, 0.0).astype(BF)

    def add_up(buf):
        total = buf[0].astype(F32)
        for n in range(1, Y):
            total = total + buf[n].astype(F32)
        return total

    def gated(b, value):
        return (mod[3 * b + 2, y] * value.astype(F32)).astype(BF)

    FULL = FP - 128
    WP = 128 - (F - FULL)

    def shift_lanes(n):
        a, b = iota((FP, 128), 0), iota((FP, 128), 1)
        return ((a - n * WP == b - (128 - WP)) & (b >= 128 - WP)).astype(BF)

    def wg_start(b, flat):
        main = mm_tn(mp[...], flat).astype(BF)
        rest = mm_tn(mpr[...], flat).astype(BF)
        wgp[b, :, :, :Z] = main.reshape(X, C, Z, MAIN, FP)
        wgp[b, :, :, Z] = rest.reshape(X, C, Z * R2, FP)
        send(wgp.at[b, :, 1 - c], wgc.at[b], names["wc%d" % b], sibling)

    def wg_second(b):
        recv(wgc.at[b], names["wc%d" % b])
        wgx[b] = (wgp[b, :, c].astype(F32) + wgc[b].astype(F32)).astype(BF)
        ex_send(lambda p: wgx.at[b, p], wgxr.at[b], names["wx%d" % b], X, x, dev_x)
        wgxr[b, x] = wgx[b, x]

    def wg_start_own(grad):
        main = mm(grad, pm[...]).astype(BF)
        rest = mm(grad, pr[0]).astype(BF)
        for n in range(Y):
            wgp[0, n, :, :Z] = mm_tn(main, hw[n]).astype(BF).reshape(C, Z, MAIN, FP)
            part = mm_tn(rest, hw[n])[: CZ * R2].astype(BF)
            wgp[0, n, :, Z] = part.reshape(C, Z * R2, FP)
        send(wgp.at[0, :, 1 - c], wgc.at[0], names["wc0"], sibling)

    corner_sent = []

    def wg_second_own():
        recv(wgc.at[0], names["wc0"])
        wgx[0] = (wgp[0, :, c].astype(F32) + wgc[0].astype(F32)).astype(BF)
        for n in range(Y):
            peer, own = corner[n]
            copy = pltpu.make_async_remote_copy(
                src_ref=wgx.at[0, n], dst_ref=wgxr.at[0, x],
                send_sem=ssem.at[names["wx0"] + n], recv_sem=rsem.at[names["wx0"] + x],
                device_id=peer, device_id_type=MESH,
            )
            corner_sent.append((copy, own))

            @pl.when(jnp.logical_not(own))
            def _(copy=copy):
                copy.start()

            @pl.when(own)
            def _(n=n):
                wgxr[0, x] = wgx[0, n]

    def wg_wait_own():
        for n in range(X):

            @pl.when(jnp.logical_not(corner[Y + n][1]))
            def _(n=n):
                recv(wgxr.at[0, n], names["wx0"] + n)

    def wg_third(b):
        if b == 0:
            wg_wait_own()
        else:
            ex_wait(wgxr.at[b], names["wx%d" % b], X, x)
        total = wgxr[b, 0].astype(F32)
        for n in range(1, X):
            total = total + wgxr[b, n].astype(F32)
        total = total.astype(BF)
        main, rest = total[:Z].reshape(Z * MAIN, FP), total[Z]
        wgz[b, :, :, :FULL] = main[:, :FULL].reshape(Z, MAIN, FULL)
        tail = main[:, FULL:].astype(F32)
        for n in range(F // WP):
            pick = shift_lanes(n)
            o = iota((Z * MAIN, Z * R2), 0)
            slot = lax.rem(o, MAIN) - n * R2
            rows = (o // MAIN) * R2 + slot == iota((Z * MAIN, Z * R2), 1)
            rows = (rows & (slot >= 0) & (slot < R2)).astype(BF)
            tail = tail + mm(rows, mm(rest, pick).astype(BF))
        wgz[b, :, :, FULL:] = tail.astype(BF).reshape(Z, MAIN, 128)
        ex_send(
            lambda p: wgz.at[b, lax.rem(p, Z)], wgzr.at[b], names["wz%d" % b], ZG, zg, dev_zg
        )
        wgzr[b, zg] = wgz[b, z]

    def wg_end(b, ref):
        ex_wait(wgzr.at[b], names["wz%d" % b], ZG, zg)
        total = wgzr[b, 0].astype(F32)
        for n in range(1, ZG):
            total = total + wgzr[b, n].astype(F32)
        ref[:MAIN, :FULL] = total[:, :FULL]
        tail = total[:, FULL:]
        ref[:MAIN, FULL:] = tail[:, : F - FULL]
        for n in range(F // WP):
            ref[MAIN : MAIN + R2, n * WP : (n + 1) * WP] = tail[n * R2 : (n + 1) * R2, 128 - WP :]

    before = [0]
    for step in range(nup):
        here = z_step(0, step)
        for i in here:
            x_hop(i)
        for i in before:
            x_take(i)
        before = here
    z_start(1)

    ex_wait(cot_b, names["cot_x"], G, g)
    z_put(cot_c.at[0], to_z(flatten(cot_b)))
    ex_send(lambda p: cot_c.at[0, p], cot_c.at[1], names["cot_z"], Z, z, dev_z)
    cot_c[1, z] = cot_c[0, z]

    ex_wait(xw_s, names["tok"], Y, y)
    norm(xw_s, 0)

    for i in before:
        x_take(i)
    if X > 2:
        for i in range(Z):
            x_last(i)
    for i in range(Z):
        recv(w_slot(0, x, 1 - c, order(i)), names["sib0"] + i)
        recv(w_slot(0, left, 1 - c, order(i)), names["sib0"] + Z + i)
        if X > 2:
            recv(w_slot(0, right, 1 - c, order(i)), names["sib0"] + 2 * Z + i)
            recv(w_slot(0, across, 1 - c, order(i)), names["sib0"] + 3 * Z + i)

    def to_sibling(x_, n):
        send(Wt.at[:, x_, c], Wt.at[:, x_, c], names["sib1"] + n, sibling)

    z_steps = iter(range(nup))

    def z_later(n):
        for _ in range(n):
            step = next(z_steps, None)
            if step is not None:
                z_step(1, step)

    z_later(1)

    ex_wait(cot_c.at[1], names["cot_z"], Z, z)
    cot_t = flatten(cot_c.at[1])
    gw_t[y] = gated(1, cot_t)
    ex_send(lambda p: gw_t.at[y], gw_t, names["ggt"], Y, y, dev_y)

    n_rest = CZ * 8 * R2
    o = iota((n_rest, n_rest), 0)
    source = lax.rem(o // R2, CZ) * (8 * R2) + o // (CZ * R2) * R2 + lax.rem(o, R2)
    shuffle = (iota((n_rest, n_rest), 1) == source).astype(BF)
    for x_ in range(X):
        rest = mm(shuffle, Ws[4, x_].reshape(n_rest, FP)).astype(BF)
        Wr[:, x_ * CZ * R2 : (x_ + 1) * CZ * R2] = rest.reshape(8, CZ * R2, FP)

    project(0)
    z_later(1)
    flat_s[...] = attend(0)
    z_later(1)
    out_partial(0, flat_s[...], rs1_a)
    ex_send(lambda p: rs1_a.at[p], rs1_b, names["rs1"], Y, y, dev_y)
    rs1_b[y] = rs1_a[y]

    z_later(nup)
    for k in range(1, X):
        to_x = lax.rem(x + k, X)
        send(Wt.at[:, x, c], Wt.at[:, x, c], names["xp1"] + k, dev_x(to_x))
    to_sibling(x, 0)
    ex_wait(rs1_b, names["rs1"], Y, y)
    first = xw_s[y].astype(F32) + mod[2, y] * add_up(rs1_b)
    x_put(fst_a, to_groups(first.astype(BF)))
    ex_send(lambda p: fst_a.at[p], fst_b, names["fst_x"], G, g, dev_g)
    fst_b[g] = fst_a[g]
    ex_wait(fst_b, names["fst_x"], G, g)
    z_put(fst_c, to_z(flatten(fst_b)))
    ex_send(lambda p: fst_c.at[p], fst_d, names["fst_z"], Z, z, dev_z)
    fst_d[z] = fst_c[z]
    for k in range(1, X):
        x_ = lax.rem(x + X - k, X)
        recv(Wt.at[:, x_, c], names["xp1"] + k)
        to_sibling(x_, k)

    for k in range(X):
        recv(Wt.at[:, lax.rem(x + X - k, X), 1 - c], names["sib1"] + k)
    ex_wait(gw_t, names["ggt"], Y, y)

    ex_wait(fst_d, names["fst_z"], Z, z)
    xw_t[y] = flatten(fst_d)
    ex_send(lambda p: xw_t.at[y], xw_t, names["fst"], Y, y, dev_y)

    narrow([gw_t[n] for n in range(Y)])
    grad_t = grad_heads(1)

    ex_wait(xw_t, names["fst"], Y, y)
    hw[y] = flat_s[...]
    ex_send(lambda p: hw.at[y], hw, names["hw"], Y, y, dev_y)
    norm(xw_t, 1)
    project(1)
    flat_t = attend(1)
    grads = attend_back(1, grad_t)
    in_partial(1, grads, xw_t, rsg_a)
    ex_send(lambda p: rsg_a.at[p], rsg_b, names["rsg"], Y, y, dev_y)
    rsg_b[y] = rsg_a[y]

    out_partial(1, flat_t, rsp_a)
    ex_send(lambda p: rsp_a.at[p], rsp_b, names["rsp"], Y, y, dev_y)
    rsp_b[y] = rsp_a[y]

    ex_wait(rsg_b, names["rsg"], Y, y)
    z_put(fg_a, in_finish(1, rsg_b, xw_t, cot_t))
    ex_send(lambda p: fg_a.at[p], fg_b, names["fg_z"], Z, z, dev_z)
    fg_b[z] = fg_a[z]

    narrow([gw_t[n] for n in range(Y)])
    wg_start(1, flat_t)

    ex_wait(fg_b, names["fg_z"], Z, z)
    x_put(fg_c, from_z(flatten(fg_b)))
    ex_send(lambda p: fg_c.at[p], fg_d, names["fg_x"], G, g, dev_g)
    fg_d[g] = fg_c[g]
    wg_second(1)

    ex_wait(rsp_b, names["rsp"], Y, y)
    second = xw_t[y].astype(F32) + mod[5, y] * add_up(rsp_b)
    z_put(out_a, second.astype(BF))
    ex_send(lambda p: out_a.at[p], out_b, names["out_z"], Z, z, dev_z)
    out_b[z] = out_a[z]

    ex_wait(fg_d, names["fg_x"], G, g)
    fg_e[...] = from_groups(flatten(fg_d))
    gw_s[y] = gated(0, fg_e[...])
    ex_send(lambda p: gw_s.at[y], gw_s, names["ggs"], Y, y, dev_y)

    ex_wait(hw, names["hw"], Y, y)
    wg_start_own(gw_s[y])
    ex_wait(out_b, names["out_z"], Z, z)
    x_put(out_c, from_z(flatten(out_b)))
    ex_send(lambda p: out_c.at[p], out_d, names["out_x"], G, g, dev_g)
    out_d[g] = out_c[g]
    wg_second_own()

    ex_wait(gw_s, names["ggs"], Y, y)
    narrow([gw_s[n] for n in range(Y)])
    wg_third(1)
    grad_s = grad_heads(0)
    grads = attend_back(0, grad_s)
    wg_third(0)
    in_partial(0, grads, xw_s, rsf_a)
    ex_send(lambda p: rsf_a.at[p], rsf_b, names["rsf"], Y, y, dev_y)
    rsf_b[y] = rsf_a[y]

    ex_wait(out_d, names["out_x"], G, g)
    out[...] = from_groups(flatten(out_d))[:, :F]
    wg_end(1, wg_t)
    ex_wait(rsf_b, names["rsf"], Y, y)
    igrad[...] = in_finish(0, rsf_b, xw_s, fg_e[...])[:, :F]
    wg_end(0, wg_s)
    for copy in sent:
        copy.wait_send()
    for copy, own in corner_sent:

        @pl.when(jnp.logical_not(own))
        def _(copy=copy):
            copy.wait_send()


def hand_on(*refs):
    for source, target in zip(refs[:4], refs[4:]):
        target[...] = source[...]


def on_device(sizes, tokens, modulation, qkv_s, out_s, qkv_t, out_t, cotangent):
    DP, S, Y = sizes
    frames, patches, F = tokens.shape[1:]
    T = frames * patches
    X, C = Y, 2
    Z = S // (X * C)
    G = X * C
    H = F // HD
    rows = out_s.shape[0]
    R2 = rows - MAIN
    FP = (F + 2 + 127) // 128 * 128
    dims = (X, C, Z, Y, DP, T, F, FP, H, R2)
    names, count = layout(X, C, Z, Y, DP)

    K, KR = X * C * Z * MAIN, X * C * Z * R2
    xs, zs = pltpu.VMEM((G, 2 * Z, FP), BF), pltpu.VMEM((Z, 2 * G, FP), BF)
    wide = pltpu.VMEM((Y, T, FP), BF)
    scratch = [
        pltpu.SemaphoreType.DMA((count,)),
        pltpu.SemaphoreType.DMA((count,)),
        pltpu.VMEM((5, MAIN, FP), BF),
        pltpu.VMEM((4, MAIN, FP), BF),
        pltpu.VMEM((6, Y, 1, FP), F32),
        pltpu.VMEM((FP, C * Z * MAIN), BF),
        pltpu.VMEM((X, FP, KR), BF),
        wide, wide, wide, wide,
        pltpu.VMEM((5, X, C, Z, MAIN, FP), BF),
        pltpu.VMEM((4, X, C, Z, MAIN, FP), BF),
        pltpu.VMEM((8, KR, FP), BF),
        pltpu.VMEM((T, FP), BF),
        xs, xs, pltpu.VMEM((2, Z, 2 * G, FP), BF),
        xs, xs, zs, zs,
        zs, zs, xs, xs, pltpu.VMEM((T, FP), BF),
        zs, zs, xs, xs,
        pltpu.VMEM((T, K), BF),
        pltpu.VMEM((T, KR), BF),
        pltpu.VMEM((2, 3, T, FP), BF),
        pltpu.VMEM((2, H * T, T), F32),
        pltpu.VMEM((T, FP), BF),
        wide,
        pltpu.VMEM((4, T, 1), F32),
        wide, wide, wide, wide, wide, wide, wide, wide,
        pltpu.VMEM((2, X, C, Z + 1, MAIN, FP), BF),
        pltpu.VMEM((2, X, Z + 1, MAIN, FP), BF),
        pltpu.VMEM((2, X, Z + 1, MAIN, FP), BF),
        pltpu.VMEM((2, X, Z + 1, MAIN, FP), BF),
        pltpu.VMEM((2, Z, MAIN, FP), BF),
        pltpu.VMEM((2, DP * Z, MAIN, FP), BF),
    ]
    vmem = pl.BlockSpec(memory_space=pltpu.VMEM)
    out, igrad, wg_s, wg_t = pl.pallas_call(
        functools.partial(kernel, dims, names),
        out_shape=(
            jax.ShapeDtypeStruct((T, F), BF),
            jax.ShapeDtypeStruct((T, F), BF),
            jax.ShapeDtypeStruct((rows, F), F32),
            jax.ShapeDtypeStruct((rows, F), F32),
        ),
        in_specs=[vmem] * 7,
        out_specs=(vmem,) * 4,
        scratch_shapes=scratch,
        compiler_params=pltpu.CompilerParams(
            collective_id=0, has_side_effects=True, vmem_limit_bytes=56 * 2**20
        ),
    )(tokens.reshape(T, F), cotangent.reshape(T, F), modulation, qkv_s, out_s, qkv_t, out_t)
    out, igrad, wg_s, wg_t = pl.pallas_call(
        hand_on,
        out_shape=tuple(jax.ShapeDtypeStruct(v.shape, v.dtype) for v in (out, igrad, wg_s, wg_t)),
        in_specs=[vmem] * 4,
        out_specs=(vmem,) * 4,
    )(out, igrad, wg_s, wg_t)
    shape = (1, frames, patches, F)
    return out.reshape(shape), igrad.reshape(shape), wg_s, wg_t


def solution(mesh):
    sizes = tuple(mesh.shape[a] for a in ("dp", "seq", "tp"))
    placed = (
        P("dp", "seq", None, "tp"),
        P("dp", None, None),
        P("seq", None, "tp"),
        P("seq", "tp"),
        P("seq", None, "tp"),
        P("seq", "tp"),
        P("dp", "seq", None, "tp"),
    )
    return jax.shard_map(
        functools.partial(on_device, sizes),
        mesh=mesh,
        in_specs=placed,
        out_specs=(
            P("dp", "seq", None, "tp"),
            P("dp", "seq", None, "tp"),
            P("seq", "tp"),
            P("seq", "tp"),
        ),
        check_vma=False,
    )
```

```python
import functools

import jax
import jax.numpy as jnp
from jax import lax
from jax.experimental import pallas as pl
from jax.experimental.pallas import tpu as pltpu
from jax.sharding import PartitionSpec as P

HD = 72
EPS = 1e-06
MAIN = 16
MESH = pl.DeviceIdType.MESH
BF = jnp.bfloat16
F32 = jnp.float32


def mm(a, b):
    return lax.dot_general(a, b, (((1,), (0,)), ((), ())), preferred_element_type=F32)


def mm_nt(a, b):
    return lax.dot_general(a, b, (((1,), (1,)), ((), ())), preferred_element_type=F32)


def mm_tn(a, b):
    return lax.dot_general(a, b, (((0,), (0,)), ((), ())), preferred_element_type=F32)


def iota(shape, axis):
    return lax.broadcasted_iota(jnp.int32, shape, axis)


class Sems:
    def __init__(self):
        self.count = 0

    def take(self, n):
        first = self.count
        self.count += n
        return first


def layout(X, C, Z, Y, DP):
    s = Sems()
    names = {}
    G = X * C
    for name in ("tok", "ggt", "rs1", "fst", "rsg", "rsp", "ggs", "rsf"):
        names[name] = s.take(Y)
    for name in ("cot_x", "fst_x", "fg_x", "out_x"):
        names[name] = s.take(G)
    for name in ("cot_z", "fst_z", "fg_z", "out_z"):
        names[name] = s.take(Z)
    for name in ("zu0", "zd0", "zu1", "zd1", "xr0", "xl0", "xo0"):
        names[name] = s.take(Z)
    names["sib0"] = s.take(X * Z)
    names["xp1"] = s.take(X)
    names["sib1"] = s.take(X)
    for b in (0, 1):
        names["wc%d" % b] = s.take(1)
        names["wx%d" % b] = s.take(X)
        names["wy%d" % b] = s.take(X)
        names["wr%d" % b] = s.take(X)
        names["wz%d" % b] = s.take(DP * Z)
    return names, s.count


def kernel(dims, names, tok, cot, mods, qkv_s, out_s, qkv_t, out_t, out, igrad, wg_s, wg_t, *refs):
    X, C, Z, Y, DP, T, F, FP, H, R2 = dims
    G = X * C
    N = Y * F
    (
        ssem, rsem, wown, wown_t, mod, pm, pr, xw_s, xw_t, gw_t, gw_s, Ws, Wt, Wr, cotp,
        cot_a, cot_b, cot_c, fst_a, fst_b, fst_c, fst_d, fg_a, fg_b, fg_c, fg_d, fg_e,
        out_a, out_b, out_c, out_d,
        mp, mpr, qkv, prob, flat_s, stat,
        rs1_a, rs1_b, rsg_a, rsg_b, rsp_a, rsp_b, rsf_a, rsf_b,
        wgp, wgc, wgx, wgxr, wgz, wgzr,
    ) = refs

    d = lax.axis_index("dp")
    s = lax.axis_index("seq")
    y = lax.axis_index("tp")
    x = s // (Z * C)
    z = lax.rem(s // C, Z)
    c = lax.rem(s, C)
    g = x * C + c
    zg = d * Z + z

    def seq_of(x_, z_, c_):
        return (x_ * Z + z_) * C + c_

    def dev(d_, x_, z_, c_, y_):
        return {"dp": d_, "seq": seq_of(x_, z_, c_), "tp": y_}

    def dev_y(y_):
        return dev(d, x, z, c, y_)

    def dev_g(g_):
        return dev(d, g_ // C, z, lax.rem(g_, C), y)

    def dev_z(z_):
        return dev(d, x, z_, c, y)

    def dev_zg(zg_):
        return dev(zg_ // Z, x, lax.rem(zg_, Z), c, y)

    def dev_x(x_):
        return dev(d, x_, z, c, y)

    sibling = dev(d, x, z, 1 - c, y)
    ZG = DP * Z
    sent = []

    def send(src, dst, sem, device):
        copy = pltpu.make_async_remote_copy(
            src_ref=src, dst_ref=dst, send_sem=ssem.at[sem], recv_sem=rsem.at[sem],
            device_id=device, device_id_type=MESH,
        )
        copy.start()
        sent.append(copy)

    def drain(keep=0):
        while len(sent) > keep:
            sent.pop(0).wait_send()

    def recv(dst, sem):
        pltpu.make_async_remote_copy(
            src_ref=dst, dst_ref=dst, send_sem=ssem.at[sem], recv_sem=rsem.at[sem],
            device_id=sibling, device_id_type=MESH,
        ).wait_recv()

    def ex_send(src, dst, sem, n, me, device):
        for k in range(1, n):
            peer = lax.rem(me + k, n)
            send(src(peer), dst.at[me], sem + k, device(peer))

    def ex_wait(dst, sem, n, me):
        for k in range(1, n):
            recv(dst.at[lax.rem(me + n - k, n)], sem + k)

    barrier = pltpu.get_barrier_semaphore()
    peers = [dev_y(lax.rem(y + k, Y)) for k in range(1, Y)]
    peers += [dev_g(lax.rem(g + k, G)) for k in range(1, G)]
    peers += [dev_zg(lax.rem(zg + k, ZG)) for k in range(1, ZG)]
    for peer in peers:
        pl.semaphore_signal(barrier, inc=1, device_id=peer, device_id_type=MESH)

    rows = MAIN + R2

    def widened(value):
        return jnp.concatenate([value, jnp.zeros((value.shape[0], FP - F), F32)], axis=1)

    rest = []
    for ref, qkv_ref, out_ref in ((wown, qkv_s, out_s), (wown_t, qkv_t, out_t)):
        value = qkv_ref[...].astype(F32)
        for k in range(4):
            part = value[:, k, :] if k < 3 else out_ref[...].astype(F32)
            part = widened(part.reshape(rows, F))
            ref[k] = part[:MAIN].astype(BF)
            rest.append(part[MAIN:])
    wown[4] = jnp.concatenate(rest, axis=0).astype(BF)

    pl.semaphore_wait(barrier, len(peers))

    up, down = dev_zg(lax.rem(zg + 1, ZG)), dev_zg(lax.rem(zg + ZG - 1, ZG))
    right, left = lax.rem(x + 1, X), lax.rem(x + X - 1, X)
    across = lax.rem(x + X // 2, X)
    nup = Z // 2
    ndown = Z - 1 - nup

    def w_slot(b, x_, c_, z_):
        return (Wt if b else Ws).at[:, x_, c_, z_]

    def z_hop(step, first, b):
        z_ = lax.rem(z + first * step + Z * Z, Z)
        slot = w_slot(b, x, c, z_)
        src = (wown_t if b else wown) if step == 0 else slot
        send(src, slot, names["z%s%d" % ("u" if first < 0 else "d", b)] + step, up if first < 0 else down)

    def z_take(step, first, b):
        z_ = lax.rem(z + first * (step + 1) + Z * Z, Z)
        recv(w_slot(b, x, c, z_), names["z%s%d" % ("u" if first < 0 else "d", b)] + step)
        return z_

    def z_start(b):
        if nup:
            z_hop(0, -1, b)
        if ndown:
            z_hop(0, 1, b)

    def z_step(b, step):
        z_take(step, -1, b)
        if step + 1 < nup:
            z_hop(step + 1, -1, b)
        if step >= ndown:
            return [2 * step + 1]
        z_take(step, 1, b)
        if step + 1 < ndown:
            z_hop(step + 1, 1, b)
        return [2 * step + 1, 2 * step + 2]

    def order(i):
        return lax.rem(z + (-(i + 1) // 2 if i % 2 else i // 2) + Z, Z)

    def x_hop(i, own=False):
        slot = w_slot(0, x, c, order(i))
        src = wown if own else slot
        send(src, slot, names["xr0"] + i, dev_x(right))
        if X > 2:
            send(src, slot, names["xl0"] + i, dev_x(left))
        send(src, w_slot(0, x, c, order(i)), names["sib0"] + i, sibling)

    def x_take(i):
        recv(w_slot(0, left, c, order(i)), names["xr0"] + i)
        if X > 2:
            slot = w_slot(0, left, c, order(i))
            if i % 2 == 0:
                send(slot, slot, names["xo0"] + i, dev_x(right))
            send(slot, slot, names["sib0"] + Z + i, sibling)
            slot = w_slot(0, right, c, order(i))
            recv(slot, names["xl0"] + i)
            if i % 2 == 1:
                send(slot, slot, names["xo0"] + i, dev_x(left))
            send(slot, slot, names["sib0"] + 2 * Z + i, sibling)
        else:
            slot = w_slot(0, left, c, order(i))
            send(slot, slot, names["sib0"] + Z + i, sibling)

    def x_last(i):
        slot = w_slot(0, across, c, order(i))
        recv(slot, names["xo0"] + i)
        send(slot, slot, names["sib0"] + 3 * Z + i, sibling)

    z_start(0)
    x_hop(0, True)
    xw_s[y] = jnp.zeros((T, FP), BF)
    xw_s[y, :, :F] = tok[...]
    ex_send(lambda p: xw_s.at[y], xw_s, names["tok"], Y, y, dev_y)
    cotp[...] = jnp.zeros((T, FP), BF)
    cotp[:, :F] = cot[...]

    row = iota((T, T), 0)
    col = iota((T, T), 1)

    def swap_rows(value, source):
        return mm((col == source).astype(BF), value).astype(BF)

    def to_groups(value):
        return swap_rows(value, lax.rem(row // Z, 2) * (G * Z) + row // (2 * Z) * Z + lax.rem(row, Z))

    def from_groups(value):
        return swap_rows(
            value, lax.rem(row // Z, G) * (2 * Z) + row // (G * Z) * Z + lax.rem(row, Z)
        )

    def to_z(value):
        return swap_rows(value, lax.rem(row, 2 * G) * Z + row // (2 * G))

    def from_z(value):
        return swap_rows(value, lax.rem(row, Z) * (2 * G) + row // Z)

    def x_put(buf, value):
        buf[...] = value.reshape(G, 2 * Z, FP)

    def z_put(buf, value):
        buf[...] = value.reshape(Z, 2 * G, FP)

    def flatten(buf):
        return buf[...].reshape(T, FP)

    x_put(cot_a, to_groups(cotp[...]))
    ex_send(lambda p: cot_a.at[p], cot_b, names["cot_x"], G, g, dev_g)
    cot_b[g] = cot_a[g]
    for k in range(5):
        Ws[k, x, c, z] = wown[k]
    for k in range(4):
        Wt[k, x, c, z] = wown_t[k]
    mod[...] = jnp.zeros((6, Y, 1, FP), F32)
    for i in range(6):
        for n in range(Y):
            mod[i, n, :, :F] = mods[i, :, n * F : (n + 1) * F]

    CZ = C * Z
    j = iota((FP, CZ * MAIN), 1)
    target = (lax.rem(j // MAIN, Z) * C + j // (Z * MAIN)) * (MAIN + R2) + lax.rem(j, MAIN)
    pm[...] = (iota((FP, CZ * MAIN), 0) == target).astype(BF)
    j = iota((FP, X * CZ * R2), 1)
    target = (lax.rem(j // R2, Z) * C + lax.rem(j // (Z * R2), C)) * (MAIN + R2)
    target += MAIN + lax.rem(j, R2)
    hit = iota((FP, X * CZ * R2), 0) == target
    for x_ in range(X):
        pr[x_] = (hit & (j // (CZ * R2) == x_)).astype(BF)

    lane = iota((1, FP), 1)
    inside = lane < F
    head = [(lane >= h * HD) & (lane < (h + 1) * HD) for h in range(H)]

    def narrow(slices):
        rest = None
        for x_ in range(X):
            part = slices[x_]
            mp[:, x_ * CZ * MAIN : (x_ + 1) * CZ * MAIN] = mm(part, pm[...]).astype(BF)
            more = mm(part, pr[x_])
            rest = more if rest is None else rest + more
        mpr[...] = rest.astype(BF)

    def natural(main, rest, x_):
        return mm_nt(main[:, x_ * CZ * MAIN : (x_ + 1) * CZ * MAIN], pm[...]) + mm_nt(rest, pr[x_])

    def norm(xw, at):
        total = None
        for n in range(Y):
            part = jnp.sum(xw[n].astype(F32), axis=-1, keepdims=True)
            total = part if total is None else total + part
        mean = total * (1.0 / N)
        total = None
        for n in range(Y):
            center = jnp.where(inside, xw[n].astype(F32) - mean, 0.0)
            part = jnp.sum(center * center, axis=-1, keepdims=True)
            total = part if total is None else total + part
        inverse = lax.rsqrt(total * (1.0 / N) + EPS)
        stat[2 * at] = mean
        stat[2 * at + 1] = inverse
        slices = []
        for n in range(Y):
            normed = (xw[n].astype(F32) - mean) * inverse
            slices.append((normed * (1.0 + mod[3 * at + 1, n]) + mod[3 * at, n]).astype(BF))
        narrow(slices)

    K = X * CZ * MAIN

    def weight(b, k):
        return (Wt if b else Ws)[k].reshape(K, FP), Wr[b * 4 + k]

    def project(b):
        for k in range(3):
            main, rest = weight(b, k)
            qkv[b, k] = (mm(mp[...], main) + mm(mpr[...], rest)).astype(BF)

    def spread(value):
        zero = jnp.zeros_like(value)
        return jnp.concatenate([jnp.where(head[h], value, zero) for h in range(H)], axis=0)

    def gather_heads(value):
        total = None
        for h in range(H):
            part = jnp.where(head[h], value[h * T : (h + 1) * T], 0.0)
            total = part if total is None else total + part
        return total.astype(BF)

    SCALE = HD ** (-0.5)

    def attend(b):
        scores = mm_nt(spread(qkv[b, 0]), qkv[b, 1]) * SCALE
        if b == 0:
            query_frame = lax.rem(iota((H * T, T), 0), T) // (G * Z)
            same = query_frame == iota((H * T, T), 1) // (G * Z)
            scores = jnp.where(same, scores, -1e30)
        weights = jnp.exp(scores - jnp.max(scores, axis=-1, keepdims=True))
        prob[b] = weights / jnp.sum(weights, axis=-1, keepdims=True)
        return gather_heads(mm(prob[b].astype(BF), qkv[b, 2]))

    def attend_back(b, grad):
        grads = spread(grad)
        likely = prob[b]
        grad_values = mm_tn(likely.astype(BF), grads).astype(BF)
        grad_likely = mm_nt(grads, qkv[b, 2])
        shift = grad_likely - jnp.sum(likely * grad_likely, axis=-1, keepdims=True)
        grad_scores = (likely * shift * SCALE).astype(BF)
        grad_query = gather_heads(mm(grad_scores, qkv[b, 1]))
        grad_keys = mm_tn(grad_scores, spread(qkv[b, 0])).astype(BF)
        return grad_query, grad_keys, grad_values

    def out_partial(b, flat, buf):
        main, rest = weight(b, 3)
        part = mm_nt(flat, main).astype(BF)
        part_rest = mm_nt(flat, rest).astype(BF)
        for n in range(Y):
            buf[n] = natural(part, part_rest, n).astype(BF)

    def grad_heads(b):
        main, rest = weight(b, 3)
        return (mm(mp[...], main) + mm(mpr[...], rest)).astype(BF)

    def in_partial(b, grads, xw, buf):
        part, part_rest = None, None
        for k in range(3):
            main, rest = weight(b, k)
            a, r = mm_nt(grads[k], main), mm_nt(grads[k], rest)
            part = a if part is None else part + a
            part_rest = r if part_rest is None else part_rest + r
        part, part_rest = part.astype(BF), part_rest.astype(BF)
        mean, inverse = stat[2 * b], stat[2 * b + 1]
        first, second = None, None
        slices = []
        for n in range(Y):
            value = natural(part, part_rest, n)
            slices.append(value)
            scaled = value * (1.0 + mod[3 * b + 1, n])
            normed = (xw[n].astype(F32) - mean) * inverse
            a = jnp.sum(scaled, axis=-1, keepdims=True)
            r = jnp.sum(scaled * normed, axis=-1, keepdims=True)
            first = a if first is None else first + a
            second = r if second is None else second + r
        for n in range(Y):
            value = jnp.where(lane == F, first, jnp.where(lane == F + 1, second, slices[n]))
            buf[n] = value.astype(BF)

    def in_finish(b, buf, xw, incoming):
        total = buf[0].astype(F32)
        for n in range(1, Y):
            total = total + buf[n].astype(F32)
        first = total[:, F : F + 1] * (1.0 / N)
        second = total[:, F + 1 : F + 2] * (1.0 / N)
        scaled = total * (1.0 + mod[3 * b + 1, y])
        normed = (xw[y].astype(F32) - stat[2 * b]) * stat[2 * b + 1]
        grad = stat[2 * b + 1] * (scaled - first - normed * second)
        return jnp.where(inside, incoming.astype(F32) + grad, 0.0).astype(BF)

    def add_up(buf):
        total = buf[0].astype(F32)
        for n in range(1, Y):
            total = total + buf[n].astype(F32)
        return total

    def gated(b, value):
        return (mod[3 * b + 2, y] * value.astype(F32)).astype(BF)

    HZ = Z // 2
    near = z // HZ * HZ
    far = HZ - near
    FULL = FP - 128
    WP = 128 - (F - FULL)

    def shift_lanes(n):
        a, b = iota((FP, 128), 0), iota((FP, 128), 1)
        return ((a - n * WP == b - (128 - WP)) & (b >= 128 - WP)).astype(BF)

    def wg_start(b, flat):
        main = mm_tn(mp[...], flat).astype(BF)
        rest = mm_tn(mpr[...], flat).astype(BF)
        wgp[b, :, :, :Z] = main.reshape(X, C, Z, MAIN, FP)
        wgp[b, :, :, Z] = rest.reshape(X, C, Z * R2, FP)
        send(wgp.at[b, :, 1 - c], wgc.at[b], names["wc%d" % b], sibling)

    def wg_second(b):
        recv(wgc.at[b], names["wc%d" % b])
        wgx[b] = (wgp[b, :, c].astype(F32) + wgc[b].astype(F32)).astype(BF)
        for name, start in (("wx%d" % b, far), ("wr%d" % b, Z), ("wy%d" % b, near)):
            blocks = pl.ds(start, 1 if name[1] == "r" else HZ)
            for k in range(1, X):
                to_x = lax.rem(x + k, X)
                send(wgx.at[b, to_x, blocks], wgxr.at[b, x, blocks], names[name] + k, dev_x(to_x))
        wgxr[b, x] = wgx[b, x]

    def wg_take(b, name, blocks):
        for k in range(1, X):
            recv(wgxr.at[b, lax.rem(x + X - k, X), blocks], names[name + str(b)] + k)
        total = wgxr[b, 0, blocks].astype(F32)
        for n in range(1, X):
            total = total + wgxr[b, n, blocks].astype(F32)
        return total.astype(BF)

    def wg_third(b, start):
        blocks = pl.ds(start, HZ)
        main = wg_take(b, "wx" if start is far else "wy", blocks).reshape(HZ * MAIN, FP)
        if start is far:
            wgxr[b, 0, Z] = wg_take(b, "wr", pl.ds(Z, 1))[0]
        rest = wgxr[b, 0, Z]
        wgz[b, blocks, :, :FULL] = main[:, :FULL].reshape(HZ, MAIN, FULL)
        tail = main[:, FULL:].astype(F32)
        for n in range(F // WP):
            pick = shift_lanes(n)
            o = iota((HZ * MAIN, Z * R2), 0)
            slot = lax.rem(o, MAIN) - n * R2
            rows = (o // MAIN + start) * R2 + slot == iota((HZ * MAIN, Z * R2), 1)
            rows = (rows & (slot >= 0) & (slot < R2)).astype(BF)
            tail = tail + mm(rows, mm(rest, pick).astype(BF))
        wgz[b, blocks, :, FULL:] = tail.astype(BF).reshape(HZ, MAIN, 128)
        for m in range(HZ):
            for e in range(DP):
                if start is near and m == 0 and e == 0:
                    continue
                z_ = start + lax.rem(lax.rem(z, HZ) + m, HZ)
                peer = lax.rem(d + e, DP) * Z + z_
                hop = lax.rem(peer + ZG - zg, ZG)
                send(wgz.at[b, z_], wgzr.at[b, zg], names["wz%d" % b] + hop, dev_zg(peer))
        if start is near:
            wgzr[b, zg] = wgz[b, z]

    def wg_end(b, ref):
        ex_wait(wgzr.at[b], names["wz%d" % b], ZG, zg)
        total = wgzr[b, 0].astype(F32)
        for n in range(1, ZG):
            total = total + wgzr[b, n].astype(F32)
        ref[:MAIN, :FULL] = total[:, :FULL]
        tail = total[:, FULL:]
        ref[:MAIN, FULL:] = tail[:, : F - FULL]
        for n in range(F // WP):
            ref[MAIN : MAIN + R2, n * WP : (n + 1) * WP] = tail[n * R2 : (n + 1) * R2, 128 - WP :]

    before = [0]
    for step in range(nup):
        here = z_step(0, step)
        for i in here:
            x_hop(i)
        for i in before:
            x_take(i)
        before = here
    z_start(1)

    ex_wait(cot_b, names["cot_x"], G, g)
    z_put(cot_c.at[0], to_z(flatten(cot_b)))
    ex_send(lambda p: cot_c.at[0, p], cot_c.at[1], names["cot_z"], Z, z, dev_z)
    cot_c[1, z] = cot_c[0, z]

    ex_wait(xw_s, names["tok"], Y, y)
    norm(xw_s, 0)

    for i in before:
        x_take(i)
    if X > 2:
        for i in range(Z):
            x_last(i)
    for i in range(Z):
        recv(w_slot(0, x, 1 - c, order(i)), names["sib0"] + i)
        recv(w_slot(0, left, 1 - c, order(i)), names["sib0"] + Z + i)
        if X > 2:
            recv(w_slot(0, right, 1 - c, order(i)), names["sib0"] + 2 * Z + i)
            recv(w_slot(0, across, 1 - c, order(i)), names["sib0"] + 3 * Z + i)

    def to_sibling(x_, n):
        send(Wt.at[:, x_, c], Wt.at[:, x_, c], names["sib1"] + n, sibling)

    z_steps = iter(range(nup))

    def z_later(n):
        for _ in range(n):
            step = next(z_steps, None)
            if step is not None:
                z_step(1, step)

    z_later(1)

    ex_wait(cot_c.at[1], names["cot_z"], Z, z)
    cot_t = flatten(cot_c.at[1])
    gw_t[y] = gated(1, cot_t)
    ex_send(lambda p: gw_t.at[y], gw_t, names["ggt"], Y, y, dev_y)

    n_rest = CZ * 8 * R2
    o = iota((n_rest, n_rest), 0)
    source = lax.rem(o // R2, CZ) * (8 * R2) + o // (CZ * R2) * R2 + lax.rem(o, R2)
    shuffle = (iota((n_rest, n_rest), 1) == source).astype(BF)
    for x_ in range(X):
        rest = mm(shuffle, Ws[4, x_].reshape(n_rest, FP)).astype(BF)
        Wr[:, x_ * CZ * R2 : (x_ + 1) * CZ * R2] = rest.reshape(8, CZ * R2, FP)

    project(0)
    z_later(1)
    flat_s[...] = attend(0)
    z_later(1)
    out_partial(0, flat_s[...], rs1_a)
    ex_send(lambda p: rs1_a.at[p], rs1_b, names["rs1"], Y, y, dev_y)
    rs1_b[y] = rs1_a[y]

    z_later(nup)
    for k in range(1, X):
        to_x = lax.rem(x + k, X)
        send(Wt.at[:, x, c], Wt.at[:, x, c], names["xp1"] + k, dev_x(to_x))
    to_sibling(x, 0)
    drain(20)
    ex_wait(rs1_b, names["rs1"], Y, y)
    first = xw_s[y].astype(F32) + mod[2, y] * add_up(rs1_b)
    x_put(fst_a, to_groups(first.astype(BF)))
    ex_send(lambda p: fst_a.at[p], fst_b, names["fst_x"], G, g, dev_g)
    fst_b[g] = fst_a[g]
    ex_wait(fst_b, names["fst_x"], G, g)
    z_put(fst_c, to_z(flatten(fst_b)))
    ex_send(lambda p: fst_c.at[p], fst_d, names["fst_z"], Z, z, dev_z)
    fst_d[z] = fst_c[z]
    for k in range(1, X):
        x_ = lax.rem(x + X - k, X)
        recv(Wt.at[:, x_, c], names["xp1"] + k)
        to_sibling(x_, k)

    for k in range(X):
        recv(Wt.at[:, lax.rem(x + X - k, X), 1 - c], names["sib1"] + k)
    ex_wait(gw_t, names["ggt"], Y, y)

    ex_wait(fst_d, names["fst_z"], Z, z)
    xw_t[y] = flatten(fst_d)
    ex_send(lambda p: xw_t.at[y], xw_t, names["fst"], Y, y, dev_y)

    narrow([gw_t[n] for n in range(Y)])
    grad_t = grad_heads(1)
    drain(2 * Y)

    ex_wait(xw_t, names["fst"], Y, y)
    norm(xw_t, 1)
    project(1)
    flat_t = attend(1)
    grads = attend_back(1, grad_t)
    in_partial(1, grads, xw_t, rsg_a)
    ex_send(lambda p: rsg_a.at[p], rsg_b, names["rsg"], Y, y, dev_y)
    rsg_b[y] = rsg_a[y]

    out_partial(1, flat_t, rsp_a)
    ex_send(lambda p: rsp_a.at[p], rsp_b, names["rsp"], Y, y, dev_y)
    rsp_b[y] = rsp_a[y]

    ex_wait(rsg_b, names["rsg"], Y, y)
    z_put(fg_a, in_finish(1, rsg_b, xw_t, cot_t))
    ex_send(lambda p: fg_a.at[p], fg_b, names["fg_z"], Z, z, dev_z)
    fg_b[z] = fg_a[z]

    narrow([gw_t[n] for n in range(Y)])
    wg_start(1, flat_t)

    ex_wait(fg_b, names["fg_z"], Z, z)
    x_put(fg_c, from_z(flatten(fg_b)))
    ex_send(lambda p: fg_c.at[p], fg_d, names["fg_x"], G, g, dev_g)
    fg_d[g] = fg_c[g]
    wg_second(1)

    ex_wait(rsp_b, names["rsp"], Y, y)
    second = xw_t[y].astype(F32) + mod[5, y] * add_up(rsp_b)
    z_put(out_a, second.astype(BF))
    ex_send(lambda p: out_a.at[p], out_b, names["out_z"], Z, z, dev_z)
    out_b[z] = out_a[z]

    ex_wait(fg_d, names["fg_x"], G, g)
    fg_e[...] = from_groups(flatten(fg_d))
    gw_s[y] = gated(0, fg_e[...])
    ex_send(lambda p: gw_s.at[y], gw_s, names["ggs"], Y, y, dev_y)

    ex_wait(out_b, names["out_z"], Z, z)
    x_put(out_c, from_z(flatten(out_b)))
    ex_send(lambda p: out_c.at[p], out_d, names["out_x"], G, g, dev_g)
    out_d[g] = out_c[g]

    drain(Y + G)

    ex_wait(gw_s, names["ggs"], Y, y)
    narrow([gw_s[n] for n in range(Y)])
    wg_start(0, flat_s[...])
    grad_s = grad_heads(0)
    wg_third(1, far)
    wg_second(0)
    wg_third(1, near)
    grads = attend_back(0, grad_s)
    wg_third(0, far)
    in_partial(0, grads, xw_s, rsf_a)
    ex_send(lambda p: rsf_a.at[p], rsf_b, names["rsf"], Y, y, dev_y)
    rsf_b[y] = rsf_a[y]
    wg_third(0, near)

    ex_wait(out_d, names["out_x"], G, g)
    out[...] = from_groups(flatten(out_d))[:, :F]
    wg_end(1, wg_t)
    ex_wait(rsf_b, names["rsf"], Y, y)
    igrad[...] = in_finish(0, rsf_b, xw_s, fg_e[...])[:, :F]
    drain()
    wg_end(0, wg_s)
    drain()


def hand_on(*refs):
    for source, target in zip(refs[:4], refs[4:]):
        target[...] = source[...]


def on_device(sizes, tokens, modulation, qkv_s, out_s, qkv_t, out_t, cotangent):
    DP, S, Y = sizes
    frames, patches, F = tokens.shape[1:]
    T = frames * patches
    X, C = Y, 2
    Z = S // (X * C)
    G = X * C
    H = F // HD
    rows = out_s.shape[0]
    R2 = rows - MAIN
    FP = (F + 2 + 127) // 128 * 128
    dims = (X, C, Z, Y, DP, T, F, FP, H, R2)
    names, count = layout(X, C, Z, Y, DP)

    K, KR = X * C * Z * MAIN, X * C * Z * R2
    xs, zs = pltpu.VMEM((G, 2 * Z, FP), BF), pltpu.VMEM((Z, 2 * G, FP), BF)
    wide = pltpu.VMEM((Y, T, FP), BF)
    scratch = [
        pltpu.SemaphoreType.DMA((count,)),
        pltpu.SemaphoreType.DMA((count,)),
        pltpu.VMEM((5, MAIN, FP), BF),
        pltpu.VMEM((4, MAIN, FP), BF),
        pltpu.VMEM((6, Y, 1, FP), F32),
        pltpu.VMEM((FP, C * Z * MAIN), BF),
        pltpu.VMEM((X, FP, KR), BF),
        wide, wide, wide, wide,
        pltpu.VMEM((5, X, C, Z, MAIN, FP), BF),
        pltpu.VMEM((4, X, C, Z, MAIN, FP), BF),
        pltpu.VMEM((8, KR, FP), BF),
        pltpu.VMEM((T, FP), BF),
        xs, xs, pltpu.VMEM((2, Z, 2 * G, FP), BF),
        xs, xs, zs, zs,
        zs, zs, xs, xs, pltpu.VMEM((T, FP), BF),
        zs, zs, xs, xs,
        pltpu.VMEM((T, K), BF),
        pltpu.VMEM((T, KR), BF),
        pltpu.VMEM((2, 3, T, FP), BF),
        pltpu.VMEM((2, H * T, T), F32),
        pltpu.VMEM((T, FP), BF),
        pltpu.VMEM((4, T, 1), F32),
        wide, wide, wide, wide, wide, wide, wide, wide,
        pltpu.VMEM((2, X, C, Z + 1, MAIN, FP), BF),
        pltpu.VMEM((2, X, Z + 1, MAIN, FP), BF),
        pltpu.VMEM((2, X, Z + 1, MAIN, FP), BF),
        pltpu.VMEM((2, X, Z + 1, MAIN, FP), BF),
        pltpu.VMEM((2, Z, MAIN, FP), BF),
        pltpu.VMEM((2, DP * Z, MAIN, FP), BF),
    ]
    vmem = pl.BlockSpec(memory_space=pltpu.VMEM)
    out, igrad, wg_s, wg_t = pl.pallas_call(
        functools.partial(kernel, dims, names),
        out_shape=(
            jax.ShapeDtypeStruct((T, F), BF),
            jax.ShapeDtypeStruct((T, F), BF),
            jax.ShapeDtypeStruct((rows, F), F32),
            jax.ShapeDtypeStruct((rows, F), F32),
        ),
        in_specs=[vmem] * 7,
        out_specs=(vmem,) * 4,
        scratch_shapes=scratch,
        compiler_params=pltpu.CompilerParams(
            collective_id=0, has_side_effects=True, vmem_limit_bytes=56 * 2**20
        ),
    )(tokens.reshape(T, F), cotangent.reshape(T, F), modulation.transpose(1, 0, 2), qkv_s, out_s, qkv_t, out_t)
    out, igrad, wg_s, wg_t = pl.pallas_call(
        hand_on,
        out_shape=tuple(jax.ShapeDtypeStruct(v.shape, v.dtype) for v in (out, igrad, wg_s, wg_t)),
        in_specs=[vmem] * 4,
        out_specs=(vmem,) * 4,
    )(out, igrad, wg_s, wg_t)
    shape = (1, frames, patches, F)
    return out.reshape(shape), igrad.reshape(shape), wg_s, wg_t


def solution(mesh):
    sizes = tuple(mesh.shape[a] for a in ("dp", "seq", "tp"))
    placed = (
        P("dp", "seq", None, "tp"),
        P("dp", None, None),
        P("seq", None, "tp"),
        P("seq", "tp"),
        P("seq", None, "tp"),
        P("seq", "tp"),
        P("dp", "seq", None, "tp"),
    )
    return jax.shard_map(
        functools.partial(on_device, sizes),
        mesh=mesh,
        in_specs=placed,
        out_specs=(
            P("dp", "seq", None, "tp"),
            P("dp", "seq", None, "tp"),
            P("seq", "tp"),
            P("seq", "tp"),
        ),
        check_vma=False,
    )
```

```python
import functools

import jax
import jax.numpy as jnp
from jax import lax
from jax.experimental import pallas as pl
from jax.experimental.pallas import tpu as pltpu
from jax.sharding import PartitionSpec as P

HD = 72
EPS = 1e-06
MAIN = 16
MESH = pl.DeviceIdType.MESH
BF = jnp.bfloat16
F32 = jnp.float32


def mm(a, b):
    return lax.dot_general(a, b, (((1,), (0,)), ((), ())), preferred_element_type=F32)


def mm_nt(a, b):
    return lax.dot_general(a, b, (((1,), (1,)), ((), ())), preferred_element_type=F32)


def mm_tn(a, b):
    return lax.dot_general(a, b, (((0,), (0,)), ((), ())), preferred_element_type=F32)


def iota(shape, axis):
    return lax.broadcasted_iota(jnp.int32, shape, axis)


class Sems:
    def __init__(self):
        self.count = 0

    def take(self, n):
        first = self.count
        self.count += n
        return first


def layout(X, C, Z, Y, DP):
    s = Sems()
    names = {}
    G = X * C
    for name in ("tok", "ggt", "rs1", "fst", "rsg", "rsp", "ggs", "rsf"):
        names[name] = s.take(Y)
    for name in ("cot_x", "fst_x", "fg_x", "out_x"):
        names[name] = s.take(G)
    for name in ("cot_z", "fst_z", "fg_z", "out_z"):
        names[name] = s.take(Z)
    for name in ("zu0", "zd0", "zu1", "zd1", "xr0", "xl0", "xo0"):
        names[name] = s.take(Z)
    names["sib0"] = s.take(X * Z)
    names["xp1"] = s.take(X * Z)
    names["sib1"] = s.take(X)
    for b in (0, 1):
        names["wc%d" % b] = s.take(1)
        names["wx%d" % b] = s.take(X)
        names["wy%d" % b] = s.take(X)
        names["wr%d" % b] = s.take(X)
        names["wz%d" % b] = s.take(DP * Z)
    return names, s.count


def kernel(dims, names, tok, cot, mods, qkv_s, out_s, qkv_t, out_t, out, igrad, wg_s, wg_t, *refs):
    X, C, Z, Y, DP, T, F, FP, H, R2 = dims
    G = X * C
    N = Y * F
    (
        ssem, rsem, wown, wown_t, mod, pm, pr, xw_s, xw_t, gw_t, gw_s, Ws, Wt, Wr, cotp,
        cot_a, cot_b, cot_c, fst_a, fst_b, fst_c, fst_d, fg_a, fg_b, fg_c, fg_d, fg_e,
        out_a, out_b, out_c, out_d,
        mp, mpr, qkv, prob, flat_s, stat,
        rs1_a, rs1_b, rsg_a, rsg_b, rsp_a, rsp_b, rsf_a, rsf_b,
        wgp, wgc, wgx, wgxr, wgz, wgzr,
    ) = refs

    d = lax.axis_index("dp")
    s = lax.axis_index("seq")
    y = lax.axis_index("tp")
    x = s // (Z * C)
    z = lax.rem(s // C, Z)
    c = lax.rem(s, C)
    g = x * C + c
    zg = d * Z + z

    def seq_of(x_, z_, c_):
        return (x_ * Z + z_) * C + c_

    def dev(d_, x_, z_, c_, y_):
        return {"dp": d_, "seq": seq_of(x_, z_, c_), "tp": y_}

    def dev_y(y_):
        return dev(d, x, z, c, y_)

    def dev_g(g_):
        return dev(d, g_ // C, z, lax.rem(g_, C), y)

    def dev_z(z_):
        return dev(d, x, z_, c, y)

    def dev_zg(zg_):
        return dev(zg_ // Z, x, lax.rem(zg_, Z), c, y)

    def dev_x(x_):
        return dev(d, x_, z, c, y)

    sibling = dev(d, x, z, 1 - c, y)
    ZG = DP * Z
    sent = []

    def send(src, dst, sem, device):
        copy = pltpu.make_async_remote_copy(
            src_ref=src, dst_ref=dst, send_sem=ssem.at[sem], recv_sem=rsem.at[sem],
            device_id=device, device_id_type=MESH,
        )
        copy.start()
        sent.append(copy)

    def drain(keep=0):
        while len(sent) > keep:
            sent.pop(0).wait_send()

    def recv(dst, sem):
        pltpu.make_async_remote_copy(
            src_ref=dst, dst_ref=dst, send_sem=ssem.at[sem], recv_sem=rsem.at[sem],
            device_id=sibling, device_id_type=MESH,
        ).wait_recv()

    def ex_send(src, dst, sem, n, me, device):
        for k in range(1, n):
            peer = lax.rem(me + k, n)
            send(src(peer), dst.at[me], sem + k, device(peer))

    def ex_wait(dst, sem, n, me):
        for k in range(1, n):
            recv(dst.at[lax.rem(me + n - k, n)], sem + k)

    barrier = pltpu.get_barrier_semaphore()
    peers = [dev_y(lax.rem(y + k, Y)) for k in range(1, Y)]
    peers += [dev_g(lax.rem(g + k, G)) for k in range(1, G)]
    peers += [dev_zg(lax.rem(zg + k, ZG)) for k in range(1, ZG)]
    for peer in peers:
        pl.semaphore_signal(barrier, inc=1, device_id=peer, device_id_type=MESH)

    rows = MAIN + R2

    def widened(value):
        return jnp.concatenate([value, jnp.zeros((value.shape[0], FP - F), F32)], axis=1)

    rest = []
    for ref, qkv_ref, out_ref in ((wown, qkv_s, out_s), (wown_t, qkv_t, out_t)):
        value = qkv_ref[...].astype(F32)
        for k in range(4):
            part = value[:, k, :] if k < 3 else out_ref[...].astype(F32)
            part = widened(part.reshape(rows, F))
            ref[k] = part[:MAIN].astype(BF)
            rest.append(part[MAIN:])
    wown[4] = jnp.concatenate(rest, axis=0).astype(BF)

    pl.semaphore_wait(barrier, len(peers))

    up, down = dev_zg(lax.rem(zg + 1, ZG)), dev_zg(lax.rem(zg + ZG - 1, ZG))
    right, left = lax.rem(x + 1, X), lax.rem(x + X - 1, X)
    across = lax.rem(x + X // 2, X)
    nup = Z // 2
    ndown = Z - 1 - nup

    def w_slot(b, x_, c_, z_):
        return (Wt if b else Ws).at[:, x_, c_, z_]

    def z_hop(step, first, b):
        z_ = lax.rem(z + first * step + Z * Z, Z)
        slot = w_slot(b, x, c, z_)
        src = (wown_t if b else wown) if step == 0 else slot
        send(src, slot, names["z%s%d" % ("u" if first < 0 else "d", b)] + step, up if first < 0 else down)

    def z_take(step, first, b):
        z_ = lax.rem(z + first * (step + 1) + Z * Z, Z)
        recv(w_slot(b, x, c, z_), names["z%s%d" % ("u" if first < 0 else "d", b)] + step)
        return z_

    def z_start(b):
        if nup:
            z_hop(0, -1, b)
        if ndown:
            z_hop(0, 1, b)

    def z_step(b, step):
        z_take(step, -1, b)
        if step + 1 < nup:
            z_hop(step + 1, -1, b)
        if step >= ndown:
            return [2 * step + 1]
        z_take(step, 1, b)
        if step + 1 < ndown:
            z_hop(step + 1, 1, b)
        return [2 * step + 1, 2 * step + 2]

    def order(i):
        return lax.rem(z + (-(i + 1) // 2 if i % 2 else i // 2) + Z, Z)

    def x_hop(i, own=False):
        slot = w_slot(0, x, c, order(i))
        src = wown if own else slot
        send(src, slot, names["xr0"] + i, dev_x(right))
        if X > 2:
            send(src, slot, names["xl0"] + i, dev_x(left))
        send(src, w_slot(0, x, c, order(i)), names["sib0"] + i, sibling)

    def x_take(i):
        recv(w_slot(0, left, c, order(i)), names["xr0"] + i)
        if X > 2:
            slot = w_slot(0, left, c, order(i))
            if i % 2 == 0:
                send(slot, slot, names["xo0"] + i, dev_x(right))
            send(slot, slot, names["sib0"] + Z + i, sibling)
            slot = w_slot(0, right, c, order(i))
            recv(slot, names["xl0"] + i)
            if i % 2 == 1:
                send(slot, slot, names["xo0"] + i, dev_x(left))
            send(slot, slot, names["sib0"] + 2 * Z + i, sibling)
        else:
            slot = w_slot(0, left, c, order(i))
            send(slot, slot, names["sib0"] + Z + i, sibling)

    def x_last(i):
        slot = w_slot(0, across, c, order(i))
        recv(slot, names["xo0"] + i)
        send(slot, slot, names["sib0"] + 3 * Z + i, sibling)

    z_start(0)
    x_hop(0, True)
    xw_s[y] = jnp.zeros((T, FP), BF)
    xw_s[y, :, :F] = tok[...]
    ex_send(lambda p: xw_s.at[y], xw_s, names["tok"], Y, y, dev_y)
    cotp[...] = jnp.zeros((T, FP), BF)
    cotp[:, :F] = cot[...]

    row = iota((T, T), 0)
    col = iota((T, T), 1)

    def swap_rows(value, source):
        return mm((col == source).astype(BF), value).astype(BF)

    def to_groups(value):
        return swap_rows(value, lax.rem(row // Z, 2) * (G * Z) + row // (2 * Z) * Z + lax.rem(row, Z))

    def from_groups(value):
        return swap_rows(
            value, lax.rem(row // Z, G) * (2 * Z) + row // (G * Z) * Z + lax.rem(row, Z)
        )

    def to_z(value):
        return swap_rows(value, lax.rem(row, 2 * G) * Z + row // (2 * G))

    def from_z(value):
        return swap_rows(value, lax.rem(row, Z) * (2 * G) + row // Z)

    def x_put(buf, value):
        buf[...] = value.reshape(G, 2 * Z, FP)

    def z_put(buf, value):
        buf[...] = value.reshape(Z, 2 * G, FP)

    def flatten(buf):
        return buf[...].reshape(T, FP)

    x_put(cot_a, to_groups(cotp[...]))
    ex_send(lambda p: cot_a.at[p], cot_b, names["cot_x"], G, g, dev_g)
    cot_b[g] = cot_a[g]
    for k in range(5):
        Ws[k, x, c, z] = wown[k]
    for k in range(4):
        Wt[k, x, c, z] = wown_t[k]
    mod[...] = jnp.zeros((6, Y, 1, FP), F32)
    for i in range(6):
        for n in range(Y):
            mod[i, n, :, :F] = mods[i, :, n * F : (n + 1) * F]

    CZ = C * Z
    j = iota((FP, CZ * MAIN), 1)
    target = (lax.rem(j // MAIN, Z) * C + j // (Z * MAIN)) * (MAIN + R2) + lax.rem(j, MAIN)
    pm[...] = (iota((FP, CZ * MAIN), 0) == target).astype(BF)
    j = iota((FP, X * CZ * R2), 1)
    target = (lax.rem(j // R2, Z) * C + lax.rem(j // (Z * R2), C)) * (MAIN + R2)
    target += MAIN + lax.rem(j, R2)
    hit = iota((FP, X * CZ * R2), 0) == target
    for x_ in range(X):
        pr[x_] = (hit & (j // (CZ * R2) == x_)).astype(BF)

    lane = iota((1, FP), 1)
    inside = lane < F
    head = [(lane >= h * HD) & (lane < (h + 1) * HD) for h in range(H)]

    def narrow(slices):
        rest = None
        for x_ in range(X):
            part = slices[x_]
            mp[:, x_ * CZ * MAIN : (x_ + 1) * CZ * MAIN] = mm(part, pm[...]).astype(BF)
            more = mm(part, pr[x_])
            rest = more if rest is None else rest + more
        mpr[...] = rest.astype(BF)

    def natural(main, rest, x_):
        return mm_nt(main[:, x_ * CZ * MAIN : (x_ + 1) * CZ * MAIN], pm[...]) + mm_nt(rest, pr[x_])

    def norm(xw, at):
        total = None
        for n in range(Y):
            part = jnp.sum(xw[n].astype(F32), axis=-1, keepdims=True)
            total = part if total is None else total + part
        mean = total * (1.0 / N)
        total = None
        for n in range(Y):
            center = jnp.where(inside, xw[n].astype(F32) - mean, 0.0)
            part = jnp.sum(center * center, axis=-1, keepdims=True)
            total = part if total is None else total + part
        inverse = lax.rsqrt(total * (1.0 / N) + EPS)
        stat[2 * at] = mean
        stat[2 * at + 1] = inverse
        slices = []
        for n in range(Y):
            normed = (xw[n].astype(F32) - mean) * inverse
            slices.append((normed * (1.0 + mod[3 * at + 1, n]) + mod[3 * at, n]).astype(BF))
        narrow(slices)

    K = X * CZ * MAIN

    def weight(b, k):
        return (Wt if b else Ws)[k].reshape(K, FP), Wr[b * 4 + k]

    def project(b):
        for k in range(3):
            main, rest = weight(b, k)
            qkv[b, k] = (mm(mp[...], main) + mm(mpr[...], rest)).astype(BF)

    def spread(value):
        zero = jnp.zeros_like(value)
        return jnp.concatenate([jnp.where(head[h], value, zero) for h in range(H)], axis=0)

    def gather_heads(value):
        total = None
        for h in range(H):
            part = jnp.where(head[h], value[h * T : (h + 1) * T], 0.0)
            total = part if total is None else total + part
        return total.astype(BF)

    SCALE = HD ** (-0.5)

    def attend(b):
        scores = mm_nt(spread(qkv[b, 0]), qkv[b, 1]) * SCALE
        if b == 0:
            query_frame = lax.rem(iota((H * T, T), 0), T) // (G * Z)
            same = query_frame == iota((H * T, T), 1) // (G * Z)
            scores = jnp.where(same, scores, -1e30)
        weights = jnp.exp(scores - jnp.max(scores, axis=-1, keepdims=True))
        prob[b] = weights / jnp.sum(weights, axis=-1, keepdims=True)
        return gather_heads(mm(prob[b].astype(BF), qkv[b, 2]))

    def attend_back(b, grad):
        grads = spread(grad)
        likely = prob[b]
        grad_values = mm_tn(likely.astype(BF), grads).astype(BF)
        grad_likely = mm_nt(grads, qkv[b, 2])
        shift = grad_likely - jnp.sum(likely * grad_likely, axis=-1, keepdims=True)
        grad_scores = (likely * shift * SCALE).astype(BF)
        grad_query = gather_heads(mm(grad_scores, qkv[b, 1]))
        grad_keys = mm_tn(grad_scores, spread(qkv[b, 0])).astype(BF)
        return grad_query, grad_keys, grad_values

    def out_partial(b, flat, buf):
        main, rest = weight(b, 3)
        part = mm_nt(flat, main).astype(BF)
        part_rest = mm_nt(flat, rest).astype(BF)
        for n in range(Y):
            buf[n] = natural(part, part_rest, n).astype(BF)

    def grad_heads(b):
        main, rest = weight(b, 3)
        return (mm(mp[...], main) + mm(mpr[...], rest)).astype(BF)

    def in_partial(b, grads, xw, buf):
        part, part_rest = None, None
        for k in range(3):
            main, rest = weight(b, k)
            a, r = mm_nt(grads[k], main), mm_nt(grads[k], rest)
            part = a if part is None else part + a
            part_rest = r if part_rest is None else part_rest + r
        part, part_rest = part.astype(BF), part_rest.astype(BF)
        mean, inverse = stat[2 * b], stat[2 * b + 1]
        first, second = None, None
        slices = []
        for n in range(Y):
            value = natural(part, part_rest, n)
            slices.append(value)
            scaled = value * (1.0 + mod[3 * b + 1, n])
            normed = (xw[n].astype(F32) - mean) * inverse
            a = jnp.sum(scaled, axis=-1, keepdims=True)
            r = jnp.sum(scaled * normed, axis=-1, keepdims=True)
            first = a if first is None else first + a
            second = r if second is None else second + r
        for n in range(Y):
            value = jnp.where(lane == F, first, jnp.where(lane == F + 1, second, slices[n]))
            buf[n] = value.astype(BF)

    def in_finish(b, buf, xw, incoming):
        total = buf[0].astype(F32)
        for n in range(1, Y):
            total = total + buf[n].astype(F32)
        first = total[:, F : F + 1] * (1.0 / N)
        second = total[:, F + 1 : F + 2] * (1.0 / N)
        scaled = total * (1.0 + mod[3 * b + 1, y])
        normed = (xw[y].astype(F32) - stat[2 * b]) * stat[2 * b + 1]
        grad = stat[2 * b + 1] * (scaled - first - normed * second)
        return jnp.where(inside, incoming.astype(F32) + grad, 0.0).astype(BF)

    def add_up(buf):
        total = buf[0].astype(F32)
        for n in range(1, Y):
            total = total + buf[n].astype(F32)
        return total

    def gated(b, value):
        return (mod[3 * b + 2, y] * value.astype(F32)).astype(BF)

    HZ = Z // 2
    near = z // HZ * HZ
    far = HZ - near
    FULL = FP - 128
    WP = 128 - (F - FULL)

    def shift_lanes(n):
        a, b = iota((FP, 128), 0), iota((FP, 128), 1)
        return ((a - n * WP == b - (128 - WP)) & (b >= 128 - WP)).astype(BF)

    def wg_start(b, flat):
        main = mm_tn(mp[...], flat).astype(BF)
        rest = mm_tn(mpr[...], flat).astype(BF)
        wgp[b, :, :, :Z] = main.reshape(X, C, Z, MAIN, FP)
        wgp[b, :, :, Z] = rest.reshape(X, C, Z * R2, FP)
        send(wgp.at[b, :, 1 - c], wgc.at[b], names["wc%d" % b], sibling)

    def wg_second(b):
        recv(wgc.at[b], names["wc%d" % b])
        wgx[b] = (wgp[b, :, c].astype(F32) + wgc[b].astype(F32)).astype(BF)
        for name, start in (("wx%d" % b, far), ("wr%d" % b, Z), ("wy%d" % b, near)):
            blocks = pl.ds(start, 1 if name[1] == "r" else HZ)
            for k in range(1, X):
                to_x = lax.rem(x + k, X)
                send(wgx.at[b, to_x, blocks], wgxr.at[b, x, blocks], names[name] + k, dev_x(to_x))
        wgxr[b, x] = wgx[b, x]

    def wg_take(b, name, blocks):
        for k in range(1, X):
            recv(wgxr.at[b, lax.rem(x + X - k, X), blocks], names[name + str(b)] + k)
        total = wgxr[b, 0, blocks].astype(F32)
        for n in range(1, X):
            total = total + wgxr[b, n, blocks].astype(F32)
        return total.astype(BF)

    def wg_third(b, start):
        blocks = pl.ds(start, HZ)
        main = wg_take(b, "wx" if start is far else "wy", blocks).reshape(HZ * MAIN, FP)
        if start is far:
            wgxr[b, 0, Z] = wg_take(b, "wr", pl.ds(Z, 1))[0]
        rest = wgxr[b, 0, Z]
        wgz[b, blocks, :, :FULL] = main[:, :FULL].reshape(HZ, MAIN, FULL)
        tail = main[:, FULL:].astype(F32)
        for n in range(F // WP):
            pick = shift_lanes(n)
            o = iota((HZ * MAIN, Z * R2), 0)
            slot = lax.rem(o, MAIN) - n * R2
            rows = (o // MAIN + start) * R2 + slot == iota((HZ * MAIN, Z * R2), 1)
            rows = (rows & (slot >= 0) & (slot < R2)).astype(BF)
            tail = tail + mm(rows, mm(rest, pick).astype(BF))
        wgz[b, blocks, :, FULL:] = tail.astype(BF).reshape(HZ, MAIN, 128)
        for m in range(HZ):
            for e in range(DP):
                if start is near and m == 0 and e == 0:
                    continue
                z_ = start + lax.rem(lax.rem(z, HZ) + m, HZ)
                peer = lax.rem(d + e, DP) * Z + z_
                hop = lax.rem(peer + ZG - zg, ZG)
                send(wgz.at[b, z_], wgzr.at[b, zg], names["wz%d" % b] + hop, dev_zg(peer))
        if start is near:
            wgzr[b, zg] = wgz[b, z]

    def wg_end(b, ref):
        ex_wait(wgzr.at[b], names["wz%d" % b], ZG, zg)
        total = wgzr[b, 0].astype(F32)
        for n in range(1, ZG):
            total = total + wgzr[b, n].astype(F32)
        ref[:MAIN, :FULL] = total[:, :FULL]
        tail = total[:, FULL:]
        ref[:MAIN, FULL:] = tail[:, : F - FULL]
        for n in range(F // WP):
            ref[MAIN : MAIN + R2, n * WP : (n + 1) * WP] = tail[n * R2 : (n + 1) * R2, 128 - WP :]

    before = [0]
    for step in range(nup):
        here = z_step(0, step)
        for i in here:
            x_hop(i)
        for i in before:
            x_take(i)
        before = here
    z_start(1)

    ex_wait(cot_b, names["cot_x"], G, g)
    z_put(cot_c.at[0], to_z(flatten(cot_b)))
    ex_send(lambda p: cot_c.at[0, p], cot_c.at[1], names["cot_z"], Z, z, dev_z)
    cot_c[1, z] = cot_c[0, z]

    ex_wait(xw_s, names["tok"], Y, y)
    norm(xw_s, 0)

    for i in before:
        x_take(i)
    if X > 2:
        for i in range(Z):
            x_last(i)
    for i in range(Z):
        recv(w_slot(0, x, 1 - c, order(i)), names["sib0"] + i)
        recv(w_slot(0, left, 1 - c, order(i)), names["sib0"] + Z + i)
        if X > 2:
            recv(w_slot(0, right, 1 - c, order(i)), names["sib0"] + 2 * Z + i)
            recv(w_slot(0, across, 1 - c, order(i)), names["sib0"] + 3 * Z + i)

    def to_sibling(x_, n):
        send(Wt.at[:, x_, c], Wt.at[:, x_, c], names["sib1"] + n, sibling)

    z_steps = iter(range(nup))

    def z_later(n):
        for _ in range(n):
            step = next(z_steps, None)
            if step is not None:
                for i in z_step(1, step) + ([0] if step == 0 else []):
                    slot = w_slot(1, x, c, order(i))
                    for k in range(1, X):
                        send(slot, slot, names["xp1"] + k * Z + i, dev_x(lax.rem(x + k, X)))

    z_later(1)

    ex_wait(cot_c.at[1], names["cot_z"], Z, z)
    cot_t = flatten(cot_c.at[1])
    gw_t[y] = gated(1, cot_t)
    ex_send(lambda p: gw_t.at[y], gw_t, names["ggt"], Y, y, dev_y)

    n_rest = CZ * 8 * R2
    o = iota((n_rest, n_rest), 0)
    source = lax.rem(o // R2, CZ) * (8 * R2) + o // (CZ * R2) * R2 + lax.rem(o, R2)
    shuffle = (iota((n_rest, n_rest), 1) == source).astype(BF)
    for x_ in range(X):
        rest = mm(shuffle, Ws[4, x_].reshape(n_rest, FP)).astype(BF)
        Wr[:, x_ * CZ * R2 : (x_ + 1) * CZ * R2] = rest.reshape(8, CZ * R2, FP)

    project(0)
    z_later(1)
    flat_s[...] = attend(0)
    z_later(1)
    out_partial(0, flat_s[...], rs1_a)
    ex_send(lambda p: rs1_a.at[p], rs1_b, names["rs1"], Y, y, dev_y)
    rs1_b[y] = rs1_a[y]

    z_later(nup)
    to_sibling(x, 0)
    drain(20)
    ex_wait(rs1_b, names["rs1"], Y, y)
    first = xw_s[y].astype(F32) + mod[2, y] * add_up(rs1_b)
    x_put(fst_a, to_groups(first.astype(BF)))
    ex_send(lambda p: fst_a.at[p], fst_b, names["fst_x"], G, g, dev_g)
    fst_b[g] = fst_a[g]
    ex_wait(fst_b, names["fst_x"], G, g)
    z_put(fst_c, to_z(flatten(fst_b)))
    ex_send(lambda p: fst_c.at[p], fst_d, names["fst_z"], Z, z, dev_z)
    fst_d[z] = fst_c[z]
    for k in range(1, X):
        x_ = lax.rem(x + X - k, X)
        for i in range(Z):
            recv(w_slot(1, x_, c, order(i)), names["xp1"] + k * Z + i)
        to_sibling(x_, k)

    for k in range(X):
        recv(Wt.at[:, lax.rem(x + X - k, X), 1 - c], names["sib1"] + k)
    ex_wait(gw_t, names["ggt"], Y, y)

    ex_wait(fst_d, names["fst_z"], Z, z)
    xw_t[y] = flatten(fst_d)
    ex_send(lambda p: xw_t.at[y], xw_t, names["fst"], Y, y, dev_y)

    narrow([gw_t[n] for n in range(Y)])
    grad_t = grad_heads(1)
    drain(2 * Y)

    ex_wait(xw_t, names["fst"], Y, y)
    norm(xw_t, 1)
    project(1)
    flat_t = attend(1)
    grads = attend_back(1, grad_t)
    in_partial(1, grads, xw_t, rsg_a)
    ex_send(lambda p: rsg_a.at[p], rsg_b, names["rsg"], Y, y, dev_y)
    rsg_b[y] = rsg_a[y]

    out_partial(1, flat_t, rsp_a)
    ex_send(lambda p: rsp_a.at[p], rsp_b, names["rsp"], Y, y, dev_y)
    rsp_b[y] = rsp_a[y]

    ex_wait(rsg_b, names["rsg"], Y, y)
    z_put(fg_a, in_finish(1, rsg_b, xw_t, cot_t))
    ex_send(lambda p: fg_a.at[p], fg_b, names["fg_z"], Z, z, dev_z)
    fg_b[z] = fg_a[z]

    narrow([gw_t[n] for n in range(Y)])
    wg_start(1, flat_t)

    ex_wait(fg_b, names["fg_z"], Z, z)
    x_put(fg_c, from_z(flatten(fg_b)))
    ex_send(lambda p: fg_c.at[p], fg_d, names["fg_x"], G, g, dev_g)
    fg_d[g] = fg_c[g]
    wg_second(1)

    ex_wait(rsp_b, names["rsp"], Y, y)
    second = xw_t[y].astype(F32) + mod[5, y] * add_up(rsp_b)
    z_put(out_a, second.astype(BF))
    ex_send(lambda p: out_a.at[p], out_b, names["out_z"], Z, z, dev_z)
    out_b[z] = out_a[z]

    ex_wait(fg_d, names["fg_x"], G, g)
    fg_e[...] = from_groups(flatten(fg_d))
    gw_s[y] = gated(0, fg_e[...])
    ex_send(lambda p: gw_s.at[y], gw_s, names["ggs"], Y, y, dev_y)

    ex_wait(out_b, names["out_z"], Z, z)
    x_put(out_c, from_z(flatten(out_b)))
    ex_send(lambda p: out_c.at[p], out_d, names["out_x"], G, g, dev_g)
    out_d[g] = out_c[g]

    drain(Y + G)

    ex_wait(gw_s, names["ggs"], Y, y)
    narrow([gw_s[n] for n in range(Y)])
    wg_start(0, flat_s[...])
    grad_s = grad_heads(0)
    wg_third(1, far)
    wg_second(0)
    wg_third(1, near)
    grads = attend_back(0, grad_s)
    wg_third(0, far)
    in_partial(0, grads, xw_s, rsf_a)
    ex_send(lambda p: rsf_a.at[p], rsf_b, names["rsf"], Y, y, dev_y)
    rsf_b[y] = rsf_a[y]
    wg_third(0, near)

    ex_wait(out_d, names["out_x"], G, g)
    out[...] = from_groups(flatten(out_d))[:, :F]
    wg_end(1, wg_t)
    ex_wait(rsf_b, names["rsf"], Y, y)
    igrad[...] = in_finish(0, rsf_b, xw_s, fg_e[...])[:, :F]
    drain()
    wg_end(0, wg_s)
    drain()


def hand_on(*refs):
    for source, target in zip(refs[:4], refs[4:]):
        target[...] = source[...]


def on_device(sizes, tokens, modulation, qkv_s, out_s, qkv_t, out_t, cotangent):
    DP, S, Y = sizes
    frames, patches, F = tokens.shape[1:]
    T = frames * patches
    X, C = Y, 2
    Z = S // (X * C)
    G = X * C
    H = F // HD
    rows = out_s.shape[0]
    R2 = rows - MAIN
    FP = (F + 2 + 127) // 128 * 128
    dims = (X, C, Z, Y, DP, T, F, FP, H, R2)
    names, count = layout(X, C, Z, Y, DP)

    K, KR = X * C * Z * MAIN, X * C * Z * R2
    xs, zs = pltpu.VMEM((G, 2 * Z, FP), BF), pltpu.VMEM((Z, 2 * G, FP), BF)
    wide = pltpu.VMEM((Y, T, FP), BF)
    scratch = [
        pltpu.SemaphoreType.DMA((count,)),
        pltpu.SemaphoreType.DMA((count,)),
        pltpu.VMEM((5, MAIN, FP), BF),
        pltpu.VMEM((4, MAIN, FP), BF),
        pltpu.VMEM((6, Y, 1, FP), F32),
        pltpu.VMEM((FP, C * Z * MAIN), BF),
        pltpu.VMEM((X, FP, KR), BF),
        wide, wide, wide, wide,
        pltpu.VMEM((5, X, C, Z, MAIN, FP), BF),
        pltpu.VMEM((4, X, C, Z, MAIN, FP), BF),
        pltpu.VMEM((8, KR, FP), BF),
        pltpu.VMEM((T, FP), BF),
        xs, xs, pltpu.VMEM((2, Z, 2 * G, FP), BF),
        xs, xs, zs, zs,
        zs, zs, xs, xs, pltpu.VMEM((T, FP), BF),
        zs, zs, xs, xs,
        pltpu.VMEM((T, K), BF),
        pltpu.VMEM((T, KR), BF),
        pltpu.VMEM((2, 3, T, FP), BF),
        pltpu.VMEM((2, H * T, T), F32),
        pltpu.VMEM((T, FP), BF),
        pltpu.VMEM((4, T, 1), F32),
        wide, wide, wide, wide, wide, wide, wide, wide,
        pltpu.VMEM((2, X, C, Z + 1, MAIN, FP), BF),
        pltpu.VMEM((2, X, Z + 1, MAIN, FP), BF),
        pltpu.VMEM((2, X, Z + 1, MAIN, FP), BF),
        pltpu.VMEM((2, X, Z + 1, MAIN, FP), BF),
        pltpu.VMEM((2, Z, MAIN, FP), BF),
        pltpu.VMEM((2, DP * Z, MAIN, FP), BF),
    ]
    vmem = pl.BlockSpec(memory_space=pltpu.VMEM)
    out, igrad, wg_s, wg_t = pl.pallas_call(
        functools.partial(kernel, dims, names),
        out_shape=(
            jax.ShapeDtypeStruct((T, F), BF),
            jax.ShapeDtypeStruct((T, F), BF),
            jax.ShapeDtypeStruct((rows, F), F32),
            jax.ShapeDtypeStruct((rows, F), F32),
        ),
        in_specs=[vmem] * 7,
        out_specs=(vmem,) * 4,
        scratch_shapes=scratch,
        compiler_params=pltpu.CompilerParams(
            collective_id=0, has_side_effects=True, vmem_limit_bytes=56 * 2**20
        ),
    )(tokens.reshape(T, F), cotangent.reshape(T, F), modulation.transpose(1, 0, 2), qkv_s, out_s, qkv_t, out_t)
    out, igrad, wg_s, wg_t = pl.pallas_call(
        hand_on,
        out_shape=tuple(jax.ShapeDtypeStruct(v.shape, v.dtype) for v in (out, igrad, wg_s, wg_t)),
        in_specs=[vmem] * 4,
        out_specs=(vmem,) * 4,
    )(out, igrad, wg_s, wg_t)
    shape = (1, frames, patches, F)
    return out.reshape(shape), igrad.reshape(shape), wg_s, wg_t


def solution(mesh):
    sizes = tuple(mesh.shape[a] for a in ("dp", "seq", "tp"))
    placed = (
        P("dp", "seq", None, "tp"),
        P("dp", None, None),
        P("seq", None, "tp"),
        P("seq", "tp"),
        P("seq", None, "tp"),
        P("seq", "tp"),
        P("dp", "seq", None, "tp"),
    )
    return jax.shard_map(
        functools.partial(on_device, sizes),
        mesh=mesh,
        in_specs=placed,
        out_specs=(
            P("dp", "seq", None, "tp"),
            P("dp", "seq", None, "tp"),
            P("seq", "tp"),
            P("seq", "tp"),
        ),
        check_vma=False,
    )
```

```python
import functools

import jax
import jax.numpy as jnp
from jax import lax
from jax.experimental import pallas as pl
from jax.experimental.pallas import tpu as pltpu
from jax.sharding import PartitionSpec as P

HD = 72
EPS = 1e-06
MAIN = 16
MESH = pl.DeviceIdType.MESH
BF = jnp.bfloat16
F32 = jnp.float32


def mm(a, b):
    return lax.dot_general(a, b, (((1,), (0,)), ((), ())), preferred_element_type=F32)


def mm_nt(a, b):
    return lax.dot_general(a, b, (((1,), (1,)), ((), ())), preferred_element_type=F32)


def mm_tn(a, b):
    return lax.dot_general(a, b, (((0,), (0,)), ((), ())), preferred_element_type=F32)


def iota(shape, axis):
    return lax.broadcasted_iota(jnp.int32, shape, axis)


class Sems:
    def __init__(self):
        self.count = 0

    def take(self, n):
        first = self.count
        self.count += n
        return first


def layout(X, C, Z, Y, DP):
    s = Sems()
    names = {}
    G = X * C
    for name in ("tok", "ggt", "rs1", "fst", "rsg", "rsp", "ggs", "rsf"):
        names[name] = s.take(Y)
    for name in ("cot_x", "fst_x", "fg_x", "out_x"):
        names[name] = s.take(G)
    for name in ("cot_z", "fst_z", "fg_z", "out_z"):
        names[name] = s.take(Z)
    for name in ("zu0", "zd0", "zu1", "zd1", "xr0", "xl0", "xo0"):
        names[name] = s.take(Z)
    names["sib0"] = s.take(X * Z)
    names["xp1"] = s.take(X * Z)
    names["sib1"] = s.take(X)
    for b in (0, 1):
        names["wc%d" % b] = s.take(1)
        names["wx%d" % b] = s.take(X)
        names["wy%d" % b] = s.take(X)
        names["wr%d" % b] = s.take(X)
        names["wz%d" % b] = s.take(DP * Z)
    return names, s.count


def kernel(dims, names, tok, cot, mods, qkv_s, out_s, qkv_t, out_t, out, igrad, wg_s, wg_t, *refs):
    X, C, Z, Y, DP, T, F, FP, H, R2 = dims
    G = X * C
    N = Y * F
    (
        ssem, rsem, wown, wown_t, mod, pm, pr, xw_s, xw_t, gw_t, gw_s, Ws, Wt, Wr, cotp,
        cot_a, cot_b, cot_c, fst_a, fst_b, fst_c, fst_d, fg_a, fg_b, fg_c, fg_d, fg_e,
        out_a, out_b, out_c, out_d,
        mp, mpr, qkv, prob, flat_s, stat,
        rs1_a, rs1_b, rsg_a, rsg_b, rsp_a, rsp_b, rsf_a, rsf_b,
        wgp, wgc, wgx, wgxr, wgz, wgzr,
    ) = refs

    d = lax.axis_index("dp")
    s = lax.axis_index("seq")
    y = lax.axis_index("tp")
    x = s // (Z * C)
    z = lax.rem(s // C, Z)
    c = lax.rem(s, C)
    g = x * C + c
    zg = d * Z + z

    def seq_of(x_, z_, c_):
        return (x_ * Z + z_) * C + c_

    def dev(d_, x_, z_, c_, y_):
        return {"dp": d_, "seq": seq_of(x_, z_, c_), "tp": y_}

    def dev_y(y_):
        return dev(d, x, z, c, y_)

    def dev_g(g_):
        return dev(d, g_ // C, z, lax.rem(g_, C), y)

    def dev_z(z_):
        return dev(d, x, z_, c, y)

    def dev_zg(zg_):
        return dev(zg_ // Z, x, lax.rem(zg_, Z), c, y)

    def dev_x(x_):
        return dev(d, x_, z, c, y)

    sibling = dev(d, x, z, 1 - c, y)
    ZG = DP * Z
    sent = []

    def send(src, dst, sem, device):
        copy = pltpu.make_async_remote_copy(
            src_ref=src, dst_ref=dst, send_sem=ssem.at[sem], recv_sem=rsem.at[sem],
            device_id=device, device_id_type=MESH,
        )
        copy.start()
        sent.append(copy)

    def drain(keep=0):
        while len(sent) > keep:
            sent.pop(0).wait_send()

    def recv(dst, sem):
        pltpu.make_async_remote_copy(
            src_ref=dst, dst_ref=dst, send_sem=ssem.at[sem], recv_sem=rsem.at[sem],
            device_id=sibling, device_id_type=MESH,
        ).wait_recv()

    def ex_send(src, dst, sem, n, me, device):
        for k in range(1, n):
            peer = lax.rem(me + k, n)
            send(src(peer), dst.at[me], sem + k, device(peer))

    def ex_wait(dst, sem, n, me):
        for k in range(1, n):
            recv(dst.at[lax.rem(me + n - k, n)], sem + k)

    barrier = pltpu.get_barrier_semaphore()
    peers = [dev_y(lax.rem(y + k, Y)) for k in range(1, Y)]
    peers += [dev_g(lax.rem(g + k, G)) for k in range(1, G)]
    peers += [dev_zg(lax.rem(zg + k, ZG)) for k in range(1, ZG)]
    for peer in peers:
        pl.semaphore_signal(barrier, inc=1, device_id=peer, device_id_type=MESH)

    rows = MAIN + R2

    def widened(value):
        return jnp.concatenate([value, jnp.zeros((value.shape[0], FP - F), F32)], axis=1)

    rest = []
    for ref, qkv_ref, out_ref in ((wown, qkv_s, out_s), (wown_t, qkv_t, out_t)):
        value = qkv_ref[...].astype(F32)
        for k in range(4):
            part = value[:, k, :] if k < 3 else out_ref[...].astype(F32)
            part = widened(part.reshape(rows, F))
            ref[k] = part[:MAIN].astype(BF)
            rest.append(part[MAIN:])
    wown[4] = jnp.concatenate(rest, axis=0).astype(BF)

    pl.semaphore_wait(barrier, len(peers))

    up, down = dev_zg(lax.rem(zg + 1, ZG)), dev_zg(lax.rem(zg + ZG - 1, ZG))
    right, left = lax.rem(x + 1, X), lax.rem(x + X - 1, X)
    across = lax.rem(x + X // 2, X)
    nup = Z // 2
    ndown = Z - 1 - nup

    def w_slot(b, x_, c_, z_):
        return (Wt if b else Ws).at[:, x_, c_, z_]

    def z_hop(step, first, b):
        z_ = lax.rem(z + first * step + Z * Z, Z)
        slot = w_slot(b, x, c, z_)
        src = (wown_t if b else wown) if step == 0 else slot
        send(src, slot, names["z%s%d" % ("u" if first < 0 else "d", b)] + step, up if first < 0 else down)

    def z_take(step, first, b):
        z_ = lax.rem(z + first * (step + 1) + Z * Z, Z)
        recv(w_slot(b, x, c, z_), names["z%s%d" % ("u" if first < 0 else "d", b)] + step)
        return z_

    def z_start(b):
        if nup:
            z_hop(0, -1, b)
        if ndown:
            z_hop(0, 1, b)

    def z_step(b, step):
        z_take(step, -1, b)
        if step + 1 < nup:
            z_hop(step + 1, -1, b)
        if step >= ndown:
            return [2 * step + 1]
        z_take(step, 1, b)
        if step + 1 < ndown:
            z_hop(step + 1, 1, b)
        return [2 * step + 1, 2 * step + 2]

    def order(i):
        return lax.rem(z + (-(i + 1) // 2 if i % 2 else i // 2) + Z, Z)

    def x_hop(i, own=False):
        slot = w_slot(0, x, c, order(i))
        src = wown if own else slot
        send(src, slot, names["xr0"] + i, dev_x(right))
        if X > 2:
            send(src, slot, names["xl0"] + i, dev_x(left))
        send(src, w_slot(0, x, c, order(i)), names["sib0"] + i, sibling)

    def x_take(i):
        recv(w_slot(0, left, c, order(i)), names["xr0"] + i)
        if X > 2:
            slot = w_slot(0, left, c, order(i))
            if i % 2 == 0:
                send(slot, slot, names["xo0"] + i, dev_x(right))
            send(slot, slot, names["sib0"] + Z + i, sibling)
            slot = w_slot(0, right, c, order(i))
            recv(slot, names["xl0"] + i)
            if i % 2 == 1:
                send(slot, slot, names["xo0"] + i, dev_x(left))
            send(slot, slot, names["sib0"] + 2 * Z + i, sibling)
        else:
            slot = w_slot(0, left, c, order(i))
            send(slot, slot, names["sib0"] + Z + i, sibling)

    def x_last(i):
        slot = w_slot(0, across, c, order(i))
        recv(slot, names["xo0"] + i)
        send(slot, slot, names["sib0"] + 3 * Z + i, sibling)

    z_start(0)
    x_hop(0, True)
    xw_s[y] = jnp.zeros((T, FP), BF)
    xw_s[y, :, :F] = tok[...]
    ex_send(lambda p: xw_s.at[y], xw_s, names["tok"], Y, y, dev_y)
    cotp[...] = jnp.zeros((T, FP), BF)
    cotp[:, :F] = cot[...]

    row = iota((T, T), 0)
    col = iota((T, T), 1)

    def swap_rows(value, source):
        return mm((col == source).astype(BF), value).astype(BF)

    def to_groups(value):
        return swap_rows(value, lax.rem(row // Z, 2) * (G * Z) + row // (2 * Z) * Z + lax.rem(row, Z))

    def from_groups(value):
        return swap_rows(
            value, lax.rem(row // Z, G) * (2 * Z) + row // (G * Z) * Z + lax.rem(row, Z)
        )

    def to_z(value):
        return swap_rows(value, lax.rem(row, 2 * G) * Z + row // (2 * G))

    def from_z(value):
        return swap_rows(value, lax.rem(row, Z) * (2 * G) + row // Z)

    def x_put(buf, value):
        buf[...] = value.reshape(G, 2 * Z, FP)

    def z_put(buf, value):
        buf[...] = value.reshape(Z, 2 * G, FP)

    def flatten(buf):
        return buf[...].reshape(T, FP)

    x_put(cot_a, to_groups(cotp[...]))
    ex_send(lambda p: cot_a.at[p], cot_b, names["cot_x"], G, g, dev_g)
    cot_b[g] = cot_a[g]
    for k in range(5):
        Ws[k, x, c, z] = wown[k]
    for k in range(4):
        Wt[k, x, c, z] = wown_t[k]
    mod[...] = jnp.zeros((6, Y, 1, FP), F32)
    for i in range(6):
        for n in range(Y):
            mod[i, n, :, :F] = mods[i, :, n * F : (n + 1) * F]

    CZ = C * Z
    j = iota((FP, CZ * MAIN), 1)
    target = (lax.rem(j // MAIN, Z) * C + j // (Z * MAIN)) * (MAIN + R2) + lax.rem(j, MAIN)
    pm[...] = (iota((FP, CZ * MAIN), 0) == target).astype(BF)
    j = iota((FP, X * CZ * R2), 1)
    target = (lax.rem(j // R2, Z) * C + lax.rem(j // (Z * R2), C)) * (MAIN + R2)
    target += MAIN + lax.rem(j, R2)
    hit = iota((FP, X * CZ * R2), 0) == target
    for x_ in range(X):
        pr[x_] = (hit & (j // (CZ * R2) == x_)).astype(BF)

    lane = iota((1, FP), 1)
    inside = lane < F
    head = [(lane >= h * HD) & (lane < (h + 1) * HD) for h in range(H)]

    def narrow(slices):
        rest = None
        for x_ in range(X):
            part = slices[x_]
            mp[:, x_ * CZ * MAIN : (x_ + 1) * CZ * MAIN] = mm(part, pm[...]).astype(BF)
            more = mm(part, pr[x_])
            rest = more if rest is None else rest + more
        mpr[...] = rest.astype(BF)

    def natural(main, rest, x_):
        return mm_nt(main[:, x_ * CZ * MAIN : (x_ + 1) * CZ * MAIN], pm[...]) + mm_nt(rest, pr[x_])

    def norm(xw, at):
        total = None
        for n in range(Y):
            part = jnp.sum(xw[n].astype(F32), axis=-1, keepdims=True)
            total = part if total is None else total + part
        mean = total * (1.0 / N)
        total = None
        for n in range(Y):
            center = jnp.where(inside, xw[n].astype(F32) - mean, 0.0)
            part = jnp.sum(center * center, axis=-1, keepdims=True)
            total = part if total is None else total + part
        inverse = lax.rsqrt(total * (1.0 / N) + EPS)
        stat[2 * at] = mean
        stat[2 * at + 1] = inverse
        slices = []
        for n in range(Y):
            normed = (xw[n].astype(F32) - mean) * inverse
            slices.append((normed * (1.0 + mod[3 * at + 1, n]) + mod[3 * at, n]).astype(BF))
        narrow(slices)

    K = X * CZ * MAIN

    def weight(b, k):
        return (Wt if b else Ws)[k].reshape(K, FP), Wr[b * 4 + k]

    def project(b):
        for k in range(3):
            main, rest = weight(b, k)
            qkv[b, k] = (mm(mp[...], main) + mm(mpr[...], rest)).astype(BF)

    def spread(value):
        zero = jnp.zeros_like(value)
        return jnp.concatenate([jnp.where(head[h], value, zero) for h in range(H)], axis=0)

    def gather_heads(value):
        total = None
        for h in range(H):
            part = jnp.where(head[h], value[h * T : (h + 1) * T], 0.0)
            total = part if total is None else total + part
        return total.astype(BF)

    SCALE = HD ** (-0.5)

    def attend(b):
        scores = mm_nt(spread(qkv[b, 0]), qkv[b, 1]) * SCALE
        if b == 0:
            query_frame = lax.rem(iota((H * T, T), 0), T) // (G * Z)
            same = query_frame == iota((H * T, T), 1) // (G * Z)
            scores = jnp.where(same, scores, -1e30)
        weights = jnp.exp(scores - jnp.max(scores, axis=-1, keepdims=True))
        prob[b] = weights / jnp.sum(weights, axis=-1, keepdims=True)
        return gather_heads(mm(prob[b].astype(BF), qkv[b, 2]))

    def attend_back(b, grad):
        grads = spread(grad)
        likely = prob[b]
        grad_values = mm_tn(likely.astype(BF), grads).astype(BF)
        grad_likely = mm_nt(grads, qkv[b, 2])
        shift = grad_likely - jnp.sum(likely * grad_likely, axis=-1, keepdims=True)
        grad_scores = (likely * shift * SCALE).astype(BF)
        grad_query = gather_heads(mm(grad_scores, qkv[b, 1]))
        grad_keys = mm_tn(grad_scores, spread(qkv[b, 0])).astype(BF)
        return grad_query, grad_keys, grad_values

    def out_partial(b, flat, buf):
        main, rest = weight(b, 3)
        part = mm_nt(flat, main).astype(BF)
        part_rest = mm_nt(flat, rest).astype(BF)
        for n in range(Y):
            buf[n] = natural(part, part_rest, n).astype(BF)

    def grad_heads(b):
        main, rest = weight(b, 3)
        return (mm(mp[...], main) + mm(mpr[...], rest)).astype(BF)

    def in_partial(b, grads, xw, buf):
        part, part_rest = None, None
        for k in range(3):
            main, rest = weight(b, k)
            a, r = mm_nt(grads[k], main), mm_nt(grads[k], rest)
            part = a if part is None else part + a
            part_rest = r if part_rest is None else part_rest + r
        part, part_rest = part.astype(BF), part_rest.astype(BF)
        mean, inverse = stat[2 * b], stat[2 * b + 1]
        first, second = None, None
        slices = []
        for n in range(Y):
            value = natural(part, part_rest, n)
            slices.append(value)
            scaled = value * (1.0 + mod[3 * b + 1, n])
            normed = (xw[n].astype(F32) - mean) * inverse
            a = jnp.sum(scaled, axis=-1, keepdims=True)
            r = jnp.sum(scaled * normed, axis=-1, keepdims=True)
            first = a if first is None else first + a
            second = r if second is None else second + r
        for n in range(Y):
            value = jnp.where(lane == F, first, jnp.where(lane == F + 1, second, slices[n]))
            buf[n] = value.astype(BF)

    def in_finish(b, buf, xw, incoming):
        total = buf[0].astype(F32)
        for n in range(1, Y):
            total = total + buf[n].astype(F32)
        first = total[:, F : F + 1] * (1.0 / N)
        second = total[:, F + 1 : F + 2] * (1.0 / N)
        scaled = total * (1.0 + mod[3 * b + 1, y])
        normed = (xw[y].astype(F32) - stat[2 * b]) * stat[2 * b + 1]
        grad = stat[2 * b + 1] * (scaled - first - normed * second)
        return jnp.where(inside, incoming.astype(F32) + grad, 0.0).astype(BF)

    def add_up(buf):
        total = buf[0].astype(F32)
        for n in range(1, Y):
            total = total + buf[n].astype(F32)
        return total

    def gated(b, value):
        return (mod[3 * b + 2, y] * value.astype(F32)).astype(BF)

    HZ = Z // 2
    near = z // HZ * HZ
    far = HZ - near
    FULL = FP - 128
    WP = 128 - (F - FULL)

    def shift_lanes(n):
        a, b = iota((FP, 128), 0), iota((FP, 128), 1)
        return ((a - n * WP == b - (128 - WP)) & (b >= 128 - WP)).astype(BF)

    def wg_start(b, flat):
        main = mm_tn(mp[...], flat).astype(BF)
        rest = mm_tn(mpr[...], flat).astype(BF)
        wgp[b, :, :, :Z] = main.reshape(X, C, Z, MAIN, FP)
        wgp[b, :, :, Z] = rest.reshape(X, C, Z * R2, FP)
        send(wgp.at[b, :, 1 - c], wgc.at[b], names["wc%d" % b], sibling)

    def wg_second(b):
        recv(wgc.at[b], names["wc%d" % b])
        wgx[b] = (wgp[b, :, c].astype(F32) + wgc[b].astype(F32)).astype(BF)
        for name, start in (("wx%d" % b, far), ("wr%d" % b, Z), ("wy%d" % b, near)):
            blocks = pl.ds(start, 1 if name[1] == "r" else HZ)
            for k in range(1, X):
                to_x = lax.rem(x + k, X)
                send(wgx.at[b, to_x, blocks], wgxr.at[b, x, blocks], names[name] + k, dev_x(to_x))
        wgxr[b, x] = wgx[b, x]

    def wg_take(b, name, blocks):
        for k in range(1, X):
            recv(wgxr.at[b, lax.rem(x + X - k, X), blocks], names[name + str(b)] + k)
        total = wgxr[b, 0, blocks].astype(F32)
        for n in range(1, X):
            total = total + wgxr[b, n, blocks].astype(F32)
        return total.astype(BF)

    def wg_third(b, start):
        blocks = pl.ds(start, HZ)
        main = wg_take(b, "wx" if start is far else "wy", blocks).reshape(HZ * MAIN, FP)
        if start is far:
            wgxr[b, 0, Z] = wg_take(b, "wr", pl.ds(Z, 1))[0]
        rest = wgxr[b, 0, Z]
        wgz[b, blocks, :, :FULL] = main[:, :FULL].reshape(HZ, MAIN, FULL)
        tail = main[:, FULL:].astype(F32)
        for n in range(F // WP):
            pick = shift_lanes(n)
            o = iota((HZ * MAIN, Z * R2), 0)
            slot = lax.rem(o, MAIN) - n * R2
            rows = (o // MAIN + start) * R2 + slot == iota((HZ * MAIN, Z * R2), 1)
            rows = (rows & (slot >= 0) & (slot < R2)).astype(BF)
            tail = tail + mm(rows, mm(rest, pick).astype(BF))
        wgz[b, blocks, :, FULL:] = tail.astype(BF).reshape(HZ, MAIN, 128)
        for m in range(HZ):
            for e in range(DP):
                if start is near and m == 0 and e == 0:
                    continue
                z_ = start + lax.rem(lax.rem(z, HZ) + m, HZ)
                peer = lax.rem(d + e, DP) * Z + z_
                hop = lax.rem(peer + ZG - zg, ZG)
                send(wgz.at[b, z_], wgzr.at[b, zg], names["wz%d" % b] + hop, dev_zg(peer))
        if start is near:
            wgzr[b, zg] = wgz[b, z]

    def wg_end(b, ref):
        ex_wait(wgzr.at[b], names["wz%d" % b], ZG, zg)
        total = wgzr[b, 0].astype(F32)
        for n in range(1, ZG):
            total = total + wgzr[b, n].astype(F32)
        ref[:MAIN, :FULL] = total[:, :FULL]
        tail = total[:, FULL:]
        ref[:MAIN, FULL:] = tail[:, : F - FULL]
        for n in range(F // WP):
            ref[MAIN : MAIN + R2, n * WP : (n + 1) * WP] = tail[n * R2 : (n + 1) * R2, 128 - WP :]

    before = [0]
    for step in range(nup):
        here = z_step(0, step)
        for i in here:
            x_hop(i)
        for i in before:
            x_take(i)
        before = here
    z_start(1)

    ex_wait(cot_b, names["cot_x"], G, g)
    z_put(cot_c.at[0], to_z(flatten(cot_b)))
    ex_send(lambda p: cot_c.at[0, p], cot_c.at[1], names["cot_z"], Z, z, dev_z)
    cot_c[1, z] = cot_c[0, z]

    ex_wait(xw_s, names["tok"], Y, y)
    norm(xw_s, 0)

    for i in before:
        x_take(i)
    if X > 2:
        for i in range(Z):
            x_last(i)
    for i in range(Z):
        recv(w_slot(0, x, 1 - c, order(i)), names["sib0"] + i)
        recv(w_slot(0, left, 1 - c, order(i)), names["sib0"] + Z + i)
        if X > 2:
            recv(w_slot(0, right, 1 - c, order(i)), names["sib0"] + 2 * Z + i)
            recv(w_slot(0, across, 1 - c, order(i)), names["sib0"] + 3 * Z + i)

    def to_sibling(x_, n):
        send(Wt.at[:, x_, c], Wt.at[:, x_, c], names["sib1"] + n, sibling)

    z_steps = iter(range(nup))

    def z_later(n):
        for _ in range(n):
            step = next(z_steps, None)
            if step is not None:
                for i in z_step(1, step) + ([0] if step == 0 else []):
                    slot = w_slot(1, x, c, order(i))
                    for k in range(1, X):
                        send(slot, slot, names["xp1"] + k * Z + i, dev_x(lax.rem(x + k, X)))

    z_later(1)

    ex_wait(cot_c.at[1], names["cot_z"], Z, z)
    cot_t = flatten(cot_c.at[1])
    gw_t[y] = gated(1, cot_t)
    ex_send(lambda p: gw_t.at[y], gw_t, names["ggt"], Y, y, dev_y)

    n_rest = CZ * 8 * R2
    o = iota((n_rest, n_rest), 0)
    source = lax.rem(o // R2, CZ) * (8 * R2) + o // (CZ * R2) * R2 + lax.rem(o, R2)
    shuffle = (iota((n_rest, n_rest), 1) == source).astype(BF)
    for x_ in range(X):
        rest = mm(shuffle, Ws[4, x_].reshape(n_rest, FP)).astype(BF)
        Wr[:, x_ * CZ * R2 : (x_ + 1) * CZ * R2] = rest.reshape(8, CZ * R2, FP)

    project(0)
    z_later(1)
    flat_s[...] = attend(0)
    z_later(1)
    out_partial(0, flat_s[...], rs1_a)
    ex_send(lambda p: rs1_a.at[p], rs1_b, names["rs1"], Y, y, dev_y)
    rs1_b[y] = rs1_a[y]

    z_later(nup)
    to_sibling(x, 0)
    drain(20)
    ex_wait(rs1_b, names["rs1"], Y, y)
    first = xw_s[y].astype(F32) + mod[2, y] * add_up(rs1_b)
    x_put(fst_a, to_groups(first.astype(BF)))
    ex_send(lambda p: fst_a.at[p], fst_b, names["fst_x"], G, g, dev_g)
    fst_b[g] = fst_a[g]
    ex_wait(fst_b, names["fst_x"], G, g)
    z_put(fst_c, to_z(flatten(fst_b)))
    ex_send(lambda p: fst_c.at[p], fst_d, names["fst_z"], Z, z, dev_z)
    fst_d[z] = fst_c[z]
    for k in range(1, X):
        x_ = lax.rem(x + X - k, X)
        for i in range(Z):
            recv(w_slot(1, x_, c, order(i)), names["xp1"] + k * Z + i)
        to_sibling(x_, k)

    for k in range(X):
        recv(Wt.at[:, lax.rem(x + X - k, X), 1 - c], names["sib1"] + k)
    ex_wait(gw_t, names["ggt"], Y, y)

    ex_wait(fst_d, names["fst_z"], Z, z)
    xw_t[y] = flatten(fst_d)
    ex_send(lambda p: xw_t.at[y], xw_t, names["fst"], Y, y, dev_y)

    narrow([gw_t[n] for n in range(Y)])
    grad_t = grad_heads(1)
    drain(2 * Y)

    ex_wait(xw_t, names["fst"], Y, y)
    norm(xw_t, 1)
    project(1)
    flat_t = attend(1)
    grads = attend_back(1, grad_t)
    in_partial(1, grads, xw_t, rsg_a)
    ex_send(lambda p: rsg_a.at[p], rsg_b, names["rsg"], Y, y, dev_y)
    rsg_b[y] = rsg_a[y]

    out_partial(1, flat_t, rsp_a)
    ex_wait(rsg_b, names["rsg"], Y, y)
    z_put(fg_a, in_finish(1, rsg_b, xw_t, cot_t))
    ex_send(lambda p: fg_a.at[p], fg_b, names["fg_z"], Z, z, dev_z)
    fg_b[z] = fg_a[z]
    ex_send(lambda p: rsp_a.at[p], rsp_b, names["rsp"], Y, y, dev_y)
    rsp_b[y] = rsp_a[y]

    narrow([gw_t[n] for n in range(Y)])
    wg_start(1, flat_t)

    ex_wait(fg_b, names["fg_z"], Z, z)
    x_put(fg_c, from_z(flatten(fg_b)))
    ex_send(lambda p: fg_c.at[p], fg_d, names["fg_x"], G, g, dev_g)
    fg_d[g] = fg_c[g]
    ex_wait(rsp_b, names["rsp"], Y, y)
    second = xw_t[y].astype(F32) + mod[5, y] * add_up(rsp_b)
    z_put(out_a, second.astype(BF))
    ex_send(lambda p: out_a.at[p], out_b, names["out_z"], Z, z, dev_z)
    out_b[z] = out_a[z]

    ex_wait(fg_d, names["fg_x"], G, g)
    fg_e[...] = from_groups(flatten(fg_d))
    gw_s[y] = gated(0, fg_e[...])
    ex_send(lambda p: gw_s.at[y], gw_s, names["ggs"], Y, y, dev_y)
    wg_second(1)

    ex_wait(out_b, names["out_z"], Z, z)
    x_put(out_c, from_z(flatten(out_b)))
    ex_send(lambda p: out_c.at[p], out_d, names["out_x"], G, g, dev_g)
    out_d[g] = out_c[g]

    drain(Y + G)

    ex_wait(gw_s, names["ggs"], Y, y)
    narrow([gw_s[n] for n in range(Y)])
    wg_start(0, flat_s[...])
    grad_s = grad_heads(0)
    wg_third(1, far)
    wg_second(0)
    wg_third(1, near)
    grads = attend_back(0, grad_s)
    wg_third(0, far)
    in_partial(0, grads, xw_s, rsf_a)
    ex_send(lambda p: rsf_a.at[p], rsf_b, names["rsf"], Y, y, dev_y)
    rsf_b[y] = rsf_a[y]
    wg_third(0, near)

    ex_wait(out_d, names["out_x"], G, g)
    out[...] = from_groups(flatten(out_d))[:, :F]
    wg_end(1, wg_t)
    ex_wait(rsf_b, names["rsf"], Y, y)
    igrad[...] = in_finish(0, rsf_b, xw_s, fg_e[...])[:, :F]
    drain()
    wg_end(0, wg_s)
    drain()


def hand_on(*refs):
    for source, target in zip(refs[:4], refs[4:]):
        target[...] = source[...]


def on_device(sizes, tokens, modulation, qkv_s, out_s, qkv_t, out_t, cotangent):
    DP, S, Y = sizes
    frames, patches, F = tokens.shape[1:]
    T = frames * patches
    X, C = Y, 2
    Z = S // (X * C)
    G = X * C
    H = F // HD
    rows = out_s.shape[0]
    R2 = rows - MAIN
    FP = (F + 2 + 127) // 128 * 128
    dims = (X, C, Z, Y, DP, T, F, FP, H, R2)
    names, count = layout(X, C, Z, Y, DP)

    K, KR = X * C * Z * MAIN, X * C * Z * R2
    xs, zs = pltpu.VMEM((G, 2 * Z, FP), BF), pltpu.VMEM((Z, 2 * G, FP), BF)
    wide = pltpu.VMEM((Y, T, FP), BF)
    scratch = [
        pltpu.SemaphoreType.DMA((count,)),
        pltpu.SemaphoreType.DMA((count,)),
        pltpu.VMEM((5, MAIN, FP), BF),
        pltpu.VMEM((4, MAIN, FP), BF),
        pltpu.VMEM((6, Y, 1, FP), F32),
        pltpu.VMEM((FP, C * Z * MAIN), BF),
        pltpu.VMEM((X, FP, KR), BF),
        wide, wide, wide, wide,
        pltpu.VMEM((5, X, C, Z, MAIN, FP), BF),
        pltpu.VMEM((4, X, C, Z, MAIN, FP), BF),
        pltpu.VMEM((8, KR, FP), BF),
        pltpu.VMEM((T, FP), BF),
        xs, xs, pltpu.VMEM((2, Z, 2 * G, FP), BF),
        xs, xs, zs, zs,
        zs, zs, xs, xs, pltpu.VMEM((T, FP), BF),
        zs, zs, xs, xs,
        pltpu.VMEM((T, K), BF),
        pltpu.VMEM((T, KR), BF),
        pltpu.VMEM((2, 3, T, FP), BF),
        pltpu.VMEM((2, H * T, T), F32),
        pltpu.VMEM((T, FP), BF),
        pltpu.VMEM((4, T, 1), F32),
        wide, wide, wide, wide, wide, wide, wide, wide,
        pltpu.VMEM((2, X, C, Z + 1, MAIN, FP), BF),
        pltpu.VMEM((2, X, Z + 1, MAIN, FP), BF),
        pltpu.VMEM((2, X, Z + 1, MAIN, FP), BF),
        pltpu.VMEM((2, X, Z + 1, MAIN, FP), BF),
        pltpu.VMEM((2, Z, MAIN, FP), BF),
        pltpu.VMEM((2, DP * Z, MAIN, FP), BF),
    ]
    vmem = pl.BlockSpec(memory_space=pltpu.VMEM)
    out, igrad, wg_s, wg_t = pl.pallas_call(
        functools.partial(kernel, dims, names),
        out_shape=(
            jax.ShapeDtypeStruct((T, F), BF),
            jax.ShapeDtypeStruct((T, F), BF),
            jax.ShapeDtypeStruct((rows, F), F32),
            jax.ShapeDtypeStruct((rows, F), F32),
        ),
        in_specs=[vmem] * 7,
        out_specs=(vmem,) * 4,
        scratch_shapes=scratch,
        compiler_params=pltpu.CompilerParams(
            collective_id=0, has_side_effects=True, vmem_limit_bytes=56 * 2**20
        ),
    )(tokens.reshape(T, F), cotangent.reshape(T, F), modulation.transpose(1, 0, 2), qkv_s, out_s, qkv_t, out_t)
    out, igrad, wg_s, wg_t = pl.pallas_call(
        hand_on,
        out_shape=tuple(jax.ShapeDtypeStruct(v.shape, v.dtype) for v in (out, igrad, wg_s, wg_t)),
        in_specs=[vmem] * 4,
        out_specs=(vmem,) * 4,
    )(out, igrad, wg_s, wg_t)
    shape = (1, frames, patches, F)
    return out.reshape(shape), igrad.reshape(shape), wg_s, wg_t


def solution(mesh):
    sizes = tuple(mesh.shape[a] for a in ("dp", "seq", "tp"))
    placed = (
        P("dp", "seq", None, "tp"),
        P("dp", None, None),
        P("seq", None, "tp"),
        P("seq", "tp"),
        P("seq", None, "tp"),
        P("seq", "tp"),
        P("dp", "seq", None, "tp"),
    )
    return jax.shard_map(
        functools.partial(on_device, sizes),
        mesh=mesh,
        in_specs=placed,
        out_specs=(
            P("dp", "seq", None, "tp"),
            P("dp", "seq", None, "tp"),
            P("seq", "tp"),
            P("seq", "tp"),
        ),
        check_vma=False,
    )
```
